32 devices in a mesh: dp: 4 (over x, core), expert: 4 (over z), head: 2 (over y).
Axes of the slice: x: 2, y: 2, z: 4, core: 2. Of those that a mesh axis runs over, the one named last changes fastest.
Arguments:
- block_input: bfloat16 [16384, 768], P(('dp', 'expert', 'head')), may hold values from -6 to 6
- output_cotangent: bfloat16 [16384, 768], P(('dp', 'expert', 'head')), may hold values from -6 to 6
- token_ids: int32 [16384], P(('dp', 'expert', 'head')), may hold values from 0 to 8007, as said below
- positions: int32 [16384], P(('dp', 'expert', 'head')), may hold values from 0 to 1023, as said below
- hash_table: int32 [8008], replicated, may hold values from 0 to 3, as said below
- first_gain: float32 [768], replicated, may hold values from 0.5 to 1.5
- second_gain: float32 [768], replicated, may hold values from 0.5 to 1.5
- project_weight: bfloat16 [3, 768, 768], P(None, None, 'head'), may hold values from -0.21875 to 0.21875
- output_weight: bfloat16 [768, 768], P('head'), may hold values from -0.875 to 0.875
- expert_inner: bfloat16 [4, 768, 3072], P('expert'), may hold values from -0.21875 to 0.21875
- expert_outer: bfloat16 [4, 3072, 768], P('expert'), may hold values from -0.109375 to 0.109375
Outputs:
- block_output: bfloat16 [16384, 768], P(('dp', 'expert', 'head'))
- input_grad: float32 [16384, 768], P(('dp', 'expert', 'head'))
- first_gain_grad: float32 [768], replicated
- second_gain_grad: float32 [768], replicated
- project_grad: float32 [3, 768, 768], P(None, None, 'head')
- output_weight_grad: float32 [768, 768], P('head')
- expert_inner_grad: float32 [4, 768, 3072], P('expert')
- expert_outer_grad: float32 [4, 3072, 768], P('expert')
The draws below stay inside these ranges and needn't reach their ends.
Inputs may be any that keep to these rules, and one draw needn't show every extreme that they name: `token_ids`: on every device, exactly 256 of its 512 tokens have ids that hash_table maps to one expert, and at most 256 map to any other expert; within a group of devices along the expert axis this busiest expert is the same for all devices. `hash_table`: every expert is named by 2002 ids. `positions`: documents lie inside sequences of 1024 tokens; the first starts at a sequence's first token; a token's value is its index in the sequence minus that of its document's first token. In every sequence, tokens 1024 // 2 - 1 and 512 share a document. Some sequence is a single document.
All inputs are finite; a program needn't handle non-finite values.
Results may differ from the reference program's by a relative error of at most 0.012.
Values may be sent and summed in bfloat16 or wider, within the bound.
No kernel may reach another device: no remote copies, remote signals or barrier semaphores. Data moves between devices by JAX's collectives and lax.ppermute only.
A program may use at most 256 MiB of HBM per device.

```python
import jax
import jax.numpy as jnp
from jax import lax

D = 768
HEAD_DIM = 64
FF = 3072
VOCAB = 8008
EXPERTS = 4
TOK_DEV = 512
CAP = 256
SEQLEN = 1024
TOKENS = 16384
N_DP = 4
N_EXPERT = 4
N_HEAD = 2
DEVICES = 32


def routing(key):
    key_perm, key_hot, key_other, key_pick, key_shuffle = jax.random.split(key, 5)
    permuted = jax.random.permutation(key_perm, VOCAB).astype(jnp.int32)
    lookup = jnp.zeros((VOCAB,), jnp.int32).at[permuted].set(jnp.arange(VOCAB, dtype=jnp.int32) % EXPERTS)
    hottest = jax.random.randint(key_hot, (N_DP, 1, N_HEAD), 0, EXPERTS)
    hottest = jnp.broadcast_to(hottest, (N_DP, N_EXPERT, N_HEAD)).reshape(DEVICES, 1)
    others = (hottest + 1 + jax.random.randint(key_other, (DEVICES, TOK_DEV - CAP), 0, EXPERTS - 1)) % EXPERTS
    chosen = jnp.concatenate([jnp.broadcast_to(hottest, (DEVICES, CAP)), others], axis=1)
    shuffle_keys = jax.random.split(key_shuffle, DEVICES)
    chosen = jax.vmap(jax.random.permutation)(shuffle_keys, chosen)
    per_expert = VOCAB // EXPERTS
    picked = jax.random.randint(key_pick, (2, DEVICES, TOK_DEV), 0, per_expert)
    picked = jnp.minimum(picked[0], picked[1])
    token_list = permuted[chosen + EXPERTS * picked]
    return (token_list.reshape(TOKENS).astype(jnp.int32), lookup)


def draw_token_ids(key, part):
    token_list, lookup = routing(key)
    return token_list


def draw_hash_table(key, part):
    token_list, lookup = routing(key)
    return lookup


def draw_positions(key, part):
    key = jax.random.fold_in(key, 7)
    key_flag, key_whole = jax.random.split(key, 2)
    sequences = TOKENS // SEQLEN
    ordering = jnp.arange(SEQLEN, dtype=jnp.int32)
    start_flag = jax.random.randint(key_flag, (sequences, SEQLEN), 0, SEQLEN) < 4
    middle_band = (ordering >= SEQLEN // 2 - SEQLEN // 8) & (ordering <= SEQLEN // 2 + SEQLEN // 8)
    whole_seq = jax.random.randint(key_whole, (), 0, sequences)
    single = (jnp.arange(sequences, dtype=jnp.int32) == whole_seq)[:, None]
    start_flag = start_flag & jnp.logical_not(middle_band)[None, :] & jnp.logical_not(single) | (ordering == 0)[None, :]
    doc_starts = lax.cummax(jnp.where(start_flag, ordering[None, :], 0), axis=1)
    return (ordering[None, :] - doc_starts).reshape(TOKENS).astype(jnp.int32)


def levels(rng, dims, pieces, least, high):
    level, own = 1.0, jax.random.fold_in(rng, 6)
    for dim, blocks in pieces:
        heights = jnp.exp(jax.random.uniform(jax.random.fold_in(own, dim), (blocks,), jnp.float32, least / len(pieces), high / len(pieces)))
        level = level * jnp.repeat(heights, dims[dim] // blocks).reshape([-1 if axis == dim else 1 for axis in range(len(dims))])
    return level


def gaussian(key, extent, scale, most, cuts=(), kind=jnp.bfloat16):
    level = levels(key, extent, cuts, -0.22, 0.18) if cuts else 1.0
    array = jax.random.normal(key, extent, jnp.float32) * scale * level
    return jnp.minimum(jnp.maximum(array, -most), most).astype(kind)


def setup_inputs(seed: int = 0) -> dict:
    key_of = jax.random.split(jax.random.key(seed), 12)
    return {
        "block_input": gaussian(key_of[0], (TOKENS, D), 1.0, 6.0, ((0, 32),)),
        "output_cotangent": gaussian(key_of[1], (TOKENS, D), 1.0, 6.0, ((0, 32),)),
        "token_ids": draw_token_ids(jax.random.fold_in(key_of[11], 71), 0),
        "positions": draw_positions(jax.random.fold_in(key_of[11], 71), 0),
        "hash_table": draw_hash_table(jax.random.fold_in(key_of[11], 71), 0),
        "first_gain": jnp.clip(1.0 + 0.1 * jax.random.normal(key_of[5], (D,), jnp.float32), 0.5, 1.5),
        "second_gain": jnp.clip(1.0 + 0.1 * jax.random.normal(key_of[6], (D,), jnp.float32), 0.5, 1.5),
        "project_weight": gaussian(key_of[7], (3, D, D), D ** -0.5, 0.21875, ((2, 2),)),
        "output_weight": gaussian(key_of[8], (D, D), (D // 16) ** -0.5, 0.875, ((0, 2),)),
        "expert_inner": gaussian(key_of[9], (EXPERTS, D, FF), D ** -0.5, 0.21875, ((0, 4),)),
        "expert_outer": gaussian(key_of[10], (EXPERTS, FF, D), FF ** -0.5, 0.109375, ((0, 4),)),
    }


@jax.custom_vjp
def low(v):
    return lax.optimization_barrier(v.astype(jnp.bfloat16)).astype(jnp.float32)

@jax.custom_vjp
def low_back(v):
    return v

def low_keep(v):
    return (low(v), None)

def low_pass(kept, grad):
    return (grad,)

def back_keep(v):
    return (v, None)

def back_low(kept, grad):
    return (low(grad),)
low.defvjp(low_keep, low_pass)
low_back.defvjp(back_keep, back_low)

def layer_norm(values, gain):
    center = values - lax.optimization_barrier(jnp.mean(values, axis=-1, keepdims=True))
    spread = lax.optimization_barrier(jnp.mean(center * center, axis=-1, keepdims=True))
    return center * lax.rsqrt(spread + 1e-05) * gain

def attend_sequence(weights, norm_rows, seq_pos):
    length = norm_rows.shape[0]
    projected = jnp.einsum('td,cde->cte', norm_rows, weights, precision=lax.Precision.HIGHEST)
    projected = low_back(low(projected))
    head_values = projected.reshape(3, length, D // HEAD_DIM, HEAD_DIM)
    scores = jnp.einsum('qhd,khd->hqk', head_values[0], head_values[1], precision=lax.Precision.HIGHEST) * 0.125
    ordering = jnp.arange(length, dtype=jnp.int32)
    visible = (ordering[None, :] <= ordering[:, None]) & (ordering[None, :] >= (ordering - seq_pos)[:, None])
    scores = low_back(jnp.where(visible[None], scores, -1000000000.0))
    row_max = lax.optimization_barrier(jnp.max(scores, axis=-1, keepdims=True))
    exponent = jnp.exp(scores - row_max)
    probabilities = exponent / lax.optimization_barrier(jnp.sum(exponent, axis=-1, keepdims=True))
    context = jnp.einsum('hqk,khd->qhd', low(probabilities), head_values[2], precision=lax.Precision.HIGHEST)
    return low_back(low(context)).reshape(length, D)

def expert_rows(inputs):
    row_block, inner_weight, outer_weight = inputs
    pre_act = low_back(jnp.dot(row_block, inner_weight, precision=lax.Precision.HIGHEST))
    activated = low(jax.nn.gelu(pre_act))
    return low_back(low(jnp.dot(activated, outer_weight, precision=lax.Precision.HIGHEST)))

def reference(block_input, output_cotangent, token_ids, positions, hash_table, first_gain, second_gain, project_weight, output_weight, expert_inner, expert_outer):
    chosen = jnp.take(hash_table, token_ids).astype(jnp.int32).reshape(DEVICES, TOK_DEV)
    one_hot = chosen[:, :, None] == jnp.arange(EXPERTS, dtype=jnp.int32)[None, None, :]
    rank_table = jnp.cumsum(one_hot.astype(jnp.int32), axis=1) - 1
    rank_own = lax.optimization_barrier(jnp.sum(jnp.where(one_hot, rank_table, 0), axis=2)).astype(jnp.int32)
    device_index = jnp.arange(DEVICES, dtype=jnp.int32)[:, None]
    slot_index = ((chosen * DEVICES + device_index) * CAP + rank_own).reshape(TOKENS).astype(jnp.int32)
    seq_pos = positions.reshape(TOKENS // SEQLEN, SEQLEN)

    def forward(residual, gain_one, gain_two, weights, out_weight, inner_all, outer_all):
        first = low(layer_norm(residual, gain_one))

        def one_sequence(sequence_pair):
            return attend_sequence(weights, sequence_pair[0], sequence_pair[1])
        context = lax.map(jax.checkpoint(one_sequence), (first.reshape(TOKENS // SEQLEN, SEQLEN, D), seq_pos))
        attended = low_back(jnp.dot(context.reshape(TOKENS, D), out_weight, precision=lax.Precision.HIGHEST))
        hidden = residual + attended
        second = low_back(low(layer_norm(hidden, gain_two)))
        buffer = jnp.zeros((EXPERTS * DEVICES * CAP, D), jnp.float32).at[slot_index].set(second)
        buffer = buffer.reshape(EXPERTS, DEVICES * CAP, D)
        expert_out = lax.map(jax.checkpoint(expert_rows), (buffer, inner_all, outer_all))
        expert_out = expert_out.reshape(EXPERTS * DEVICES * CAP, D)
        return hidden + expert_out[slot_index]
    block_output, pullback = jax.vjp(forward, block_input.astype(jnp.float32), first_gain.astype(jnp.float32), second_gain.astype(jnp.float32), project_weight.astype(jnp.float32), output_weight.astype(jnp.float32), expert_inner.astype(jnp.float32), expert_outer.astype(jnp.float32))
    grads = pullback(output_cotangent.astype(jnp.float32))
    return (block_output.astype(jnp.bfloat16), grads[0], grads[1], grads[2], grads[3], grads[4], grads[5], grads[6])
```

```python
import jax
import jax.numpy as jnp
from jax import lax
from jax.sharding import PartitionSpec as P

HEAD_DIM = 64
BF = jnp.bfloat16
F32 = jnp.float32


def layer_norm(values, gain):
    center = values - jnp.mean(values, axis=-1, keepdims=True)
    spread = jnp.mean(center * center, axis=-1, keepdims=True)
    return center * lax.rsqrt(spread + 1e-05) * gain


def swap(values, axis, bit):
    size = lax.axis_size(axis)
    return lax.ppermute(values, axis, [(i, i ^ bit) for i in range(size)])


def bits_of(axis, low=1):
    size = lax.axis_size(axis)
    found = []
    while low < size:
        found.append((axis, low))
        low *= 2
    return found


def side(axis, bit):
    return (lax.axis_index(axis) // bit) % 2


def half_of(values, which):
    rows = values.shape[0] // 2
    return lax.dynamic_slice_in_dim(values, which * rows, rows, 0)


def scatter_sum(values, steps):
    for axis, bit in steps:
        mine = side(axis, bit)
        got = swap(half_of(values, 1 - mine), axis, bit)
        values = (half_of(values, mine).astype(F32) + got.astype(F32)).astype(BF)
    return values


def gather_back(values, steps):
    for axis, bit in reversed(steps):
        mine = side(axis, bit)
        got = swap(values, axis, bit)
        rows = values.shape[0]
        whole = jnp.zeros((2 * rows,) + values.shape[1:], values.dtype)
        whole = lax.dynamic_update_slice_in_dim(whole, values, mine * rows, 0)
        values = lax.dynamic_update_slice_in_dim(whole, got, (1 - mine) * rows, 0)
    return values


def on_device(
    block_input,
    output_cotangent,
    token_ids,
    positions,
    hash_table,
    first_gain,
    second_gain,
    project_weight,
    output_weight,
    expert_inner,
    expert_outer,
):
    tok_rows, model_width = block_input.shape
    local_cols = output_weight.shape[0]
    head_count = local_cols // HEAD_DIM
    expert_count = lax.axis_size("expert")
    capacity = tok_rows // 2
    inner_weight = expert_inner[0]
    outer_weight = expert_outer[0]
    my_head = lax.axis_index("head")
    my_expert = lax.axis_index("expert")

    chosen = jnp.take(hash_table, token_ids)
    relative = chosen ^ my_expert
    one_hot = relative[:, None] == jnp.arange(expert_count, dtype=jnp.int32)[None, :]
    rank_table = jnp.cumsum(one_hot.astype(jnp.int32), axis=0) - 1
    slot_index = relative * capacity + jnp.sum(jnp.where(one_hot, rank_table, 0), axis=1)
    place = (
        slot_index[None, :] == jnp.arange(expert_count * capacity, dtype=jnp.int32)[:, None]
    ).astype(BF)

    def dispatch(rows):
        return jnp.dot(place, rows, preferred_element_type=F32).astype(BF)

    def exchange(rows):
        blocks = rows.reshape(expert_count, capacity, model_width)
        return [blocks[0]] + [swap(blocks[k], "expert", k) for k in range(1, expert_count)]

    def put_back(blocks):
        return lax.dot_general(
            place,
            jnp.concatenate(blocks, axis=0),
            (((0,), (0,)), ((), ())),
            preferred_element_type=F32,
        )

    grad_blocks = exchange(dispatch(output_cotangent))

    def in_order(own, other):
        return jnp.where(
            my_head == 0,
            jnp.concatenate([own, other], axis=0),
            jnp.concatenate([other, own], axis=0),
        )

    residual = block_input.astype(F32)
    first_low = layer_norm(residual, first_gain).astype(BF)
    gathered = in_order(first_low, swap(first_low, "head", 1))
    seq_pos = in_order(positions, swap(positions, "head", 1))
    seq_len = gathered.shape[0]
    projected = jnp.einsum(
        "td,cde->cte", gathered, project_weight, preferred_element_type=F32
    ).astype(BF)
    head_values = projected.reshape(3, seq_len, head_count, HEAD_DIM)
    ordering = jnp.arange(seq_len, dtype=jnp.int32)
    visible = (ordering[None, :] <= ordering[:, None]) & (
        ordering[None, :] >= (ordering - seq_pos)[:, None]
    )
    scores = (
        jnp.einsum("qhd,khd->hqk", head_values[0], head_values[1], preferred_element_type=F32)
        * 0.125
    )
    scores = jnp.where(visible[None], scores, -1000000000.0)
    row_max = jnp.max(scores, axis=-1, keepdims=True)
    exponent = jnp.exp(scores - row_max)
    row_total = jnp.sum(exponent, axis=-1, keepdims=True)
    log_total = row_max + jnp.log(row_total)
    probabilities = (exponent / row_total).astype(BF)
    context = jnp.einsum(
        "hqk,khd->qhd", probabilities, head_values[2], preferred_element_type=F32
    )
    context = context.astype(BF).reshape(seq_len, local_cols)

    def half_rows(values, which):
        return lax.dynamic_slice_in_dim(values, which * tok_rows, tok_rows, 0)

    theirs = jnp.dot(
        half_rows(context, 1 - my_head), output_weight, preferred_element_type=F32
    ).astype(BF)
    theirs = swap(theirs, "head", 1)
    hidden = (
        residual
        + jnp.dot(half_rows(context, my_head), output_weight, preferred_element_type=F32)
        + theirs.astype(F32)
    )
    second_low = layer_norm(hidden, second_gain).astype(BF)

    row_blocks = exchange(dispatch(second_low))
    arrived = jnp.concatenate(row_blocks, axis=0)
    grad_arrived = jnp.concatenate(grad_blocks, axis=0)
    pre_act = jnp.dot(arrived, inner_weight, preferred_element_type=F32)
    act_grad = lax.dot_general(
        grad_arrived, outer_weight, (((1,), (1,)), ((), ())), preferred_element_type=F32
    )
    pre_grad = jax.vjp(jax.nn.gelu, pre_act)[1](act_grad)[0].astype(BF)
    rows_grad = lax.dot_general(
        pre_grad, inner_weight, (((1,), (1,)), ((), ())), preferred_element_type=F32
    ).astype(BF)
    returned = exchange(rows_grad)
    activated = jax.nn.gelu(pre_act).astype(BF)
    produced = jnp.dot(activated, outer_weight, preferred_element_type=F32).astype(BF)
    combined = exchange(produced)
    block_output = (hidden + put_back(combined)).astype(BF)

    core = side("dp", 1)

    def halves_sum(left, right):
        def part(which):
            cols = left.shape[1] // 2
            return lax.dot_general(
                lax.dynamic_slice_in_dim(left, which * cols, cols, 1),
                right,
                (((0,), (0,)), ((), ())),
                preferred_element_type=F32,
            )

        got = swap(part(1 - core).astype(BF), "dp", 1)
        return (part(core) + got.astype(F32)).astype(BF)

    steps = bits_of("dp", 2) + bits_of("head")
    outer_part = scatter_sum(halves_sum(activated, grad_arrived), steps)
    inner_part = scatter_sum(halves_sum(arrived, pre_grad), steps[::-1])
    outer_total = gather_back(gather_back(outer_part, steps), [("dp", 1)]).astype(F32)
    inner_total = gather_back(gather_back(inner_part, steps[::-1]), [("dp", 1)]).astype(F32)

    second_grad = put_back(returned)
    second_back = jax.vjp(layer_norm, hidden, second_gain)[1]
    hidden_part, second_gain_part = second_back(second_grad)
    hidden_grad = output_cotangent.astype(F32) + hidden_part

    hidden_low = hidden_grad.astype(BF)
    shard_rows = in_order(hidden_low, swap(hidden_low, "head", 1))
    context_grad = jnp.einsum("td,cd->tc", shard_rows, output_weight, preferred_element_type=F32)
    weight_run = jnp.einsum("tc,td->cd", context, shard_rows, preferred_element_type=F32)
    context_grad = context_grad.astype(BF).reshape(seq_len, head_count, HEAD_DIM)
    scores = (
        jnp.einsum("qhd,khd->hqk", head_values[0], head_values[1], preferred_element_type=F32)
        * 0.125
    )
    scores = jnp.where(visible[None], scores, -1000000000.0)
    soft = jnp.exp(scores - log_total)
    value_grad = jnp.einsum(
        "hqk,qhd->khd", soft.astype(BF), context_grad, preferred_element_type=F32
    ).astype(BF)
    prob_grad = jnp.einsum(
        "qhd,khd->hqk", context_grad, head_values[2], preferred_element_type=F32
    )
    inner_sum = jnp.sum(soft * prob_grad, axis=-1, keepdims=True)
    score_grad = (soft * (prob_grad - inner_sum)).astype(BF)
    query_grad = (
        jnp.einsum("hqk,khd->qhd", score_grad, head_values[1], preferred_element_type=F32) * 0.125
    ).astype(BF)
    key_grad = (
        jnp.einsum("hqk,qhd->khd", score_grad, head_values[0], preferred_element_type=F32) * 0.125
    ).astype(BF)
    mixed_grad = jnp.stack([query_grad, key_grad, value_grad]).reshape(3, seq_len, local_cols)
    project_part = jnp.einsum("td,cte->cde", gathered, mixed_grad, preferred_element_type=F32)

    def first_rows(which):
        return jnp.einsum(
            "cte,cde->td",
            lax.dynamic_slice_in_dim(mixed_grad, which * tok_rows, tok_rows, 1),
            project_weight,
            preferred_element_type=F32,
        )

    theirs = swap(first_rows(1 - my_head).astype(BF), "head", 1)
    first_grad = first_rows(my_head) + theirs.astype(F32)
    input_part, _ = jax.vjp(layer_norm, residual, first_gain)[1](first_grad)
    input_grad = hidden_grad + input_part

    first_gain_part = (
        jnp.sum(project_part * project_weight.astype(F32), axis=(0, 2)) / first_gain
    )
    gains = jnp.stack([first_gain_part, second_gain_part])
    for axis, bit in bits_of("dp") + bits_of("expert") + bits_of("head"):
        gains = gains + swap(gains, axis, bit)

    steps = bits_of("dp") + bits_of("expert")
    project_part = project_part.reshape(3 * model_width, local_cols).astype(BF)
    project_grad = gather_back(scatter_sum(project_part, steps), steps).astype(F32)
    output_weight_grad = gather_back(scatter_sum(weight_run.astype(BF), steps), steps).astype(F32)
    return (
        block_output,
        input_grad,
        gains[0],
        gains[1],
        project_grad.reshape(3, model_width, local_cols),
        output_weight_grad,
        inner_total[None],
        outer_total[None],
    )


def solution(mesh):
    in_specs = (
        P(("dp", "expert", "head"), None),
        P(("dp", "expert", "head"), None),
        P(("dp", "expert", "head")),
        P(("dp", "expert", "head")),
        P(),
        P(),
        P(),
        P(None, None, "head"),
        P("head", None),
        P("expert", None, None),
        P("expert", None, None),
    )
    out_specs = (
        P(("dp", "expert", "head"), None),
        P(("dp", "expert", "head"), None),
        P(),
        P(),
        P(None, None, "head"),
        P("head", None),
        P("expert", None, None),
        P("expert", None, None),
    )
    return jax.shard_map(
        on_device, mesh=mesh, in_specs=in_specs, out_specs=out_specs, check_vma=False
    )
```

```python
import jax
import jax.numpy as jnp
from jax import lax
from jax.experimental import pallas as pl
from jax.experimental.pallas import tpu as pltpu
from jax.sharding import PartitionSpec as P

HEAD_DIM = 64
BF = jnp.bfloat16
F32 = jnp.float32


def swap(values, axis, bit):
    size = lax.axis_size(axis)
    return lax.ppermute(values, axis, [(i, i ^ bit) for i in range(size)])


def bits_of(axis, low=1):
    size = lax.axis_size(axis)
    found = []
    while low < size:
        found.append((axis, low))
        low *= 2
    return found


def side(axis, bit):
    return (lax.axis_index(axis) // bit) % 2


def half_of(values, which):
    rows = values.shape[0] // 2
    return lax.dynamic_slice_in_dim(values, which * rows, rows, 0)


def scatter_sum(values, steps):
    for axis, bit in steps:
        mine = side(axis, bit)
        got = swap(half_of(values, 1 - mine), axis, bit)
        values = (half_of(values, mine).astype(F32) + got.astype(F32)).astype(BF)
    return values


def gather_back(values, steps):
    for axis, bit in reversed(steps):
        mine = side(axis, bit)
        got = swap(values, axis, bit)
        rows = values.shape[0]
        whole = jnp.zeros((2 * rows,) + values.shape[1:], values.dtype)
        whole = lax.dynamic_update_slice_in_dim(whole, values, mine * rows, 0)
        values = lax.dynamic_update_slice_in_dim(whole, got, (1 - mine) * rows, 0)
    return values


PAIR = 2 * HEAD_DIM
HIDE = -1000000000.0
VMEM_LIMIT = 50 * 1024 * 1024


def dot(left, right):
    return jnp.dot(left, right, preferred_element_type=F32)


def dot_nt(left, right):
    return lax.dot_general(left, right, (((1,), (1,)), ((), ())), preferred_element_type=F32)


def norm_parts(values):
    center = values - jnp.mean(values, axis=-1, keepdims=True)
    scale = lax.rsqrt(jnp.mean(center * center, axis=-1, keepdims=True) + 1e-05)
    return center * scale, scale


def norm_back(grad, normed, scale):
    along = jnp.mean(grad * normed, axis=-1, keepdims=True)
    return scale * (grad - jnp.mean(grad, axis=-1, keepdims=True) - normed * along)


def params():
    return pltpu.CompilerParams(vmem_limit_bytes=VMEM_LIMIT)


def shaped(shape, dtype):
    return jax.ShapeDtypeStruct(shape, dtype)


def cost(flops, moved, trans=0):
    return pl.CostEstimate(flops=int(flops), bytes_accessed=int(moved), transcendentals=int(trans))


def project_kernel(which_ref, x_ref, gain_ref, weight_ref, *refs):
    first_ref, out_ref = refs[-2:]

    @pl.when(pl.program_id(0) == 0)
    def _():
        normed, _ = norm_parts(x_ref[...].astype(F32))
        first_ref[0] = (normed * gain_ref[...]).astype(BF)

    out_ref[0, 0] = dot(first_ref[0], weight_ref[0]).astype(BF)


def project(which, rows, gain, weight, earlier):
    count, width = rows.shape
    cols = weight.shape[2]
    anywhere = pl.BlockSpec(memory_space=pl.ANY)
    return pl.pallas_call(
        project_kernel,
        grid_spec=pltpu.PrefetchScalarGridSpec(
            num_scalar_prefetch=1,
            grid=(3,),
            in_specs=[
                pl.BlockSpec((count, width), lambda c, w: (0, 0)),
                pl.BlockSpec((1, width), lambda c, w: (0, 0)),
                pl.BlockSpec((1, width, cols), lambda c, w: (c, 0, 0)),
            ]
            + [anywhere] * len(earlier),
            out_specs=[
                pl.BlockSpec((1, count, width), lambda c, w: (w[0], 0, 0)),
                pl.BlockSpec((1, 1, count, cols), lambda c, w: (c, w[0], 0, 0)),
            ],
        ),
        out_shape=[shaped((2, count, width), BF), shaped((3, 2, count, cols), BF)],
        input_output_aliases={4 + i: i for i in range(len(earlier))},
        compiler_params=params(),
        cost_estimate=cost(6 * count * width * cols, 2 * width * (count * 2 + 3 * cols)),
        name="project",
    )(which, rows, gain, weight, *earlier)


def attend_kernel(
    which_ref, q_ref, kd_ref, vd_ref, kc_ref, vc_ref, pos_ref, wo_ref, *refs
):
    context_ref, pd_ref, pc_ref, rl_ref, out_ref, bias_d, bias_c, acc = refs[-8:]
    group = pl.program_id(0)
    count = q_ref.shape[2]
    step = count // 2

    @pl.when(group == 0)
    def _():
        row = lax.broadcasted_iota(jnp.int32, (count, count), 0)
        col = lax.broadcasted_iota(jnp.int32, (count, count), 1)
        start = row - pos_ref[0]
        bias_d[...] = jnp.where((col <= row) & (col >= start), 0.0, HIDE)
        bias_c[...] = jnp.where(col >= start + count, 0.0, HIDE)

    lane = lax.broadcasted_iota(jnp.int32, (1, PAIR), 1) // HEAD_DIM

    def half(late):
        for at in (0, step):
            rows = pl.ds(at, step)
            keys = at + step
            q = q_ref[0, 0, rows, :] * 0.125
            mixed, scale = 0.0, []
            for a in (0, 1):
                mine = jnp.where(lane == a, q, 0.0).astype(BF)
                s_d = dot_nt(mine, kd_ref[0, 0, :keys, :]) + bias_d[rows, :keys]
                top = jnp.max(s_d, axis=-1, keepdims=True)
                if late:
                    s_c = dot_nt(mine, kc_ref[0, 0]) + bias_c[rows, :]
                    top = jnp.maximum(top, jnp.max(s_c, axis=-1, keepdims=True))
                p_d = jnp.exp(s_d - top)
                total = jnp.sum(p_d, axis=-1, keepdims=True)
                p_d = p_d.astype(BF)
                pd_ref[0, a, rows, :keys] = p_d
                value = jnp.where(lane == a, vd_ref[0, 0, :keys, :], 0.0).astype(BF)
                mixed = mixed + dot(p_d, value)
                if late:
                    p_c = jnp.exp(s_c - top)
                    total = total + jnp.sum(p_c, axis=-1, keepdims=True)
                    p_c = p_c.astype(BF)
                    pc_ref[0, a, rows, :] = p_c
                    value = jnp.where(lane == a, vc_ref[0, 0], 0.0).astype(BF)
                    mixed = mixed + dot(p_c, value)
                scale.append(1.0 / total)
            scale = jnp.where(lane == 0, scale[0], scale[1])
            rl_ref[0, rows, :] = scale
            context_ref[0, rows, :] = (mixed * scale).astype(BF)

    pl.when(which_ref[0] == 0)(lambda: half(False))
    pl.when(which_ref[0] == 1)(lambda: half(True))
    part = dot(context_ref[0], wo_ref[...])

    @pl.when(group == 0)
    def _():
        acc[...] = part

    @pl.when(group > 0)
    def _():
        acc[...] += part

    @pl.when(group == pl.num_programs(0) - 1)
    def _():
        out_ref[...] = acc[...].astype(out_ref.dtype)


def attend(which, projected, positions, output_weight, earlier, out_type):
    _, _, count, cols = projected.shape
    width = output_weight.shape[1]
    heads = cols // HEAD_DIM
    anywhere = pl.BlockSpec(memory_space=pl.ANY)

    def block(part, other):
        if other:
            return pl.BlockSpec((1, 1, count, PAIR), lambda g, w: (part, 0, 0, g))
        return pl.BlockSpec((1, 1, count, PAIR), lambda g, w: (part, w[0], 0, g))

    score_spec = pl.BlockSpec((1, 2, count, count), lambda g, w: (w[0], g, 0, 0))
    row_spec = pl.BlockSpec((1, count, PAIR), lambda g, w: (w[0], 0, g))
    return pl.pallas_call(
        attend_kernel,
        grid_spec=pltpu.PrefetchScalarGridSpec(
            num_scalar_prefetch=1,
            grid=(cols // PAIR,),
            in_specs=[
                block(0, False),
                block(1, False),
                block(2, False),
                block(1, True),
                block(2, True),
                pl.BlockSpec((1, count, 1), lambda g, w: (w[0], 0, 0)),
                pl.BlockSpec((PAIR, width), lambda g, w: (g, 0)),
            ]
            + [anywhere] * len(earlier),
            out_specs=[
                row_spec,
                score_spec,
                score_spec,
                row_spec,
                pl.BlockSpec((count, width), lambda g, w: (0, 0)),
            ],
            scratch_shapes=[
                pltpu.VMEM((count, count), F32),
                pltpu.VMEM((count, count), F32),
                pltpu.VMEM((count, width), F32),
            ],
        ),
        out_shape=[
            shaped((2, count, cols), BF),
            shaped((2, heads, count, count), BF),
            shaped((2, heads, count, count), BF),
            shaped((2, count, cols), F32),
            shaped((count, width), out_type),
        ],
        input_output_aliases={8 + i: i for i in range(len(earlier))},
        compiler_params=params(),
        cost_estimate=cost(
            8 * heads * count * count * HEAD_DIM, 8 * heads * count * count, heads * count * count
        ),
        name="attend",
    )(which, *[projected] * 5, positions, output_weight, *earlier)


def hidden_kernel(x_ref, own_ref, theirs_ref, gain_ref, slot_ref, hidden_ref, *out_refs):
    hidden = x_ref[...].astype(F32) + own_ref[...] + theirs_ref[...].astype(F32)
    hidden_ref[...] = hidden
    normed, _ = norm_parts(hidden)
    second = (normed * gain_ref[...]).astype(BF)
    send_rows(second, slot_ref, out_refs)


def send_rows(rows, slot_ref, out_refs):
    capacity = out_refs[0].shape[0]
    for k, ref in enumerate(out_refs):
        slot = lax.broadcasted_iota(jnp.int32, (capacity, rows.shape[0]), 0) + k * capacity
        place = jnp.where(slot_ref[...] == slot, 1.0, 0.0).astype(BF)
        ref[...] = dot(place, rows).astype(BF)


def hidden_rows(x, own, theirs, gain, slot_row, experts):
    count, width = x.shape
    return pl.pallas_call(
        hidden_kernel,
        out_shape=[shaped((count, width), F32)] + [shaped((count // 2, width), BF)] * experts,
        compiler_params=params(),
        cost_estimate=cost(count * count * width * experts, 10 * count * width),
        name="hidden_rows",
    )(x, own, theirs, gain, slot_row)


def send_kernel(rows_ref, slot_ref, *out_refs):
    send_rows(rows_ref[...], slot_ref, out_refs)


def sent_rows(rows, slot_row, experts):
    count, width = rows.shape
    return pl.pallas_call(
        send_kernel,
        out_shape=[shaped((count // 2, width), BF)] * experts,
        compiler_params=params(),
        cost_estimate=cost(count * count * width * experts, 6 * count * width),
        name="sent_rows",
    )(rows, slot_row)


def taken_rows(slot_ref, block_refs):
    count, capacity = slot_ref.shape[0], block_refs[0].shape[0]
    total = 0.0
    for k, ref in enumerate(block_refs):
        slot = lax.broadcasted_iota(jnp.int32, (count, capacity), 1) + k * capacity
        place = jnp.where(slot_ref[...] == slot, 1.0, 0.0).astype(BF)
        total = total + dot(place, ref[...])
    return total


def output_kernel(hidden_ref, slot_ref, *refs):
    refs[-1][...] = (hidden_ref[...] + taken_rows(slot_ref, refs[:-1])).astype(BF)


def output_rows(hidden, slot_col, blocks):
    count, width = hidden.shape
    return pl.pallas_call(
        output_kernel,
        out_shape=shaped((count, width), BF),
        compiler_params=params(),
        cost_estimate=cost(count * count * width * len(blocks), 12 * count * width),
        name="output_rows",
    )(hidden, slot_col, *blocks)


def second_kernel(cot_ref, hidden_ref, gain_ref, slot_ref, *refs):
    grad_ref, low_ref, gain_grad_ref = refs[-3:]
    second_grad = taken_rows(slot_ref, refs[:-3])
    normed, scale = norm_parts(hidden_ref[...])
    gain_grad_ref[...] = jnp.sum(second_grad * normed, axis=0, keepdims=True)
    grad = cot_ref[...].astype(F32) + norm_back(second_grad * gain_ref[...], normed, scale)
    grad_ref[...] = grad
    low_ref[...] = grad.astype(BF)


def second_back(cot, hidden, gain, slot_col, blocks):
    count, width = hidden.shape
    return pl.pallas_call(
        second_kernel,
        out_shape=[
            shaped((count, width), F32),
            shaped((count, width), BF),
            shaped((1, width), F32),
        ],
        compiler_params=params(),
        cost_estimate=cost(count * count * width * len(blocks), 16 * count * width),
        name="second_back",
    )(cot, hidden, gain, slot_col, *blocks)


def first_kernel(x_ref, gain_ref, hidden_grad_ref, own_ref, theirs_ref, out_ref):
    grad = (own_ref[...] + theirs_ref[...].astype(F32)) * gain_ref[...]
    normed, scale = norm_parts(x_ref[...].astype(F32))
    out_ref[...] = hidden_grad_ref[...] + norm_back(grad, normed, scale)


def first_back(x, gain, hidden_grad, own, theirs):
    count, width = x.shape
    return pl.pallas_call(
        first_kernel,
        out_shape=shaped((count, width), F32),
        compiler_params=params(),
        cost_estimate=cost(20 * count * width, 16 * count * width),
        name="first_back",
    )(x, gain, hidden_grad, own, theirs)


def expert_kernel(x_ref, cot_ref, inner_ref, outer_ref, *refs):
    act_ref, pre_ref, grad_ref, out_ref, grad_acc, out_acc = refs[-6:]
    at = pl.program_id(0)
    x = dot(x_ref[...], inner_ref[...])
    act_grad = dot_nt(cot_ref[...], outer_ref[...])
    square = x * x
    tanh = jnp.tanh(x * (0.7978845608028654 + 0.035677408136300125 * square))
    half = 0.5 * (1.0 + tanh)
    act = (x * half).astype(BF)
    slope = half + (0.5 * x) * (1.0 - tanh * tanh) * (
        0.7978845608028654 + 0.10703222440890037 * square
    )
    pre = (act_grad * slope).astype(BF)
    act_ref[0] = act
    pre_ref[0] = pre
    grad = dot_nt(pre, inner_ref[...])
    out = dot(act, outer_ref[...])

    @pl.when(at == 0)
    def _():
        grad_acc[...] = grad
        out_acc[...] = out

    @pl.when(at > 0)
    def _():
        grad_acc[...] += grad
        out_acc[...] += out

    @pl.when(at == pl.num_programs(0) - 1)
    def _():
        grad_ref[...] = grad_acc[...].astype(BF)
        out_ref[...] = out_acc[...].astype(BF)


def expert(index, blocks, x, cot, inner, outer, earlier, tile=512):
    count, width = x.shape
    units = inner.shape[1]
    anywhere = pl.BlockSpec(memory_space=pl.ANY)
    whole = pl.BlockSpec((count, width), lambda j: (0, 0))
    wide = pl.BlockSpec((1, count, tile), lambda j: (index, 0, j))
    return pl.pallas_call(
        expert_kernel,
        grid=(units // tile,),
        in_specs=[
            whole,
            whole,
            pl.BlockSpec((width, tile), lambda j: (0, j)),
            pl.BlockSpec((tile, width), lambda j: (j, 0)),
        ]
        + [anywhere] * len(earlier),
        out_specs=[wide, wide, whole, whole],
        out_shape=[
            shaped((blocks, count, units), BF),
            shaped((blocks, count, units), BF),
            shaped((count, width), BF),
            shaped((count, width), BF),
        ],
        scratch_shapes=[pltpu.VMEM((count, width), F32)] * 2,
        input_output_aliases={4 + i: i for i in range(len(earlier))},
        compiler_params=params(),
        cost_estimate=cost(
            8 * count * width * units, 4 * units * (width + count), count * units
        ),
        name="expert",
    )(x, cot, inner, outer, *earlier)


def back_kernel(
    head_ref, own_ref, other_ref, wo_ref, q_ref, k_ref, v_ref, pd_ref, pc_ref, context_ref, rl_ref,
    first_ref, wp_ref, gain_ref,
    project_ref, output_ref, mine_ref, theirs_ref, gain_grad_ref,
    scaled, acc, key_acc, value_acc, queries,
):
    group = pl.program_id(0)
    count = own_ref.shape[0]
    step = count // 2
    me = head_ref[0]
    lane = lax.broadcasted_iota(jnp.int32, (1, PAIR), 1) // HEAD_DIM
    wo = wo_ref[...]

    context_t = 0.0
    for ref, at in ((own_ref, me), (other_ref, 1 - me)):
        grad = dot_nt(ref[...], wo).astype(BF).astype(F32)
        scaled[at] = grad * rl_ref[at]
        context_t = context_t + lax.dot_general(
            context_ref[at], ref[...], (((0,), (0,)), ((), ())), preferred_element_type=F32
        )
    output_ref[...] = context_t.astype(BF)
    key_acc[...] = jnp.zeros_like(key_acc)
    value_acc[...] = jnp.zeros_like(value_acc)

    for h in (0, 1):
        for at in (0, step):
            rows = pl.ds(at, step)
            grads = scaled[h, rows, :]
            context = context_ref[h, rows, :].astype(F32)
            low = grads.astype(BF)
            through = low.astype(F32) * context
            low_t = jnp.transpose(grads).astype(BF)
            q_t = jnp.transpose(q_ref[0, h, rows, :].astype(F32)).astype(BF)
            query = 0.0
            for a in (0, 1):
                line = pl.ds(a * HEAD_DIM, HEAD_DIM)
                mine = jnp.where(lane == a, low, 0.0).astype(BF)
                total = jnp.sum(jnp.where(lane == a, through, 0.0), axis=-1, keepdims=True)
                parts = [(pd_ref, h, h * count, at + step)]
                if h:
                    parts.append((pc_ref, 0, 0, count))
                for p_ref, p_at, key_at, keys in parts:
                    source = key_at // count
                    p = p_ref[p_at, a, rows, :keys]
                    prob_grad = dot_nt(mine, v_ref[0, source, :keys, :])
                    score = (p.astype(F32) * (prob_grad - total)).astype(BF)
                    k = jnp.where(lane == a, k_ref[0, source, :keys, :], 0.0).astype(BF)
                    query = query + dot(score, k)
                    cols = pl.ds(key_at, keys)
                    key_acc[line, cols] += dot(q_t[a * HEAD_DIM : (a + 1) * HEAD_DIM], score)
                    value_acc[line, cols] += dot(low_t[a * HEAD_DIM : (a + 1) * HEAD_DIM], p)
            queries[pl.ds(h * count + at, step), :] = query * 0.125

    query = queries[...]
    key_t = key_acc[...] * 0.125
    value_t = value_acc[...]
    both = jnp.concatenate(
        [query.astype(BF), jnp.transpose(key_t).astype(BF), jnp.transpose(value_t).astype(BF)],
        axis=1,
    )
    both_t = jnp.concatenate(
        [jnp.transpose(query).astype(BF), key_t.astype(BF), value_t.astype(BF)], axis=0
    )
    first = jnp.concatenate([first_ref[0], first_ref[1]], axis=0)
    weight_t = dot(both_t, first)
    for c in range(3):
        project_ref[c] = weight_t[c * PAIR : (c + 1) * PAIR].astype(BF)
    weight = jnp.concatenate([wp_ref[0], wp_ref[1], wp_ref[2]], axis=1)
    part = dot_nt(both, weight)

    @pl.when(group == 0)
    def _():
        for h in (0, 1):
            acc[h] = part[h * count : (h + 1) * count]

    @pl.when(group > 0)
    def _():
        for h in (0, 1):
            acc[h] += part[h * count : (h + 1) * count]

    @pl.when(group == pl.num_programs(0) - 1)
    def _():
        mine_ref[...] = acc[me]
        theirs_ref[...] = acc[1 - me].astype(BF)
        total = 0.0
        for h in (0, 1):
            total = total + jnp.sum(acc[h] * first_ref[h].astype(F32), axis=0, keepdims=True)
        gain_grad_ref[...] = total / gain_ref[...]


def attend_back(
    me, own, other, output_weight, projected, p_diag, p_cross, context, inverse, first, weight, gain
):
    _, _, count, cols = projected.shape
    width = output_weight.shape[1]
    heads = cols // HEAD_DIM
    rows = pl.BlockSpec((count, width), lambda g, w: (0, 0))

    def block(part):
        return pl.BlockSpec((1, 2, count, PAIR), lambda g, w: (part, 0, 0, g))

    halves = pl.BlockSpec((2, count, PAIR), lambda g, w: (0, 0, g))
    return pl.pallas_call(
        back_kernel,
        grid_spec=pltpu.PrefetchScalarGridSpec(
            num_scalar_prefetch=1,
            grid=(cols // PAIR,),
            in_specs=[
                rows,
                rows,
                pl.BlockSpec((PAIR, width), lambda g, w: (g, 0)),
                block(0),
                block(1),
                block(2),
                pl.BlockSpec((2, 2, count, count), lambda g, w: (0, g, 0, 0)),
                pl.BlockSpec((1, 2, count, count), lambda g, w: (1, g, 0, 0)),
                halves,
                halves,
                pl.BlockSpec((2, count, width), lambda g, w: (0, 0, 0)),
                pl.BlockSpec((3, width, PAIR), lambda g, w: (0, 0, g)),
                pl.BlockSpec((1, width), lambda g, w: (0, 0)),
            ],
            out_specs=[
                pl.BlockSpec((3, PAIR, width), lambda g, w: (0, g, 0)),
                pl.BlockSpec((PAIR, width), lambda g, w: (g, 0)),
                rows,
                rows,
                pl.BlockSpec((1, width), lambda g, w: (0, 0)),
            ],
            scratch_shapes=[
                pltpu.VMEM((2, count, PAIR), F32),
                pltpu.VMEM((2, count, width), F32),
                pltpu.VMEM((PAIR, 2 * count), F32),
                pltpu.VMEM((PAIR, 2 * count), F32),
                pltpu.VMEM((2 * count, PAIR), F32),
            ],
        ),
        out_shape=[
            shaped((3, cols, width), BF),
            shaped((cols, width), BF),
            shaped((count, width), F32),
            shaped((count, width), BF),
            shaped((1, width), F32),
        ],
        compiler_params=params(),
        cost_estimate=cost(
            24 * heads * count * count * HEAD_DIM, 8 * heads * count * count
        ),
        name="attend_back",
    )(
        me, own, other, output_weight, projected, projected, projected, p_diag, p_cross,
        context, inverse, first, weight, gain,
    )


def on_device(
    block_input,
    output_cotangent,
    token_ids,
    positions,
    hash_table,
    first_gain,
    second_gain,
    project_weight,
    output_weight,
    expert_inner,
    expert_outer,
):
    tok_rows, model_width = block_input.shape
    local_cols = output_weight.shape[0]
    expert_count = lax.axis_size("expert")
    capacity = tok_rows // 2
    inner_weight = expert_inner[0]
    outer_weight = expert_outer[0]
    my_head = lax.axis_index("head")
    my_expert = lax.axis_index("expert")
    own_at = my_head.reshape(1).astype(jnp.int32)
    other_at = 1 - own_at
    first_gain = first_gain.reshape(1, model_width)
    second_gain = second_gain.reshape(1, model_width)

    other_input = swap(block_input, "head", 1)
    other_pos = swap(positions, "head", 1)
    seq_pos = jnp.where(
        my_head == 0, jnp.stack([positions, other_pos]), jnp.stack([other_pos, positions])
    )[:, :, None]

    chosen = jnp.take(hash_table, token_ids)
    relative = chosen ^ my_expert
    one_hot = relative[:, None] == jnp.arange(expert_count, dtype=jnp.int32)[None, :]
    rank_table = jnp.cumsum(one_hot.astype(jnp.int32), axis=0) - 1
    slot_index = relative * capacity + jnp.sum(jnp.where(one_hot, rank_table, 0), axis=1)
    slot_row, slot_col = slot_index[None, :], slot_index[:, None]

    def exchange(blocks):
        return [blocks[0]] + [swap(blocks[k], "expert", k) for k in range(1, expert_count)]

    grad_blocks = exchange(sent_rows(output_cotangent, slot_row, expert_count))

    done = project(own_at, block_input, first_gain, project_weight, [])
    first_low, projected = project(other_at, other_input, first_gain, project_weight, done)
    *done, theirs = attend(other_at, projected, seq_pos, output_weight, [], BF)
    theirs = swap(theirs, "head", 1)
    context, p_diag, p_cross, inverse, mine = attend(
        own_at, projected, seq_pos, output_weight, done, F32
    )
    hidden, *outgoing = hidden_rows(
        block_input, mine, theirs, second_gain, slot_row, expert_count
    )

    row_blocks = exchange(outgoing)
    done, rows_grad, produced = [], [], []
    for k in range(expert_count):
        *done, grad, out = expert(
            k, expert_count, row_blocks[k], grad_blocks[k], inner_weight, outer_weight, done
        )
        rows_grad.append(grad)
        produced.append(out)
    returned = exchange(rows_grad)
    combined = exchange(produced)
    activated, pre_grad = [
        values.reshape(expert_count * capacity, inner_weight.shape[1]) for values in done
    ]
    arrived = jnp.concatenate(row_blocks, axis=0)
    grad_arrived = jnp.concatenate(grad_blocks, axis=0)
    block_output = output_rows(hidden, slot_col, combined)

    core = side("dp", 1)

    def halves_sum(left, right):
        def part(which):
            cols = left.shape[1] // 2
            return lax.dot_general(
                lax.dynamic_slice_in_dim(left, which * cols, cols, 1),
                right,
                (((0,), (0,)), ((), ())),
                preferred_element_type=F32,
            )

        got = swap(part(1 - core).astype(BF), "dp", 1)
        return (part(core) + got.astype(F32)).astype(BF)

    steps = bits_of("dp", 2) + bits_of("head")
    outer_part = scatter_sum(halves_sum(activated, grad_arrived), steps)
    inner_part = scatter_sum(halves_sum(arrived, pre_grad), steps[::-1])
    outer_total = gather_back(gather_back(outer_part, steps), [("dp", 1)]).astype(F32)
    inner_total = gather_back(gather_back(inner_part, steps[::-1]), [("dp", 1)]).astype(F32)

    hidden_grad, hidden_low, second_gain_part = second_back(
        output_cotangent, hidden, second_gain, slot_col, returned
    )

    other_low = swap(hidden_low, "head", 1)
    project_part, weight_run, mine, theirs, first_gain_part = attend_back(
        own_at, hidden_low, other_low, output_weight, projected, p_diag, p_cross, context, inverse,
        first_low, project_weight, first_gain,
    )
    theirs = swap(theirs, "head", 1)
    input_grad = first_back(block_input, first_gain, hidden_grad, mine, theirs)

    gains = jnp.concatenate([first_gain_part, second_gain_part], axis=0)
    for axis, bit in bits_of("dp") + bits_of("expert") + bits_of("head"):
        gains = gains + swap(gains, axis, bit)

    steps = bits_of("dp") + bits_of("expert")
    project_part = project_part.reshape(3 * local_cols, model_width)
    project_grad = gather_back(scatter_sum(project_part, steps), steps).astype(F32)
    project_grad = project_grad.reshape(3, local_cols, model_width).swapaxes(1, 2)
    output_weight_grad = gather_back(scatter_sum(weight_run, steps), steps).astype(F32)
    return (
        block_output,
        input_grad,
        gains[0],
        gains[1],
        project_grad,
        output_weight_grad,
        inner_total[None],
        outer_total[None],
    )


def solution(mesh):
    in_specs = (
        P(("dp", "expert", "head"), None),
        P(("dp", "expert", "head"), None),
        P(("dp", "expert", "head")),
        P(("dp", "expert", "head")),
        P(),
        P(),
        P(),
        P(None, None, "head"),
        P("head", None),
        P("expert", None, None),
        P("expert", None, None),
    )
    out_specs = (
        P(("dp", "expert", "head"), None),
        P(("dp", "expert", "head"), None),
        P(),
        P(),
        P(None, None, "head"),
        P("head", None),
        P("expert", None, None),
        P("expert", None, None),
    )
    return jax.shard_map(
        on_device, mesh=mesh, in_specs=in_specs, out_specs=out_specs, check_vma=False
    )
```

```python
import functools

import jax
import jax.numpy as jnp
from jax import lax
from jax.experimental import pallas as pl
from jax.experimental.pallas import tpu as pltpu
from jax.sharding import Mesh
from jax.sharding import PartitionSpec as P

HEAD_DIM = 64
BF = jnp.bfloat16
F32 = jnp.float32


def swap(values, axis, bit, name):
    size = lax.axis_size(axis)
    with jax.named_scope(name):
        return lax.ppermute(values, axis, [(i, i ^ bit) for i in range(size)])


def bits_of(axis, low=1):
    size = lax.axis_size(axis)
    found = []
    while low < size:
        found.append((axis, low))
        low *= 2
    return found


def side(axis, bit):
    return (lax.axis_index(axis) // bit) % 2


PAIR = 2 * HEAD_DIM
ATTEND_FLOPS = 20 * 10**9
BACK_FLOPS = 300 * 10**9
HIDE = -1000000000.0
VMEM_LIMIT = 64 * 1024 * 1024


def dot(left, right):
    return jnp.dot(left, right, preferred_element_type=F32)


def dot_nt(left, right):
    return lax.dot_general(left, right, (((1,), (1,)), ((), ())), preferred_element_type=F32)


def norm_parts(values):
    center = values - jnp.mean(values, axis=-1, keepdims=True)
    scale = lax.rsqrt(jnp.mean(center * center, axis=-1, keepdims=True) + 1e-05)
    return center * scale, scale


def norm_back(grad, normed, scale):
    along = jnp.mean(grad * normed, axis=-1, keepdims=True)
    return scale * (grad - jnp.mean(grad, axis=-1, keepdims=True) - normed * along)


def shaped(shape, dtype):
    return jax.ShapeDtypeStruct(shape, dtype)


def call(kernel, operands, after=(), alias=(), prefetch=(), flops=1, **options):
    extra = [*alias, *after]
    anywhere = pl.BlockSpec(memory_space=pl.ANY)
    options["in_specs"] = [*options["in_specs"], *[anywhere] * len(extra)]
    first = len(prefetch) + len(operands)
    fixed, skip = len(operands), len(extra)

    def body(*refs):
        cut = len(prefetch) + fixed
        kernel(*refs[:cut], *refs[cut + skip :])

    if prefetch:
        specs = {name: options.pop(name) for name in ("grid", "in_specs", "out_specs")}
        specs["scratch_shapes"] = options.pop("scratch_shapes", ())
        options["grid_spec"] = pltpu.PrefetchScalarGridSpec(
            num_scalar_prefetch=len(prefetch), **specs
        )
    return pl.pallas_call(
        body,
        input_output_aliases={first + i: i for i in range(len(alias))},
        compiler_params=pltpu.CompilerParams(vmem_limit_bytes=VMEM_LIMIT),
        cost_estimate=pl.CostEstimate(flops=flops, bytes_accessed=1, transcendentals=0),
        **options,
    )(*prefetch, *operands, *extra)


def whole(shape):
    return pl.BlockSpec(shape, lambda *_: (0,) * len(shape))


def plain(kernel, operands, out_shape, name, after=(), scratch=(), flops=1):
    return call(
        kernel,
        operands,
        after=after,
        flops=flops,
        grid=(1,),
        in_specs=[whole(x.shape) for x in operands],
        out_specs=jax.tree.map(lambda s: whole(s.shape), out_shape),
        out_shape=out_shape,
        scratch_shapes=scratch,
        name=name,
    )


def project_kernel(which_ref, x_ref, gain_ref, weight_ref, first_ref, out_ref):
    @pl.when(pl.program_id(0) == 0)
    def _():
        normed, _ = norm_parts(x_ref[...].astype(F32))
        first_ref[0] = (normed * gain_ref[...]).astype(BF)

    out_ref[0, 0] = dot(first_ref[0], weight_ref[0]).astype(BF)


def project(which, rows, gain, weight, earlier, after=()):
    count, width = rows.shape
    cols = weight.shape[2]
    return call(
        project_kernel,
        [rows, gain, weight],
        after=after,
        alias=earlier,
        prefetch=[which],
        grid=(3,),
        in_specs=[
            whole((count, width)),
            whole((1, width)),
            pl.BlockSpec((1, width, cols), lambda c, w: (c, 0, 0)),
        ],
        out_specs=[
            pl.BlockSpec((1, count, width), lambda c, w: (w[0], 0, 0)),
            pl.BlockSpec((1, 1, count, cols), lambda c, w: (c, w[0], 0, 0)),
        ],
        out_shape=[shaped((2, count, width), BF), shaped((3, 2, count, cols), BF)],
        name="project",
    )


def attend_kernel(
    which_ref, q_ref, kd_ref, vd_ref, kc_ref, vc_ref, pos_ref,
    pd_ref, pc_ref, rl_ref, context_ref, bias_d, bias_c,
):
    count = q_ref.shape[2]
    step = count // 2

    @pl.when(pl.program_id(0) == 0)
    def _():
        row = lax.broadcasted_iota(jnp.int32, (count, count), 0)
        col = lax.broadcasted_iota(jnp.int32, (count, count), 1)
        start = row - pos_ref[0]
        bias_d[...] = jnp.where((col <= row) & (col >= start), 0.0, HIDE)
        bias_c[...] = jnp.where(col >= start + count, 0.0, HIDE)

    lane = lax.broadcasted_iota(jnp.int32, (1, PAIR), 1) // HEAD_DIM

    def half(late):
        for at in (0, step):
            rows = pl.ds(at, step)
            keys = at + step
            q = q_ref[0, 0, rows, :] * 0.125
            mixed, scale = 0.0, []
            for a in (0, 1):
                mine = jnp.where(lane == a, q, 0.0).astype(BF)
                s_d = dot_nt(mine, kd_ref[0, 0, :keys, :]) + bias_d[rows, :keys]
                top = jnp.max(s_d, axis=-1, keepdims=True)
                if late:
                    s_c = dot_nt(mine, kc_ref[0, 0]) + bias_c[rows, :]
                    top = jnp.maximum(top, jnp.max(s_c, axis=-1, keepdims=True))
                p_d = jnp.exp(s_d - top)
                total = jnp.sum(p_d, axis=-1, keepdims=True)
                p_d = p_d.astype(BF)
                pd_ref[0, a, rows, :keys] = p_d
                value = jnp.where(lane == a, vd_ref[0, 0, :keys, :], 0.0).astype(BF)
                mixed = mixed + dot(p_d, value)
                if late:
                    p_c = jnp.exp(s_c - top)
                    total = total + jnp.sum(p_c, axis=-1, keepdims=True)
                    p_c = p_c.astype(BF)
                    pc_ref[0, a, rows, :] = p_c
                    value = jnp.where(lane == a, vc_ref[0, 0], 0.0).astype(BF)
                    mixed = mixed + dot(p_c, value)
                scale.append(1.0 / total)
            scale = jnp.where(lane == 0, scale[0], scale[1])
            rl_ref[0, rows, :] = scale
            context_ref[rows, :] = (mixed * scale).astype(BF)

    pl.when(which_ref[0] == 0)(lambda: half(False))
    pl.when(which_ref[0] == 1)(lambda: half(True))


def attend(which, projected, positions, earlier, after=(), flops=1):
    _, _, count, cols = projected.shape
    heads = cols // HEAD_DIM

    def block(part, other):
        if other:
            return pl.BlockSpec((1, 1, count, PAIR), lambda g, w: (part, 0, 0, g))
        return pl.BlockSpec((1, 1, count, PAIR), lambda g, w: (part, w[0], 0, g))

    score_spec = pl.BlockSpec((1, 2, count, count), lambda g, w: (w[0], g, 0, 0))
    return call(
        attend_kernel,
        [*[projected] * 5, positions],
        after=after,
        alias=earlier,
        prefetch=[which],
        flops=flops,
        grid=(cols // PAIR,),
        in_specs=[
            block(0, False),
            block(1, False),
            block(2, False),
            block(1, True),
            block(2, True),
            pl.BlockSpec((1, count, 1), lambda g, w: (w[0], 0, 0)),
        ],
        out_specs=[
            score_spec,
            score_spec,
            pl.BlockSpec((1, count, PAIR), lambda g, w: (w[0], 0, g)),
            pl.BlockSpec((count, PAIR), lambda g, w: (0, g)),
        ],
        scratch_shapes=[pltpu.VMEM((count, count), F32)] * 2,
        out_shape=[
            shaped((2, heads, count, count), BF),
            shaped((2, heads, count, count), BF),
            shaped((2, count, cols), F32),
            shaped((count, cols), BF),
        ],
        name="attend",
    )


def hidden_kernel(
    x_ref, own_ref, got_ref, own_weight_ref, got_weight_ref, gain_ref, slot_ref, hidden_ref, *out_refs
):
    attended = dot(own_ref[...], own_weight_ref[...]) + dot(got_ref[...], got_weight_ref[...])
    hidden = x_ref[...].astype(F32) + attended
    hidden_ref[...] = hidden
    normed, _ = norm_parts(hidden)
    second = (normed * gain_ref[...]).astype(BF)
    send_rows(second, slot_ref, out_refs)


def send_rows(rows, slot_ref, out_refs):
    capacity = out_refs[0].shape[0]
    for k, ref in enumerate(out_refs):
        slot = lax.broadcasted_iota(jnp.int32, (capacity, rows.shape[0]), 0) + k * capacity
        place = jnp.where(slot_ref[...] == slot, 1.0, 0.0).astype(BF)
        ref[...] = dot(place, rows).astype(BF)


def hidden_rows(x, own, got, own_weight, got_weight, gain, slot_row, experts, after=()):
    count, width = x.shape
    out = [shaped((count, width), F32)] + [shaped((count // 2, width), BF)] * experts
    return plain(
        hidden_kernel,
        [x, own, got, own_weight, got_weight, gain, slot_row],
        out,
        "hidden_rows",
        after,
    )


def send_kernel(rows_ref, slot_ref, out_ref):
    send_rows(rows_ref[...], slot_ref, [out_ref.at[k] for k in range(out_ref.shape[0])])


def sent_rows(rows, slot_row, experts):
    count, width = rows.shape
    out = shaped((experts, count // 2, width), BF)
    return plain(send_kernel, [rows, slot_row], out, "sent_rows")


def taken_rows(slot_ref, block_refs):
    count, capacity = slot_ref.shape[0], block_refs[0].shape[0]
    total = 0.0
    for k, ref in enumerate(block_refs):
        slot = lax.broadcasted_iota(jnp.int32, (count, capacity), 1) + k * capacity
        place = jnp.where(slot_ref[...] == slot, 1.0, 0.0).astype(BF)
        total = total + dot(place, ref[...])
    return total


def output_kernel(hidden_ref, slot_ref, *refs):
    blocks = [refs[0].at[k] for k in range(refs[0].shape[0])]
    refs[-1][...] = (hidden_ref[...] + taken_rows(slot_ref, blocks)).astype(BF)


def output_rows(hidden, slot_col, blocks, after=()):
    return plain(
        output_kernel,
        [hidden, slot_col, blocks],
        shaped(hidden.shape, BF),
        "output_rows",
        after,
    )


def second_kernel(cot_ref, hidden_ref, gain_ref, slot_ref, own_weight_ref, got_weight_ref, *refs):
    grad_ref, low_ref, gain_grad_ref, own_ref, send_ref = refs[-5:]
    second_grad = taken_rows(slot_ref, refs[:-5])
    normed, scale = norm_parts(hidden_ref[...])
    gain_grad_ref[...] = jnp.sum(second_grad * normed, axis=0, keepdims=True)
    grad = cot_ref[...].astype(F32) + norm_back(second_grad * gain_ref[...], normed, scale)
    grad_ref[...] = grad
    low = grad.astype(BF)
    low_ref[...] = low
    send_ref[...] = dot_nt(low, got_weight_ref[...]).astype(BF)
    own_ref[...] = dot_nt(low, own_weight_ref[...]).astype(BF)


def second_back(cot, hidden, gain, slot_col, own_weight, got_weight, blocks, after=()):
    count, width = hidden.shape
    part = shaped((count, own_weight.shape[0]), BF)
    out = [
        shaped((count, width), F32),
        shaped((count, width), BF),
        shaped((1, width), F32),
        part,
        part,
    ]
    return plain(
        second_kernel,
        [cot, hidden, gain, slot_col, own_weight, got_weight, *blocks],
        out,
        "second_back",
        after,
        flops=BACK_FLOPS,
    )


def output_weight_kernel(
    core_ref, own_ref, got_ref, low_ref, own_out, kept_out, sent_out, scratch
):
    def part(ref):
        return lax.dot_general(
            ref[...], low_ref[...], (((0,), (0,)), ((), ())), preferred_element_type=F32
        ).astype(BF)

    scratch[...] = part(got_ref)
    rows = kept_out.shape[0]
    for ref, half in ((kept_out, core_ref[0]), (sent_out, 1 - core_ref[0])):
        ref[...] = scratch[pl.ds(pl.multiple_of(half * rows, rows), rows), :]
    own_out[...] = part(own_ref)


def output_weight_parts(core, own, got, low, after=()):
    cols, width = own.shape[1], low.shape[1]
    part = shaped((cols // 2, width), BF)
    out = [shaped((cols, width), BF), part, part]
    return call(
        output_weight_kernel,
        [own, got, low],
        after=after,
        prefetch=[core.reshape(1).astype(jnp.int32)],
        grid=(1,),
        in_specs=[whole(x.shape) for x in (own, got, low)],
        out_specs=[whole(o.shape) for o in out],
        out_shape=out,
        scratch_shapes=[pltpu.VMEM((cols, width), BF)],
        name="output_weight_parts",
    )


def first_kernel(x_ref, gain_ref, hidden_grad_ref, own_ref, theirs_ref, out_ref):
    grad = (own_ref[...] + theirs_ref[...].astype(F32)) * gain_ref[...]
    normed, scale = norm_parts(x_ref[...].astype(F32))
    out_ref[...] = hidden_grad_ref[...] + norm_back(grad, normed, scale)


def first_back(x, gain, hidden_grad, own, theirs, after=()):
    return plain(
        first_kernel, [x, gain, hidden_grad, own, theirs], shaped(x.shape, F32), "first_back", after
    )


def fill(target, refs):
    rows = refs[0].shape[0]
    for i, ref in enumerate(refs):
        target[i * rows : (i + 1) * rows] = ref[...]


def expert_kernel(count, sub, place_ref, *refs):
    x_refs, cot_refs, refs = refs[:count], refs[count : 2 * count], refs[2 * count :]
    inner_ref, outer_ref, act_ref, pre_ref, out_ref, *grad_refs, x, cot, grad_acc, out_acc = refs
    at = pl.program_id(0)
    last = pl.num_programs(0) - count
    size = out_ref.shape[1]

    @pl.when(at > last)
    def _():
        rows = pl.ds(pl.multiple_of((at - last) * size, size), size)
        out_ref[0] = out_acc[rows, :].astype(BF)

    pl.when(at <= last)(
        lambda: expert_step(
            count, sub, x_refs, cot_refs, inner_ref, outer_ref, act_ref, pre_ref, out_ref,
            grad_refs, x, cot, grad_acc, out_acc, at, last,
        )
    )


def expert_step(
    count, sub, x_refs, cot_refs, inner_ref, outer_ref, act_ref, pre_ref, out_ref, grad_refs,
    x, cot, grad_acc, out_acc, at, last,
):

    @pl.when(at == 0)
    def _():
        fill(x, x_refs)
        fill(cot, [ref.at[0] for ref in cot_refs])
        grad_acc[...] = jnp.zeros_like(grad_acc)
        out_acc[...] = jnp.zeros_like(out_acc)

    def front(i):
        cols = slice(i * sub, (i + 1) * sub)
        return dot(x[...], inner_ref[:, cols]), dot_nt(cot[...], outer_ref[cols, :])

    parts = inner_ref.shape[1] // sub
    now = front(0)
    for i in range(parts):
        later = front(i + 1) if i + 1 < parts else None
        value, grad = now
        square = value * value
        half = 0.5 + 0.5 * jnp.tanh(
            value * (0.7978845608028654 + 0.035677408136300125 * square)
        )
        act = value * half
        slope = half + act * (1.0 - half) * (1.5957691216057308 + 0.21406444881780074 * square)
        cols = slice(i * sub, (i + 1) * sub)
        act_ref[:, cols] = act.astype(BF)
        pre_ref[:, cols] = (grad * slope).astype(BF)
        now = later
    grad_acc[...] += dot_nt(pre_ref[...], inner_ref[...])
    out_acc[...] += dot(act_ref[...], outer_ref[...])

    @pl.when(at == last)
    def _():
        size = out_ref.shape[1]
        out_ref[0] = out_acc[:size].astype(BF)
        for i, ref in enumerate(grad_refs):
            ref[...] = grad_acc[i * size : (i + 1) * size].astype(BF)


def expert(index, blocks, cot, places, inner, outer, earlier, after=(), tile=768, sub=256):
    count, width = blocks[0].shape
    size, units = len(blocks), inner.shape[1]
    total = count * cot.shape[0]
    tiles = units // tile

    def held(j):
        return jnp.minimum(j, tiles - 1)

    wide = pl.BlockSpec((count * size, tile), lambda j, p: (index // size, held(j)))
    out = pl.BlockSpec(
        (1, count, width), lambda j, p: (p[jnp.maximum(j - tiles + 1, 0)], 0, 0)
    )

    def placed(i):
        return pl.BlockSpec((1, count, width), lambda j, p: (p[i], 0, 0))

    return call(
        functools.partial(expert_kernel, size, sub),
        [*blocks, *[cot] * size, inner, outer],
        after=after,
        alias=earlier,
        prefetch=[jnp.stack(places).astype(jnp.int32)],
        grid=(tiles + size - 1,),
        in_specs=[whole((count, width))] * size
        + [placed(i) for i in range(size)]
        + [
            pl.BlockSpec((width, tile), lambda j, p: (0, held(j))),
            pl.BlockSpec((tile, width), lambda j, p: (held(j), 0)),
        ],
        out_specs=[wide, wide, out] + [whole((count, width))] * size,
        out_shape=[shaped((total, units), BF)] * 2
        + [shaped(cot.shape, BF)]
        + [shaped((count, width), BF)] * size,
        scratch_shapes=[pltpu.VMEM((count * size, width), BF)] * 2
        + [pltpu.VMEM((count * size, width), F32)] * 2,
        name="expert",
    )


def weight_kernel(is_outer, count, which_ref, place_ref, wide_ref, *refs):
    *row_refs, out_ref, rows = refs
    if is_outer:
        row_refs = [row_refs[0].at[place_ref[i]] for i in range(count)]
    pl.when(pl.program_id(0) == 0)(lambda: fill(rows, row_refs))
    sides = (wide_ref[...], rows[...]) if is_outer else (rows[...], wide_ref[...])
    out_ref[...] = lax.dot_general(
        *sides, (((0,), (0,)), ((), ())), preferred_element_type=F32
    ).astype(BF)


def weight_part(is_outer, half, blocks, places, wide, after=(), tiles=4):
    count, width = blocks[0].shape
    total, units = wide.shape
    tile = units // 2 // tiles
    if is_outer:
        row_specs, blocks = [whole(blocks.shape)], [blocks]
        shape, spec = (units // 2, width), pl.BlockSpec((tile, width), lambda j, w, p: (j, 0))
    else:
        row_specs = [whole((count, width))] * len(blocks)
        shape, spec = (width, units // 2), pl.BlockSpec((width, tile), lambda j, w, p: (0, j))
    return call(
        functools.partial(weight_kernel, is_outer, len(places)),
        [wide, *blocks],
        after=after,
        prefetch=[half.reshape(1).astype(jnp.int32), jnp.stack(places).astype(jnp.int32)],
        grid=(tiles,),
        in_specs=[pl.BlockSpec((total, tile), lambda j, w, p: (0, w[0] * tiles + j))] + row_specs,
        out_specs=spec,
        out_shape=shaped(shape, BF),
        scratch_shapes=[pltpu.VMEM((total, width), BF)],
        name="weight_part",
    )


def split_kernel(place_ref, kept_ref, got_ref, sent_out, kept_out):
    total = (kept_ref[...].astype(F32) + got_ref[...].astype(F32)).astype(BF)
    half = pl.num_programs(0) // 2

    @pl.when(pl.program_id(0) < half)
    def _():
        sent_out[...] = total

    @pl.when(pl.program_id(0) >= half)
    def _():
        kept_out[...] = total


def split_sum(kept, got, turn, by_rows, after=(), tiles=4):
    rows, cols = kept.shape
    if by_rows:
        tile, out = (rows // tiles, cols), (rows // 2, cols)
    else:
        tile, out = (rows, cols // tiles), (rows, cols // 2)

    def at(j):
        return (j, 0) if by_rows else (0, j)

    def place(j, w):
        return at((w[0] * (tiles // 2) + j) % tiles)

    return call(
        split_kernel,
        [kept, got],
        after=after,
        prefetch=[turn.reshape(1).astype(jnp.int32)],
        grid=(tiles,),
        in_specs=[pl.BlockSpec(tile, place)] * 2,
        out_specs=[
            pl.BlockSpec(tile, lambda j, w: at(jnp.minimum(j, tiles // 2 - 1))),
            pl.BlockSpec(tile, lambda j, w: at(jnp.maximum(j - tiles // 2, 0))),
        ],
        out_shape=[shaped(out, BF)] * 2,
        name="split_sum",
    )


def assemble_kernel(place_ref, *refs):
    *piece_refs, out_ref = refs
    for i, ref in enumerate(piece_refs):

        @pl.when(pl.program_id(0) == i)
        def _(ref=ref):
            out_ref[...] = ref[...].astype(F32)


def assemble(pieces, places, shape, earlier, after=()):
    size = pieces[0].shape
    table = jnp.stack([jnp.stack(place) for place in places]).astype(jnp.int32)
    return call(
        assemble_kernel,
        pieces,
        after=after,
        alias=earlier,
        prefetch=[table],
        grid=(len(pieces),),
        in_specs=[whole(size)] * len(pieces),
        out_specs=[pl.BlockSpec(size, lambda i, t: (t[i, 0], t[i, 1]))],
        out_shape=[shaped(shape, F32)],
        name="assemble",
    )


def add_kernel(more_at, place_ref, kept_ref, got_ref, *refs):
    out_refs, more_refs = (refs, ()) if more_at is None else (refs[1:-1], refs[:1])
    rows = out_refs[0].shape[0]
    if more_refs:
        kept_ref, scratch = refs[-1], kept_ref
        kept_ref[...] = scratch[...].astype(F32)
        span = pl.ds(more_at, more_refs[0].shape[0])
        for ref in more_refs:
            kept_ref[span, :] += ref[...].astype(F32)
    for i, ref in enumerate(out_refs):
        cut = pl.ds(pl.multiple_of(place_ref[i] * rows, rows), rows)
        ref[...] = (kept_ref[cut, :].astype(F32) + got_ref[cut, :].astype(F32)).astype(BF)


def add(kept, got, places, after=(), more=(), more_at=None):
    shape = kept.shape
    out = [shaped((shape[0] // len(places), *shape[1:]), BF)] * len(places)
    return call(
        functools.partial(add_kernel, more_at),
        [kept, got, *more],
        after=after,
        prefetch=[jnp.stack(places).astype(jnp.int32)],
        grid=(1,),
        in_specs=[whole(shape)] * 2 + [whole(x.shape) for x in more],
        out_specs=[whole(o.shape) for o in out],
        scratch_shapes=[pltpu.VMEM(shape, F32)] if more else [],
        out_shape=out,
        name="add",
    )


def adds_kernel(count, cuts, place_ref, *refs):
    in_refs, out_refs = refs[: 2 * count], refs[2 * count :]
    for i in range(count):
        kept_ref, got_ref = in_refs[2 * i : 2 * i + 2]
        for j in range(cuts):
            ref = out_refs[cuts * i + j]
            rows = ref.shape[0]
            cut = pl.ds(pl.multiple_of(place_ref[cuts * i + j] * rows, rows), rows)
            ref[...] = (kept_ref[cut, :].astype(F32) + got_ref[cut, :].astype(F32)).astype(BF)


def adds(pairs, places, after=()):
    cuts = len(places[0])
    out = [
        shaped((kept.shape[0] // cuts, kept.shape[1]), BF) for kept, _ in pairs for _ in range(cuts)
    ]
    operands = [x for pair in pairs for x in pair]
    parts = call(
        functools.partial(adds_kernel, len(pairs), cuts),
        operands,
        after=after,
        prefetch=[jnp.stack([p for at in places for p in at]).astype(jnp.int32)],
        grid=(1,),
        in_specs=[whole(x.shape) for x in operands],
        out_specs=[whole(o.shape) for o in out],
        out_shape=out,
        name="adds",
    )
    return [parts[cuts * i : cuts * (i + 1)] for i in range(len(pairs))]


def gather_pieces(own, steps, order):
    weights = {step: 1 << (len(steps) - 1 - i) for i, step in enumerate(steps)}
    place = sum(side(*step) * weight for step, weight in weights.items())
    pieces = [(place, own)]
    for step in order:
        change = weights[step] * (1 - 2 * side(*step))
        pieces += [(at + change, swap(piece, *step, "piece")) for at, piece in pieces]
    return pieces


def total_kernel(in_ref, out_ref):
    count = in_ref.shape[0]
    value = sum(in_ref[i].astype(F32) for i in range(count)).astype(BF)
    for i in range(count):
        out_ref[i] = value


def total(blocks, after=()):
    return plain(total_kernel, [blocks], shaped(blocks.shape, BF), "total", after)


def halves(step):
    mine = side(*step)
    return [1 - mine, mine]


def touch_kernel(*out_refs):
    pass


def touch(values, after, flops=1):
    return call(
        touch_kernel,
        [],
        after=after,
        alias=values,
        flops=flops,
        in_specs=[],
        out_specs=[pl.BlockSpec(memory_space=pl.ANY)] * len(values),
        out_shape=[shaped(x.shape, x.dtype) for x in values],
        name="touch",
    )


def back_kernel(
    at_ref, own_ref, other_ref, q_ref, k_ref, v_ref, pd_ref, pc_ref, own_context_ref,
    other_context_ref, rl_ref, first_ref, wp_ref, gain_ref, second_ref, own_output_ref,
    sent_ref, kept_ref, mine_ref, theirs_ref,
    acc, scaled, through, key_acc, value_acc, queries, weights,
):
    group = pl.program_id(0)
    count = own_ref.shape[0]
    step = count // 2
    me, core = at_ref[0], at_ref[1]
    lane = lax.broadcasted_iota(jnp.int32, (1, PAIR), 1) // HEAD_DIM

    for ref, context, at in (
        (own_ref, own_context_ref, me),
        (other_ref, other_context_ref, 1 - me),
    ):
        grad = ref[...].astype(F32) * rl_ref[at]
        scaled[at] = grad
        through[at] = grad.astype(BF).astype(F32) * context[...].astype(F32)
    key_acc[...] = jnp.zeros_like(key_acc)
    value_acc[...] = jnp.zeros_like(value_acc)

    for h in (0, 1):
        for at in (0, step):
            rows = pl.ds(at, step)
            grads = scaled[h, rows, :]
            low = grads.astype(BF)
            low_t = jnp.transpose(grads).astype(BF)
            q_t = jnp.transpose(q_ref[0, h, rows, :].astype(F32)).astype(BF)
            query = 0.0
            for a in (0, 1):
                line = pl.ds(a * HEAD_DIM, HEAD_DIM)
                mine = jnp.where(lane == a, low, 0.0).astype(BF)
                along = jnp.sum(
                    jnp.where(lane == a, through[h, rows, :], 0.0), axis=-1, keepdims=True
                )
                parts = [(pd_ref, h, h * count, at + step)]
                if h:
                    parts.append((pc_ref, 0, 0, count))
                for p_ref, p_at, key_at, keys in parts:
                    source = key_at // count
                    p = p_ref[p_at, a, rows, :keys]
                    prob_grad = dot_nt(mine, v_ref[0, source, :keys, :])
                    score = (p.astype(F32) * (prob_grad - along)).astype(BF)
                    k = jnp.where(lane == a, k_ref[0, source, :keys, :], 0.0).astype(BF)
                    query = query + dot(score, k)
                    cols = pl.ds(key_at, keys)
                    key_acc[line, cols] += dot(q_t[a * HEAD_DIM : (a + 1) * HEAD_DIM], score)
                    value_acc[line, cols] += dot(low_t[a * HEAD_DIM : (a + 1) * HEAD_DIM], p)
            queries[pl.ds(h * count + at, step), :] = query * 0.125

    query = queries[...]
    key_t = key_acc[...] * 0.125
    value_t = value_acc[...]
    both = jnp.concatenate(
        [query.astype(BF), jnp.transpose(key_t).astype(BF), jnp.transpose(value_t).astype(BF)],
        axis=1,
    )
    both_t = jnp.concatenate(
        [jnp.transpose(query).astype(BF), key_t.astype(BF), value_t.astype(BF)], axis=0
    )
    first = jnp.concatenate([first_ref[0], first_ref[1]], axis=0)
    weights[...] = dot(both_t, first)
    size = 3 * PAIR // 2
    groups = pl.num_programs(0)
    here = pl.ds(pl.multiple_of(group * size, size), size)
    for ref, half in ((sent_ref, 1 - core), (kept_ref, core)):
        ref[here, :] = weights[pl.ds(pl.multiple_of(half * size, size), size), :].astype(BF)
    weight = jnp.concatenate([wp_ref[0], wp_ref[1], wp_ref[2]], axis=1)
    added = dot_nt(both, weight)

    @pl.when(group == 0)
    def _():
        for h in (0, 1):
            acc[h] = added[h * count : (h + 1) * count]

    @pl.when(group > 0)
    def _():
        for h in (0, 1):
            acc[h] += added[h * count : (h + 1) * count]

    @pl.when(group == groups - 1)
    def _():
        mine_ref[...] = acc[me]
        theirs_ref[...] = acc[1 - me].astype(BF)
        gain = 0.0
        for h in (0, 1):
            gain = gain + jnp.sum(acc[h] * first_ref[h].astype(F32), axis=0, keepdims=True)
        gain = gain / gain_ref[...]
        part = own_output_ref.shape[0] // 2
        at = groups * size
        end = at + part
        for ref, half in ((sent_ref, 1 - core), (kept_ref, core)):
            cut = pl.ds(pl.multiple_of(half * part, part), part)
            ref[at:end, :] = own_output_ref[cut, :]
            value = jnp.where(half == 0, gain, second_ref[...])
            high = value.astype(BF).astype(F32)
            line = lax.broadcasted_iota(jnp.int32, (ref.shape[0] - end, value.shape[1]), 0)
            tail = jnp.where(line == 0, high, jnp.where(line == 1, value - high, 0.0))
            ref[end:, :] = tail.astype(BF)


def attend_back(
    at, own, other, projected, p_diag, p_cross, own_context, other_context, inverse, first, weight,
    gain, second, own_output, lines, after=(),
):
    _, _, count, cols = projected.shape
    width = first.shape[2]
    rows = whole((count, width))
    pair = pl.BlockSpec((count, PAIR), lambda g, w: (0, g))

    def block(part):
        return pl.BlockSpec((1, 2, count, PAIR), lambda g, w: (part, 0, 0, g))

    sent = shaped((lines, width), BF)
    out = [sent, sent, shaped((count, width), F32), shaped((count, width), BF)]
    return call(
        back_kernel,
        [
            own, other, projected, projected, projected, p_diag, p_cross, own_context,
            other_context, inverse, first, weight, gain, second, own_output,
        ],
        after=after,
        prefetch=[at],
        grid=(cols // PAIR,),
        in_specs=[
            pair,
            pair,
            block(0),
            block(1),
            block(2),
            pl.BlockSpec((2, 2, count, count), lambda g, w: (0, g, 0, 0)),
            pl.BlockSpec((1, 2, count, count), lambda g, w: (1, g, 0, 0)),
            pair,
            pair,
            pl.BlockSpec((2, count, PAIR), lambda g, w: (0, 0, g)),
            whole((2, count, width)),
            pl.BlockSpec((3, width, PAIR), lambda g, w: (0, 0, g)),
            whole((1, width)),
            whole((1, width)),
            whole((cols, width)),
        ],
        out_specs=[whole(o.shape) for o in out],
        scratch_shapes=[
            pltpu.VMEM((2, count, width), F32),
            pltpu.VMEM((2, count, PAIR), F32),
            pltpu.VMEM((2, count, PAIR), F32),
            pltpu.VMEM((PAIR, 2 * count), F32),
            pltpu.VMEM((PAIR, 2 * count), F32),
            pltpu.VMEM((2 * count, PAIR), F32),
            pltpu.VMEM((3 * PAIR, width), F32),
        ],
        out_shape=out,
        name="attend_back",
    )


def project_grad_kernel(low_ref, high_ref, out_ref):
    both = jnp.concatenate([low_ref[...], high_ref[...]], axis=0).astype(F32)
    flat = jnp.transpose(both)
    for c in range(3):
        out_ref[c] = flat[:, c * PAIR : (c + 1) * PAIR]


def project_grads(low, high, cols):
    width = low.shape[1]
    part = pl.BlockSpec((3 * PAIR // 2, width), lambda g: (g, 0))
    return call(
        project_grad_kernel,
        [low, high],
        grid=(cols // PAIR,),
        in_specs=[part, part],
        out_specs=pl.BlockSpec((3, width, PAIR), lambda g: (0, 0, g)),
        out_shape=shaped((3, width, cols), F32),
        name="project_grads",
    )


def on_device(
    block_input,
    output_cotangent,
    token_ids,
    positions,
    hash_table,
    first_gain,
    second_gain,
    project_weight,
    output_weight,
    expert_inner,
    expert_outer,
):
    tok_rows, model_width = block_input.shape
    local_cols = output_weight.shape[0]
    expert_count = lax.axis_size("expert")
    capacity = tok_rows // 2
    inner_weight = expert_inner[0]
    outer_weight = expert_outer[0]
    my_head = lax.axis_index("head")
    my_expert = lax.axis_index("expert")
    own_at = my_head.reshape(1).astype(jnp.int32)
    other_at = 1 - own_at
    first_gain = first_gain.reshape(1, model_width)
    second_gain = second_gain.reshape(1, model_width)

    other_input = swap(block_input, "head", 1, "rows")
    other_pos = swap(positions, "head", 1, "positions")
    seq_pos = jnp.where(
        my_head == 0, jnp.stack([positions, other_pos]), jnp.stack([other_pos, positions])
    )[:, :, None]

    chosen = jnp.take(hash_table, token_ids)
    relative = chosen ^ my_expert
    one_hot = relative[:, None] == jnp.arange(expert_count, dtype=jnp.int32)[None, :]
    rank_table = jnp.cumsum(one_hot.astype(jnp.int32), axis=0) - 1
    slot_index = relative * capacity + jnp.sum(jnp.where(one_hot, rank_table, 0), axis=1)
    slot_row, slot_col = slot_index[None, :], slot_index[:, None]
    absolute = slot_index + (chosen - relative) * capacity
    order = [my_expert ^ k for k in range(expert_count)]

    def exchange(blocks, name, first=0):
        return [
            swap(block, "expert", k, f"{name}{k}") if k else block
            for k, block in enumerate(blocks, first)
        ]

    def exchange_all(blocks):
        return lax.all_to_all(blocks, "expert", split_axis=0, concat_axis=0, tiled=True)

    sent = sent_rows(output_cotangent, absolute[None, :], expert_count)
    grad_blocks = exchange_all(sent)

    done = project(
        own_at, block_input, first_gain, project_weight, [], after=[sent, other_pos]
    )
    first_low, projected = project(other_at, other_input, first_gain, project_weight, done)
    other_weight = swap(touch([output_weight], [done[0]])[0], "head", 1, "output_weight")
    *done, other_context = attend(other_at, projected, seq_pos, [])
    got_context = swap(other_context, "head", 1, "context")
    p_diag, p_cross, inverse, own_context = attend(
        own_at,
        projected,
        seq_pos,
        done,
        after=[other_weight],
        flops=ATTEND_FLOPS,
    )
    hidden, *outgoing = hidden_rows(
        block_input,
        own_context,
        got_context,
        output_weight,
        other_weight,
        second_gain,
        slot_row,
        expert_count,
    )

    row_blocks = exchange(outgoing, "dispatch")
    done, returned, at = [], [], 0
    while at < expert_count:
        size = max(at, 1)
        parts = expert(
            at, row_blocks[at : at + size], grad_blocks, order[at : at + size], inner_weight,
            outer_weight, done,
        )
        done, grads = parts[:3], parts[3:]
        returned += exchange(grads, "return", at)
        at += size
    activated, pre_grad, produced = done

    core = lax.axis_index("core")
    turns = bits_of("x") + bits_of("head")
    outer_steps, inner_steps = turns, turns[::-1]
    outer_sent = weight_part(True, 1 - core, grad_blocks, order, activated, after=grads)
    outer_got = swap(outer_sent, "core", 1, "outer_core")
    inner_sent = weight_part(False, 1 - core, row_blocks, order, pre_grad, after=[outer_sent])
    inner_got = swap(inner_sent, "core", 1, "inner_core")
    outer_kept = weight_part(True, core, grad_blocks, order, activated, after=[inner_sent])
    inner_kept = weight_part(False, core, row_blocks, order, pre_grad, after=[outer_kept])

    hidden_grad, hidden_low, second_gain_part, own_grad, grad_sent = second_back(
        output_cotangent,
        hidden,
        second_gain,
        slot_col,
        output_weight,
        other_weight,
        returned,
        after=[inner_kept],
    )
    other_grad = swap(grad_sent, "head", 1, "context_grad")
    def pairs_of(outer, inner, i):
        return [
            (outer[1], swap(outer[0], *outer_steps[i], f"outer{i}")),
            (inner[1], swap(inner[0], *inner_steps[i], f"inner{i}")),
        ]

    outer_parts = split_sum(
        outer_kept, outer_got, 1 - side(*outer_steps[0]), True, after=[grad_sent]
    )
    inner_parts = split_sum(
        inner_kept, inner_got, 1 - side(*inner_steps[0]), False, after=[outer_parts[0]]
    )

    combined = exchange_all(produced)
    own_output, output_kept, output_sent = output_weight_parts(
        core, own_context, got_context, hidden_low, after=[grad_sent]
    )
    (output_sent,) = add(output_kept, swap(output_sent, "core", 1, "output_core"), [0 * core])
    output_sent, outer_sent, inner_sent = touch(
        [output_sent, outer_parts[0], inner_parts[0]], [other_grad]
    )
    got_output = swap(output_sent, "head", 1, "output_grad")
    outer_parts, inner_parts = [outer_sent, outer_parts[1]], [inner_sent, inner_parts[1]]

    groups = local_cols // PAIR
    end = 2 * local_cols
    grain = 16 * expert_count * lax.axis_size("x")
    lines = -(-(end + 16) // grain) * grain
    sent, kept, mine, theirs = attend_back(
        jnp.stack([my_head, core]).astype(jnp.int32), own_grad, other_grad, projected, p_diag,
        p_cross, own_context, other_context, inverse, first_low, project_weight, first_gain,
        second_gain_part, own_output, lines, after=[inner_parts[0]],
    )
    theirs = swap(theirs, "head", 1, "theirs")

    at = 3 * local_cols // 2
    for i in range(len(turns) - 1):
        outer_parts, inner_parts = adds(
            pairs_of(outer_parts, inner_parts, i),
            [halves(outer_steps[i + 1]), halves(inner_steps[i + 1])],
            after=[kept],
        )
    more = touch([got_output], [*outer_parts, combined], flops=BACK_FLOPS)
    got = swap(sent, "core", 1, "weight")
    (summed,) = add(kept, got, [0 * core], more=more, more_at=at)
    crowd = ("x", "expert")
    summed = summed.reshape(-1, lines // lax.axis_size(crowd), model_width)
    arrived = lax.all_to_all(summed, crowd, split_axis=0, concat_axis=0, tiled=True)
    block_output = output_rows(hidden, absolute[:, None], combined, after=[summed])
    input_grad = first_back(
        block_input, first_gain, hidden_grad, mine, theirs, after=[block_output]
    )
    (outer_own,), (inner_own,) = adds(
        pairs_of(outer_parts, inner_parts, -1), [[0 * core]] * 2, after=[input_grad]
    )
    outer_pieces = gather_pieces(outer_own, outer_steps, outer_steps[::-1])
    inner_pieces = gather_pieces(inner_own, inner_steps, inner_steps[::-1])
    summed = lax.all_to_all(
        total(arrived, after=[outer_own, inner_own]), crowd, split_axis=0, concat_axis=0, tiled=True
    )

    def whole_sum(pieces, is_outer, shape, which, earlier, after):
        half = 1 << (len(turns) - 1)

        def placed(place):
            if is_outer:
                return which * 2 * half + place, 0 * place
            return place % half, which * 2 + place // half

        return assemble(
            [piece for _, piece in pieces],
            [placed(at) for at, _ in pieces],
            shape,
            earlier,
            after=after,
        )

    outer_total = whole_sum(outer_pieces, True, outer_weight.shape, core, [], [])
    inner_total = whole_sum(inner_pieces, False, inner_weight.shape, core, [], outer_total)
    kept = summed.reshape(lines, model_width)
    got = swap(kept, "core", 1, "weight_back")
    outer_pieces, inner_pieces = [
        [(at, swap(piece, "core", 1, "piece_core")) for at, piece in pieces]
        for pieces in (outer_pieces, inner_pieces)
    ]
    (outer_total,) = whole_sum(
        outer_pieces, True, outer_weight.shape, 1 - core, outer_total, inner_total
    )
    (inner_total,) = whole_sum(
        inner_pieces, False, inner_weight.shape, 1 - core, inner_total, [outer_total]
    )
    low, high = jnp.where(core == 0, kept, got), jnp.where(core == 0, got, kept)

    project_grad = project_grads(low, high, local_cols)
    output_weight_grad = jnp.concatenate([low[at:end], high[at:end]]).astype(F32)
    gains = jnp.stack([x[end : end + 2].astype(F32).sum(axis=0) for x in (low, high)])
    gains = gains + swap(gains, "head", 1, "gains")
    return (
        block_output,
        input_grad,
        gains[0],
        gains[1],
        project_grad,
        output_weight_grad,
        inner_total[None],
        outer_total[None],
    )


def solution(mesh):
    devices = mesh.devices
    mesh = Mesh(
        devices.reshape(devices.shape[0] // 2, 2, *devices.shape[1:]), ("x", "core", "expert", "head")
    )
    in_specs = (
        P(("x", "core", "expert", "head"), None),
        P(("x", "core", "expert", "head"), None),
        P(("x", "core", "expert", "head")),
        P(("x", "core", "expert", "head")),
        P(),
        P(),
        P(),
        P(None, None, "head"),
        P("head", None),
        P("expert", None, None),
        P("expert", None, None),
    )
    out_specs = (
        P(("x", "core", "expert", "head"), None),
        P(("x", "core", "expert", "head"), None),
        P(),
        P(),
        P(None, None, "head"),
        P("head", None),
        P("expert", None, None),
        P("expert", None, None),
    )
    return jax.shard_map(
        on_device, mesh=mesh, in_specs=in_specs, out_specs=out_specs, check_vma=False
    )
```

```python
import functools

import jax
import jax.numpy as jnp
from jax import lax
from jax.experimental import pallas as pl
from jax.experimental.pallas import tpu as pltpu
from jax.sharding import Mesh
from jax.sharding import PartitionSpec as P

HEAD_DIM = 64
BF = jnp.bfloat16
F32 = jnp.float32


def swap(values, axis, bit, name):
    size = lax.axis_size(axis)
    with jax.named_scope(name):
        return lax.ppermute(values, axis, [(i, i ^ bit) for i in range(size)])


def bits_of(axis, low=1):
    size = lax.axis_size(axis)
    found = []
    while low < size:
        found.append((axis, low))
        low *= 2
    return found


def side(axis, bit):
    return (lax.axis_index(axis) // bit) % 2


PAIR = 2 * HEAD_DIM
ATTEND_FLOPS = 20 * 10**9
BACK_FLOPS = 300 * 10**9
FIRST_FLOPS = 300 * 10**9
HIDE = -1000000000.0
VMEM_LIMIT = 64 * 1024 * 1024


def dot(left, right):
    return jnp.dot(left, right, preferred_element_type=F32)


def dot_nt(left, right):
    return lax.dot_general(left, right, (((1,), (1,)), ((), ())), preferred_element_type=F32)


def norm_parts(values):
    center = values - jnp.mean(values, axis=-1, keepdims=True)
    scale = lax.rsqrt(jnp.mean(center * center, axis=-1, keepdims=True) + 1e-05)
    return center * scale, scale


def norm_back(grad, normed, scale):
    along = jnp.mean(grad * normed, axis=-1, keepdims=True)
    return scale * (grad - jnp.mean(grad, axis=-1, keepdims=True) - normed * along)


def shaped(shape, dtype):
    return jax.ShapeDtypeStruct(shape, dtype)


def call(kernel, operands, after=(), alias=(), prefetch=(), flops=1, **options):
    extra = [*alias, *after]
    anywhere = pl.BlockSpec(memory_space=pl.ANY)
    options["in_specs"] = [*options["in_specs"], *[anywhere] * len(extra)]
    first = len(prefetch) + len(operands)
    fixed, skip = len(operands), len(extra)

    def body(*refs):
        cut = len(prefetch) + fixed
        kernel(*refs[:cut], *refs[cut + skip :])

    if prefetch:
        specs = {name: options.pop(name) for name in ("grid", "in_specs", "out_specs")}
        specs["scratch_shapes"] = options.pop("scratch_shapes", ())
        options["grid_spec"] = pltpu.PrefetchScalarGridSpec(
            num_scalar_prefetch=len(prefetch), **specs
        )
    return pl.pallas_call(
        body,
        input_output_aliases={first + i: i for i in range(len(alias))},
        compiler_params=pltpu.CompilerParams(vmem_limit_bytes=VMEM_LIMIT),
        cost_estimate=pl.CostEstimate(flops=flops, bytes_accessed=1, transcendentals=0),
        **options,
    )(*prefetch, *operands, *extra)


def whole(shape):
    return pl.BlockSpec(shape, lambda *_: (0,) * len(shape))


def plain(kernel, operands, out_shape, name, after=(), scratch=(), flops=1):
    return call(
        kernel,
        operands,
        after=after,
        flops=flops,
        grid=(1,),
        in_specs=[whole(x.shape) for x in operands],
        out_specs=jax.tree.map(lambda s: whole(s.shape), out_shape),
        out_shape=out_shape,
        scratch_shapes=scratch,
        name=name,
    )


def project_kernel(which_ref, x_ref, gain_ref, weight_ref, first_ref, out_ref):
    @pl.when(pl.program_id(0) == 0)
    def _():
        normed, _ = norm_parts(x_ref[...].astype(F32))
        first_ref[0] = (normed * gain_ref[...]).astype(BF)

    out_ref[0, 0] = dot(first_ref[0], weight_ref[0]).astype(BF)


def project(which, rows, gain, weight, earlier, after=()):
    count, width = rows.shape
    cols = weight.shape[2]
    return call(
        project_kernel,
        [rows, gain, weight],
        after=after,
        alias=earlier,
        prefetch=[which],
        grid=(3,),
        in_specs=[
            whole((count, width)),
            whole((1, width)),
            pl.BlockSpec((1, width, cols), lambda c, w: (c, 0, 0)),
        ],
        out_specs=[
            pl.BlockSpec((1, count, width), lambda c, w: (w[0], 0, 0)),
            pl.BlockSpec((1, 1, count, cols), lambda c, w: (c, w[0], 0, 0)),
        ],
        out_shape=[shaped((2, count, width), BF), shaped((3, 2, count, cols), BF)],
        name="project",
    )


def attend_kernel(
    which_ref, q_ref, kd_ref, vd_ref, kc_ref, vc_ref, pos_ref,
    pd_ref, pc_ref, rl_ref, context_ref, bias_d, bias_c,
):
    count = q_ref.shape[2]
    step = count // 2

    @pl.when(pl.program_id(0) == 0)
    def _():
        row = lax.broadcasted_iota(jnp.int32, (count, count), 0)
        col = lax.broadcasted_iota(jnp.int32, (count, count), 1)
        start = row - pos_ref[0]
        bias_d[...] = jnp.where((col <= row) & (col >= start), 0.0, HIDE)
        bias_c[...] = jnp.where(col >= start + count, 0.0, HIDE)

    lane = lax.broadcasted_iota(jnp.int32, (1, PAIR), 1) // HEAD_DIM

    def half(late):
        for at in (0, step):
            rows = pl.ds(at, step)
            keys = at + step
            q = q_ref[0, 0, rows, :] * 0.125
            mixed, scale = 0.0, []
            for a in (0, 1):
                mine = jnp.where(lane == a, q, 0.0).astype(BF)
                s_d = dot_nt(mine, kd_ref[0, 0, :keys, :]) + bias_d[rows, :keys]
                top = jnp.max(s_d, axis=-1, keepdims=True)
                if late:
                    s_c = dot_nt(mine, kc_ref[0, 0]) + bias_c[rows, :]
                    top = jnp.maximum(top, jnp.max(s_c, axis=-1, keepdims=True))
                p_d = jnp.exp(s_d - top)
                total = jnp.sum(p_d, axis=-1, keepdims=True)
                p_d = p_d.astype(BF)
                pd_ref[0, a, rows, :keys] = p_d
                value = jnp.where(lane == a, vd_ref[0, 0, :keys, :], 0.0).astype(BF)
                mixed = mixed + dot(p_d, value)
                if late:
                    p_c = jnp.exp(s_c - top)
                    total = total + jnp.sum(p_c, axis=-1, keepdims=True)
                    p_c = p_c.astype(BF)
                    pc_ref[0, a, rows, :] = p_c
                    value = jnp.where(lane == a, vc_ref[0, 0], 0.0).astype(BF)
                    mixed = mixed + dot(p_c, value)
                scale.append(1.0 / total)
            scale = jnp.where(lane == 0, scale[0], scale[1])
            rl_ref[0, rows, :] = scale
            context_ref[rows, :] = (mixed * scale).astype(BF)

    pl.when(which_ref[0] == 0)(lambda: half(False))
    pl.when(which_ref[0] == 1)(lambda: half(True))


def attend(which, projected, positions, earlier, after=(), flops=1):
    _, _, count, cols = projected.shape
    heads = cols // HEAD_DIM

    def block(part, other):
        if other:
            return pl.BlockSpec((1, 1, count, PAIR), lambda g, w: (part, 0, 0, g))
        return pl.BlockSpec((1, 1, count, PAIR), lambda g, w: (part, w[0], 0, g))

    score_spec = pl.BlockSpec((1, 2, count, count), lambda g, w: (w[0], g, 0, 0))
    return call(
        attend_kernel,
        [*[projected] * 5, positions],
        after=after,
        alias=earlier,
        prefetch=[which],
        flops=flops,
        grid=(cols // PAIR,),
        in_specs=[
            block(0, False),
            block(1, False),
            block(2, False),
            block(1, True),
            block(2, True),
            pl.BlockSpec((1, count, 1), lambda g, w: (w[0], 0, 0)),
        ],
        out_specs=[
            score_spec,
            score_spec,
            pl.BlockSpec((1, count, PAIR), lambda g, w: (w[0], 0, g)),
            pl.BlockSpec((count, PAIR), lambda g, w: (0, g)),
        ],
        scratch_shapes=[pltpu.VMEM((count, count), F32)] * 2,
        out_shape=[
            shaped((2, heads, count, count), BF),
            shaped((2, heads, count, count), BF),
            shaped((2, count, cols), F32),
            shaped((count, cols), BF),
        ],
        name="attend",
    )


def hidden_kernel(
    x_ref, own_ref, got_ref, own_weight_ref, got_weight_ref, gain_ref, slot_ref, hidden_ref, *out_refs
):
    attended = dot(own_ref[...], own_weight_ref[...]) + dot(got_ref[...], got_weight_ref[...])
    hidden = x_ref[...].astype(F32) + attended
    hidden_ref[...] = hidden
    normed, _ = norm_parts(hidden)
    second = (normed * gain_ref[...]).astype(BF)
    send_rows(second, slot_ref, out_refs)


def send_rows(rows, slot_ref, out_refs):
    capacity = out_refs[0].shape[0]
    for k, ref in enumerate(out_refs):
        slot = lax.broadcasted_iota(jnp.int32, (capacity, rows.shape[0]), 0) + k * capacity
        place = jnp.where(slot_ref[...] == slot, 1.0, 0.0).astype(BF)
        ref[...] = dot(place, rows).astype(BF)


def hidden_rows(x, own, got, own_weight, got_weight, gain, slot_row, experts, after=()):
    count, width = x.shape
    out = [shaped((count, width), F32)] + [shaped((count // 2, width), BF)] * experts
    return plain(
        hidden_kernel,
        [x, own, got, own_weight, got_weight, gain, slot_row],
        out,
        "hidden_rows",
        after,
    )


def send_kernel(rows_ref, slot_ref, out_ref):
    send_rows(rows_ref[...], slot_ref, [out_ref.at[k] for k in range(out_ref.shape[0])])


def sent_rows(rows, slot_row, experts):
    count, width = rows.shape
    out = shaped((experts, count // 2, width), BF)
    return plain(send_kernel, [rows, slot_row], out, "sent_rows")


def taken_rows(slot_ref, block_refs):
    count, capacity = slot_ref.shape[0], block_refs[0].shape[0]
    total = 0.0
    for k, ref in enumerate(block_refs):
        slot = lax.broadcasted_iota(jnp.int32, (count, capacity), 1) + k * capacity
        place = jnp.where(slot_ref[...] == slot, 1.0, 0.0).astype(BF)
        total = total + dot(place, ref[...])
    return total


def output_kernel(hidden_ref, slot_ref, *refs):
    blocks = [refs[0].at[k] for k in range(refs[0].shape[0])]
    refs[-1][...] = (hidden_ref[...] + taken_rows(slot_ref, blocks)).astype(BF)


def output_rows(hidden, slot_col, blocks, after=()):
    return plain(
        output_kernel,
        [hidden, slot_col, blocks],
        shaped(hidden.shape, BF),
        "output_rows",
        after,
    )


def second_kernel(cot_ref, hidden_ref, gain_ref, slot_ref, own_weight_ref, got_weight_ref, *refs):
    grad_ref, low_ref, gain_grad_ref, own_ref, send_ref = refs[-5:]
    second_grad = taken_rows(slot_ref, refs[:-5])
    normed, scale = norm_parts(hidden_ref[...])
    gain_grad_ref[...] = jnp.sum(second_grad * normed, axis=0, keepdims=True)
    grad = cot_ref[...].astype(F32) + norm_back(second_grad * gain_ref[...], normed, scale)
    grad_ref[...] = grad
    low = grad.astype(BF)
    low_ref[...] = low
    send_ref[...] = dot_nt(low, got_weight_ref[...]).astype(BF)
    own_ref[...] = dot_nt(low, own_weight_ref[...]).astype(BF)


def second_back(cot, hidden, gain, slot_col, own_weight, got_weight, blocks, after=()):
    count, width = hidden.shape
    part = shaped((count, own_weight.shape[0]), BF)
    out = [
        shaped((count, width), F32),
        shaped((count, width), BF),
        shaped((1, width), F32),
        part,
        part,
    ]
    return plain(
        second_kernel,
        [cot, hidden, gain, slot_col, own_weight, got_weight, *blocks],
        out,
        "second_back",
        after,
        flops=BACK_FLOPS,
    )


def output_weight_kernel(
    core_ref, own_ref, got_ref, low_ref, own_out, kept_out, sent_out, scratch
):
    def part(ref):
        return lax.dot_general(
            ref[...], low_ref[...], (((0,), (0,)), ((), ())), preferred_element_type=F32
        ).astype(BF)

    scratch[...] = part(got_ref)
    rows = kept_out.shape[0]
    for ref, half in ((kept_out, core_ref[0]), (sent_out, 1 - core_ref[0])):
        ref[...] = scratch[pl.ds(pl.multiple_of(half * rows, rows), rows), :]
    own_out[...] = part(own_ref)


def output_weight_parts(core, own, got, low, after=()):
    cols, width = own.shape[1], low.shape[1]
    part = shaped((cols // 2, width), BF)
    out = [shaped((cols, width), BF), part, part]
    return call(
        output_weight_kernel,
        [own, got, low],
        after=after,
        prefetch=[core.reshape(1).astype(jnp.int32)],
        grid=(1,),
        in_specs=[whole(x.shape) for x in (own, got, low)],
        out_specs=[whole(o.shape) for o in out],
        out_shape=out,
        scratch_shapes=[pltpu.VMEM((cols, width), BF)],
        name="output_weight_parts",
    )


def first_kernel(x_ref, gain_ref, hidden_grad_ref, own_ref, theirs_ref, out_ref):
    grad = (own_ref[...] + theirs_ref[...].astype(F32)) * gain_ref[...]
    normed, scale = norm_parts(x_ref[...].astype(F32))
    out_ref[...] = hidden_grad_ref[...] + norm_back(grad, normed, scale)


def first_back(x, gain, hidden_grad, own, theirs, after=()):
    return plain(
        first_kernel,
        [x, gain, hidden_grad, own, theirs],
        shaped(x.shape, F32),
        "first_back",
        after,
        flops=FIRST_FLOPS,
    )


def fill(target, refs):
    rows = refs[0].shape[0]
    for i, ref in enumerate(refs):
        target[i * rows : (i + 1) * rows] = ref[...]


def expert_kernel(count, sub, place_ref, *refs):
    x_refs, cot_refs, refs = refs[:count], refs[count : 2 * count], refs[2 * count :]
    inner_ref, outer_ref, act_ref, pre_ref, out_ref, *grad_refs, x, cot, grad_acc, out_acc = refs
    at = pl.program_id(0)
    last = pl.num_programs(0) - count
    size = out_ref.shape[1]

    @pl.when(at > last)
    def _():
        rows = pl.ds(pl.multiple_of((at - last) * size, size), size)
        out_ref[0] = out_acc[rows, :].astype(BF)

    pl.when(at <= last)(
        lambda: expert_step(
            count, sub, x_refs, cot_refs, inner_ref, outer_ref, act_ref, pre_ref, out_ref,
            grad_refs, x, cot, grad_acc, out_acc, at, last,
        )
    )


def expert_step(
    count, sub, x_refs, cot_refs, inner_ref, outer_ref, act_ref, pre_ref, out_ref, grad_refs,
    x, cot, grad_acc, out_acc, at, last,
):

    @pl.when(at == 0)
    def _():
        fill(x, x_refs)
        fill(cot, [ref.at[0] for ref in cot_refs])
        grad_acc[...] = jnp.zeros_like(grad_acc)
        out_acc[...] = jnp.zeros_like(out_acc)

    def front(i):
        cols = slice(i * sub, (i + 1) * sub)
        return dot(x[...], inner_ref[:, cols]), dot_nt(cot[...], outer_ref[cols, :])

    parts = inner_ref.shape[1] // sub
    now = front(0)
    for i in range(parts):
        later = front(i + 1) if i + 1 < parts else None
        value, grad = now
        square = value * value
        half = 0.5 + 0.5 * jnp.tanh(
            value * (0.7978845608028654 + 0.035677408136300125 * square)
        )
        act = value * half
        slope = half + act * (1.0 - half) * (1.5957691216057308 + 0.21406444881780074 * square)
        cols = slice(i * sub, (i + 1) * sub)
        act_ref[:, cols] = act.astype(BF)
        pre_ref[:, cols] = (grad * slope).astype(BF)
        now = later
    grad_acc[...] += dot_nt(pre_ref[...], inner_ref[...])
    out_acc[...] += dot(act_ref[...], outer_ref[...])

    @pl.when(at == last)
    def _():
        size = out_ref.shape[1]
        out_ref[0] = out_acc[:size].astype(BF)
        for i, ref in enumerate(grad_refs):
            ref[...] = grad_acc[i * size : (i + 1) * size].astype(BF)


def expert(index, blocks, cot, places, inner, outer, earlier, after=(), tile=768, sub=256):
    count, width = blocks[0].shape
    size, units = len(blocks), inner.shape[1]
    total = count * cot.shape[0]
    tiles = units // tile

    def held(j):
        return jnp.minimum(j, tiles - 1)

    wide = pl.BlockSpec((count * size, tile), lambda j, p: (index // size, held(j)))
    out = pl.BlockSpec(
        (1, count, width), lambda j, p: (p[jnp.maximum(j - tiles + 1, 0)], 0, 0)
    )

    def placed(i):
        return pl.BlockSpec((1, count, width), lambda j, p: (p[i], 0, 0))

    return call(
        functools.partial(expert_kernel, size, sub),
        [*blocks, *[cot] * size, inner, outer],
        after=after,
        alias=earlier,
        prefetch=[jnp.stack(places).astype(jnp.int32)],
        grid=(tiles + size - 1,),
        in_specs=[whole((count, width))] * size
        + [placed(i) for i in range(size)]
        + [
            pl.BlockSpec((width, tile), lambda j, p: (0, held(j))),
            pl.BlockSpec((tile, width), lambda j, p: (held(j), 0)),
        ],
        out_specs=[wide, wide, out] + [whole((count, width))] * size,
        out_shape=[shaped((total, units), BF)] * 2
        + [shaped(cot.shape, BF)]
        + [shaped((count, width), BF)] * size,
        scratch_shapes=[pltpu.VMEM((count * size, width), BF)] * 2
        + [pltpu.VMEM((count * size, width), F32)] * 2,
        name="expert",
    )


def weight_kernel(count, which_ref, place_ref, act_ref, pre_ref, *refs):
    x_refs, (cot_ref, outer_out, inner_out, x, cot) = refs[:count], refs[count:]
    at = pl.program_id(0)
    half = pl.num_programs(0) // 2

    @pl.when(at == 0)
    def _():
        fill(cot, [cot_ref.at[place_ref[i]] for i in range(count)])
        fill(x, x_refs)

    def put(ref, left, right):
        ref[...] = lax.dot_general(
            left, right, (((0,), (0,)), ((), ())), preferred_element_type=F32
        ).astype(BF)

    pl.when(at < half)(lambda: put(outer_out, act_ref[...], cot[...]))
    pl.when(at >= half)(lambda: put(inner_out, x[...], pre_ref[...]))


def weight_parts(half, x_blocks, cot_blocks, places, act, pre, after=(), tiles=4):
    count, width = x_blocks[0].shape
    total, units = act.shape
    tile = units // 2 // tiles

    def early(j):
        return jnp.minimum(j, tiles - 1)

    def late(j):
        return jnp.maximum(j - tiles, 0)

    return call(
        functools.partial(weight_kernel, len(x_blocks)),
        [act, pre, *x_blocks, cot_blocks],
        after=after,
        prefetch=[half.reshape(1).astype(jnp.int32), jnp.stack(places).astype(jnp.int32)],
        grid=(2 * tiles,),
        in_specs=[
            pl.BlockSpec((total, tile), lambda j, w, p: (0, w[0] * tiles + early(j))),
            pl.BlockSpec((total, tile), lambda j, w, p: (0, w[0] * tiles + late(j))),
        ]
        + [whole((count, width))] * len(x_blocks)
        + [whole(cot_blocks.shape)],
        out_specs=[
            pl.BlockSpec((tile, width), lambda j, w, p: (early(j), 0)),
            pl.BlockSpec((width, tile), lambda j, w, p: (0, late(j))),
        ],
        out_shape=[shaped((units // 2, width), BF), shaped((width, units // 2), BF)],
        scratch_shapes=[pltpu.VMEM((total, width), BF)] * 2,
        name="weight_parts",
    )


def split_kernel(place_ref, outer_kept, outer_got, inner_kept, inner_got, *out_refs):
    at = pl.program_id(0)
    quarter = pl.num_programs(0) // 4
    for i, out_ref in enumerate(out_refs):
        kept_ref, got_ref = ((outer_kept, outer_got), (inner_kept, inner_got))[i // 2]

        @pl.when(at // quarter == i)
        def _(kept_ref=kept_ref, got_ref=got_ref, out_ref=out_ref):
            out_ref[...] = (kept_ref[...].astype(F32) + got_ref[...].astype(F32)).astype(BF)


def split_sums(outer, inner, outer_turn, inner_turn, after=(), tiles=4):
    rows, cols = outer[0].shape
    outer_tile, inner_tile = (rows // tiles, cols), (cols, rows // tiles)

    def held(j, i):
        return jnp.clip(j - i * (tiles // 2), 0, tiles // 2 - 1)

    def source(i):
        def at(j, w):
            step = jnp.clip(j - i * tiles, 0, tiles - 1)
            return (w[i] * (tiles // 2) + step) % tiles

        return at

    outer_at, inner_at = source(0), source(1)
    outer_in = pl.BlockSpec(outer_tile, lambda j, w: (outer_at(j, w), 0))
    inner_in = pl.BlockSpec(inner_tile, lambda j, w: (0, inner_at(j, w)))
    parts = call(
        split_kernel,
        [*outer, *inner],
        after=after,
        prefetch=[jnp.stack([outer_turn, inner_turn]).astype(jnp.int32)],
        grid=(2 * tiles,),
        in_specs=[outer_in, outer_in, inner_in, inner_in],
        out_specs=[
            pl.BlockSpec(outer_tile, lambda j, w: (held(j, 0), 0)),
            pl.BlockSpec(outer_tile, lambda j, w: (held(j, 1), 0)),
            pl.BlockSpec(inner_tile, lambda j, w: (0, held(j, 2))),
            pl.BlockSpec(inner_tile, lambda j, w: (0, held(j, 3))),
        ],
        out_shape=[shaped((rows // 2, cols), BF)] * 2 + [shaped((cols, rows // 2), BF)] * 2,
        name="split_sums",
    )
    return parts[:2], parts[2:]


def assemble_kernel(place_ref, *refs):
    *piece_refs, out_ref = refs
    for i, ref in enumerate(piece_refs):

        @pl.when(pl.program_id(0) == i)
        def _(ref=ref):
            out_ref[...] = ref[...].astype(F32)


def assemble(pieces, places, shape, earlier, after=(), flops=1):
    size = pieces[0].shape
    table = jnp.stack([jnp.stack(place) for place in places]).astype(jnp.int32)
    return call(
        assemble_kernel,
        pieces,
        flops=flops,
        after=after,
        alias=earlier,
        prefetch=[table],
        grid=(len(pieces),),
        in_specs=[whole(size)] * len(pieces),
        out_specs=[pl.BlockSpec(size, lambda i, t: (t[i, 0], t[i, 1]))],
        out_shape=[shaped(shape, F32)],
        name="assemble",
    )


def add_kernel(more_at, place_ref, kept_ref, got_ref, *refs):
    out_refs, more_refs = (refs, ()) if more_at is None else (refs[1:-1], refs[:1])
    rows = out_refs[0].shape[0]
    if more_refs:
        kept_ref, scratch = refs[-1], kept_ref
        kept_ref[...] = scratch[...].astype(F32)
        span = pl.ds(more_at, more_refs[0].shape[0])
        for ref in more_refs:
            kept_ref[span, :] += ref[...].astype(F32)
    for i, ref in enumerate(out_refs):
        cut = pl.ds(pl.multiple_of(place_ref[i] * rows, rows), rows)
        ref[...] = (kept_ref[cut, :].astype(F32) + got_ref[cut, :].astype(F32)).astype(BF)


def add(kept, got, places, after=(), more=(), more_at=None):
    shape = kept.shape
    out = [shaped((shape[0] // len(places), *shape[1:]), BF)] * len(places)
    return call(
        functools.partial(add_kernel, more_at),
        [kept, got, *more],
        after=after,
        prefetch=[jnp.stack(places).astype(jnp.int32)],
        grid=(1,),
        in_specs=[whole(shape)] * 2 + [whole(x.shape) for x in more],
        out_specs=[whole(o.shape) for o in out],
        scratch_shapes=[pltpu.VMEM(shape, F32)] if more else [],
        out_shape=out,
        name="add",
    )


def adds_kernel(count, cuts, place_ref, *refs):
    in_refs, out_refs = refs[: 2 * count], refs[2 * count :]
    for i in range(count):
        kept_ref, got_ref = in_refs[2 * i : 2 * i + 2]
        for j in range(cuts):
            ref = out_refs[cuts * i + j]
            rows = ref.shape[0]
            cut = pl.ds(pl.multiple_of(place_ref[cuts * i + j] * rows, rows), rows)
            ref[...] = (kept_ref[cut, :].astype(F32) + got_ref[cut, :].astype(F32)).astype(BF)


def adds(pairs, places, after=()):
    cuts = len(places[0])
    out = [
        shaped((kept.shape[0] // cuts, kept.shape[1]), BF) for kept, _ in pairs for _ in range(cuts)
    ]
    operands = [x for pair in pairs for x in pair]
    parts = call(
        functools.partial(adds_kernel, len(pairs), cuts),
        operands,
        after=after,
        prefetch=[jnp.stack([p for at in places for p in at]).astype(jnp.int32)],
        grid=(1,),
        in_specs=[whole(x.shape) for x in operands],
        out_specs=[whole(o.shape) for o in out],
        out_shape=out,
        name="adds",
    )
    return [parts[cuts * i : cuts * (i + 1)] for i in range(len(pairs))]


def gather_pieces(own, steps, order):
    weights = {step: 1 << (len(steps) - 1 - i) for i, step in enumerate(steps)}
    place = sum(side(*step) * weight for step, weight in weights.items())
    pieces = [(0, place, own)]
    for step in order:
        change = weights[step] * (1 - 2 * side(*step))
        pieces += [
            (hops + 1, at + change, swap(piece, *step, "piece")) for hops, at, piece in pieces
        ]
    pieces.sort(key=lambda piece: piece[0])
    return [piece[1:] for piece in pieces]


def total_kernel(in_ref, out_ref):
    count = in_ref.shape[0]
    value = sum(in_ref[i].astype(F32) for i in range(count)).astype(BF)
    for i in range(count):
        out_ref[i] = value


def total(blocks, after=()):
    return plain(total_kernel, [blocks], shaped(blocks.shape, BF), "total", after)


def halves(step):
    mine = side(*step)
    return [1 - mine, mine]


def touch_kernel(*out_refs):
    pass


def touch(values, after, flops=1):
    return call(
        touch_kernel,
        [],
        after=after,
        alias=values,
        flops=flops,
        in_specs=[],
        out_specs=[pl.BlockSpec(memory_space=pl.ANY)] * len(values),
        out_shape=[shaped(x.shape, x.dtype) for x in values],
        name="touch",
    )


def back_kernel(
    at_ref, own_ref, other_ref, q_ref, k_ref, v_ref, pd_ref, pc_ref, own_context_ref,
    other_context_ref, rl_ref, first_ref, wp_ref, gain_ref, second_ref, own_output_ref,
    sent_ref, kept_ref, mine_ref, theirs_ref,
    acc, scaled, through, key_acc, value_acc, queries, weights,
):
    group = pl.program_id(0)
    count = own_ref.shape[0]
    step = count // 2
    me, core = at_ref[0], at_ref[1]
    lane = lax.broadcasted_iota(jnp.int32, (1, PAIR), 1) // HEAD_DIM

    for ref, context, at in (
        (own_ref, own_context_ref, me),
        (other_ref, other_context_ref, 1 - me),
    ):
        grad = ref[...].astype(F32) * rl_ref[at]
        scaled[at] = grad
        through[at] = grad.astype(BF).astype(F32) * context[...].astype(F32)
    key_acc[...] = jnp.zeros_like(key_acc)
    value_acc[...] = jnp.zeros_like(value_acc)

    for h in (0, 1):
        for at in (0, step):
            rows = pl.ds(at, step)
            grads = scaled[h, rows, :]
            low = grads.astype(BF)
            low_t = jnp.transpose(grads).astype(BF)
            q_t = jnp.transpose(q_ref[0, h, rows, :].astype(F32)).astype(BF)
            query = 0.0
            for a in (0, 1):
                line = pl.ds(a * HEAD_DIM, HEAD_DIM)
                mine = jnp.where(lane == a, low, 0.0).astype(BF)
                along = jnp.sum(
                    jnp.where(lane == a, through[h, rows, :], 0.0), axis=-1, keepdims=True
                )
                parts = [(pd_ref, h, h * count, at + step)]
                if h:
                    parts.append((pc_ref, 0, 0, count))
                for p_ref, p_at, key_at, keys in parts:
                    source = key_at // count
                    p = p_ref[p_at, a, rows, :keys]
                    prob_grad = dot_nt(mine, v_ref[0, source, :keys, :])
                    score = (p.astype(F32) * (prob_grad - along)).astype(BF)
                    k = jnp.where(lane == a, k_ref[0, source, :keys, :], 0.0).astype(BF)
                    query = query + dot(score, k)
                    cols = pl.ds(key_at, keys)
                    key_acc[line, cols] += dot(q_t[a * HEAD_DIM : (a + 1) * HEAD_DIM], score)
                    value_acc[line, cols] += dot(low_t[a * HEAD_DIM : (a + 1) * HEAD_DIM], p)
            queries[pl.ds(h * count + at, step), :] = query * 0.125

    query = queries[...]
    key_t = key_acc[...] * 0.125
    value_t = value_acc[...]
    both = jnp.concatenate(
        [query.astype(BF), jnp.transpose(key_t).astype(BF), jnp.transpose(value_t).astype(BF)],
        axis=1,
    )
    both_t = jnp.concatenate(
        [jnp.transpose(query).astype(BF), key_t.astype(BF), value_t.astype(BF)], axis=0
    )
    first = jnp.concatenate([first_ref[0], first_ref[1]], axis=0)
    weights[...] = dot(both_t, first)
    size = 3 * PAIR // 2
    groups = pl.num_programs(0)
    here = pl.ds(pl.multiple_of(group * size, size), size)
    for ref, half in ((sent_ref, 1 - core), (kept_ref, core)):
        ref[here, :] = weights[pl.ds(pl.multiple_of(half * size, size), size), :].astype(BF)
    weight = jnp.concatenate([wp_ref[0], wp_ref[1], wp_ref[2]], axis=1)
    added = dot_nt(both, weight)

    @pl.when(group == 0)
    def _():
        for h in (0, 1):
            acc[h] = added[h * count : (h + 1) * count]

    @pl.when(group > 0)
    def _():
        for h in (0, 1):
            acc[h] += added[h * count : (h + 1) * count]

    @pl.when(group == groups - 1)
    def _():
        mine_ref[...] = acc[me]
        theirs_ref[...] = acc[1 - me].astype(BF)
        gain = 0.0
        for h in (0, 1):
            gain = gain + jnp.sum(acc[h] * first_ref[h].astype(F32), axis=0, keepdims=True)
        gain = gain / gain_ref[...]
        part = own_output_ref.shape[0] // 2
        at = groups * size
        end = at + part
        for ref, half in ((sent_ref, 1 - core), (kept_ref, core)):
            cut = pl.ds(pl.multiple_of(half * part, part), part)
            ref[at:end, :] = own_output_ref[cut, :]
            value = jnp.where(half == 0, gain, second_ref[...])
            high = value.astype(BF).astype(F32)
            line = lax.broadcasted_iota(jnp.int32, (ref.shape[0] - end, value.shape[1]), 0)
            tail = jnp.where(line == 0, high, jnp.where(line == 1, value - high, 0.0))
            ref[end:, :] = tail.astype(BF)


def attend_back(
    at, own, other, projected, p_diag, p_cross, own_context, other_context, inverse, first, weight,
    gain, second, own_output, lines, after=(),
):
    _, _, count, cols = projected.shape
    width = first.shape[2]
    rows = whole((count, width))
    pair = pl.BlockSpec((count, PAIR), lambda g, w: (0, g))

    def block(part):
        return pl.BlockSpec((1, 2, count, PAIR), lambda g, w: (part, 0, 0, g))

    sent = shaped((lines, width), BF)
    out = [sent, sent, shaped((count, width), F32), shaped((count, width), BF)]
    return call(
        back_kernel,
        [
            own, other, projected, projected, projected, p_diag, p_cross, own_context,
            other_context, inverse, first, weight, gain, second, own_output,
        ],
        after=after,
        prefetch=[at],
        grid=(cols // PAIR,),
        in_specs=[
            pair,
            pair,
            block(0),
            block(1),
            block(2),
            pl.BlockSpec((2, 2, count, count), lambda g, w: (0, g, 0, 0)),
            pl.BlockSpec((1, 2, count, count), lambda g, w: (1, g, 0, 0)),
            pair,
            pair,
            pl.BlockSpec((2, count, PAIR), lambda g, w: (0, 0, g)),
            whole((2, count, width)),
            pl.BlockSpec((3, width, PAIR), lambda g, w: (0, 0, g)),
            whole((1, width)),
            whole((1, width)),
            whole((cols, width)),
        ],
        out_specs=[whole(o.shape) for o in out],
        scratch_shapes=[
            pltpu.VMEM((2, count, width), F32),
            pltpu.VMEM((2, count, PAIR), F32),
            pltpu.VMEM((2, count, PAIR), F32),
            pltpu.VMEM((PAIR, 2 * count), F32),
            pltpu.VMEM((PAIR, 2 * count), F32),
            pltpu.VMEM((2 * count, PAIR), F32),
            pltpu.VMEM((3 * PAIR, width), F32),
        ],
        out_shape=out,
        name="attend_back",
    )


def weight_outputs_kernel(core_ref, kept_ref, got_ref, project_ref, output_ref, gains_ref):
    group, groups = pl.program_id(0), pl.num_programs(0)
    size = 3 * PAIR // 2

    def halves_of(start, rows):
        cut = pl.ds(start, rows)
        kept, got = kept_ref[cut, :].astype(F32), got_ref[cut, :].astype(F32)
        low = jnp.where(core_ref[0] == 0, kept, got)
        return low, jnp.where(core_ref[0] == 0, got, kept)

    low, high = halves_of(pl.multiple_of(group * size, size), size)
    flat = jnp.transpose(jnp.concatenate([low, high], axis=0))
    for c in range(3):
        project_ref[c] = flat[:, c * PAIR : (c + 1) * PAIR]

    @pl.when(group == groups - 1)
    def _():
        part = output_ref.shape[0] // 2
        output_ref[:part], output_ref[part:] = halves_of(groups * size, part)
        for i, rows in enumerate(halves_of(groups * size + part, 16)):
            gains_ref[i : i + 1] = rows[0:1] + rows[1:2]


def weight_outputs(core, kept, got, cols, after=()):
    lines, width = kept.shape
    return call(
        weight_outputs_kernel,
        [kept, got],
        after=after,
        prefetch=[core.reshape(1).astype(jnp.int32)],
        grid=(cols // PAIR,),
        in_specs=[whole((lines, width))] * 2,
        out_specs=[
            pl.BlockSpec((3, width, PAIR), lambda g, w: (0, 0, g)),
            whole((cols, width)),
            whole((2, width)),
        ],
        out_shape=[shaped((3, width, cols), F32), shaped((cols, width), F32), shaped((2, width), F32)],
        name="weight_outputs",
    )


def on_device(
    block_input,
    output_cotangent,
    token_ids,
    positions,
    hash_table,
    first_gain,
    second_gain,
    project_weight,
    output_weight,
    expert_inner,
    expert_outer,
):
    tok_rows, model_width = block_input.shape
    local_cols = output_weight.shape[0]
    expert_count = lax.axis_size("expert")
    capacity = tok_rows // 2
    inner_weight = expert_inner[0]
    outer_weight = expert_outer[0]
    my_head = lax.axis_index("head")
    my_expert = lax.axis_index("expert")
    own_at = my_head.reshape(1).astype(jnp.int32)
    other_at = 1 - own_at
    first_gain = first_gain.reshape(1, model_width)
    second_gain = second_gain.reshape(1, model_width)

    other_input = swap(block_input, "head", 1, "rows")
    other_pos = swap(positions, "head", 1, "positions")
    seq_pos = jnp.where(
        my_head == 0, jnp.stack([positions, other_pos]), jnp.stack([other_pos, positions])
    )[:, :, None]

    chosen = jnp.take(hash_table, token_ids)
    relative = chosen ^ my_expert
    one_hot = relative[:, None] == jnp.arange(expert_count, dtype=jnp.int32)[None, :]
    rank_table = jnp.cumsum(one_hot.astype(jnp.int32), axis=0) - 1
    slot_index = relative * capacity + jnp.sum(jnp.where(one_hot, rank_table, 0), axis=1)
    slot_row, slot_col = slot_index[None, :], slot_index[:, None]
    absolute = slot_index + (chosen - relative) * capacity
    order = [my_expert ^ k for k in range(expert_count)]

    def exchange(blocks, name, first=0):
        return [
            swap(block, "expert", k, f"{name}{k}") if k else block
            for k, block in enumerate(blocks, first)
        ]

    def exchange_all(blocks):
        return lax.all_to_all(blocks, "expert", split_axis=0, concat_axis=0, tiled=True)

    sent = sent_rows(output_cotangent, absolute[None, :], expert_count)
    grad_blocks = exchange_all(sent)

    done = project(
        own_at, block_input, first_gain, project_weight, [], after=[sent, other_pos]
    )
    first_low, projected = project(other_at, other_input, first_gain, project_weight, done)
    other_weight = swap(touch([output_weight], [done[0]])[0], "head", 1, "output_weight")
    *done, other_context = attend(other_at, projected, seq_pos, [])
    got_context = swap(other_context, "head", 1, "context")
    p_diag, p_cross, inverse, own_context = attend(
        own_at,
        projected,
        seq_pos,
        done,
        after=[other_weight],
        flops=ATTEND_FLOPS,
    )
    hidden, *outgoing = hidden_rows(
        block_input,
        own_context,
        got_context,
        output_weight,
        other_weight,
        second_gain,
        slot_row,
        expert_count,
    )

    row_blocks = exchange(outgoing, "dispatch")
    done, returned, at = [], [], 0
    while at < expert_count:
        size = max(at, 1)
        parts = expert(
            at, row_blocks[at : at + size], grad_blocks, order[at : at + size], inner_weight,
            outer_weight, done,
        )
        done, grads = parts[:3], parts[3:]
        returned += exchange(grads, "return", at)
        at += size
    activated, pre_grad, produced = done

    core = lax.axis_index("core")
    turns = bits_of("x") + bits_of("head")
    outer_steps, inner_steps = turns, turns[::-1]
    outer_sent, inner_sent = weight_parts(
        1 - core, row_blocks, grad_blocks, order, activated, pre_grad, after=grads
    )
    outer_got = swap(outer_sent, "core", 1, "outer_core")
    inner_got = swap(inner_sent, "core", 1, "inner_core")
    outer_kept, inner_kept = weight_parts(
        core, row_blocks, grad_blocks, order, activated, pre_grad, after=[inner_sent]
    )

    hidden_grad, hidden_low, second_gain_part, own_grad, grad_sent = second_back(
        output_cotangent,
        hidden,
        second_gain,
        slot_col,
        output_weight,
        other_weight,
        returned,
        after=[inner_kept],
    )
    other_grad = swap(grad_sent, "head", 1, "context_grad")
    def pairs_of(outer, inner, i):
        return [
            (outer[1], swap(outer[0], *outer_steps[i], f"outer{i}")),
            (inner[1], swap(inner[0], *inner_steps[i], f"inner{i}")),
        ]

    outer_parts, inner_parts = split_sums(
        (outer_kept, outer_got),
        (inner_kept, inner_got),
        1 - side(*outer_steps[0]),
        1 - side(*inner_steps[0]),
        after=[grad_sent],
    )

    combined = exchange_all(touch([produced], [grad_sent])[0])
    own_output, output_kept, output_sent = output_weight_parts(
        core, own_context, got_context, hidden_low, after=[grad_sent]
    )
    (output_sent,) = add(output_kept, swap(output_sent, "core", 1, "output_core"), [0 * core])
    output_sent, outer_sent, inner_sent = touch(
        [output_sent, outer_parts[0], inner_parts[0]], [other_grad]
    )
    got_output = swap(output_sent, "head", 1, "output_grad")
    outer_parts, inner_parts = [outer_sent, outer_parts[1]], [inner_sent, inner_parts[1]]

    groups = local_cols // PAIR
    end = 2 * local_cols
    grain = 16 * expert_count * lax.axis_size("x")
    lines = -(-(end + 16) // grain) * grain
    sent, kept, mine, theirs = attend_back(
        jnp.stack([my_head, core]).astype(jnp.int32), own_grad, other_grad, projected, p_diag,
        p_cross, own_context, other_context, inverse, first_low, project_weight, first_gain,
        second_gain_part, own_output, lines, after=[inner_parts[0]],
    )
    at = 3 * local_cols // 2
    for i in range(len(turns) - 1):
        outer_parts, inner_parts = adds(
            pairs_of(outer_parts, inner_parts, i),
            [halves(outer_steps[i + 1]), halves(inner_steps[i + 1])],
            after=[kept],
        )
    more = touch([got_output], [*outer_parts, combined], flops=BACK_FLOPS)
    got = swap(sent, "core", 1, "weight")
    (summed,) = add(kept, got, [0 * core], more=more, more_at=at)
    crowd = ("x", "expert")
    summed = summed.reshape(-1, lines // lax.axis_size(crowd), model_width)
    arrived = lax.all_to_all(summed, crowd, split_axis=0, concat_axis=0, tiled=True)
    theirs = swap(theirs, "head", 1, "theirs")
    block_output = output_rows(hidden, absolute[:, None], combined, after=[summed])
    input_grad = first_back(
        block_input, first_gain, hidden_grad, mine, theirs, after=[block_output]
    )
    (outer_own,), (inner_own,) = adds(
        pairs_of(outer_parts, inner_parts, -1), [[0 * core]] * 2, after=[input_grad]
    )
    outer_pieces = gather_pieces(outer_own, outer_steps, outer_steps[::-1])
    inner_pieces = gather_pieces(inner_own, inner_steps, inner_steps[::-1])
    arrived = total(arrived, after=[outer_own, inner_own])
    summed = lax.all_to_all(arrived, crowd, split_axis=0, concat_axis=0, tiled=True)

    def whole_sum(own_core, other_core, is_outer, earlier, after):
        half = 1 << (len(turns) - 1)

        def placed(place, which):
            if is_outer:
                return which * 2 * half + place, 0 * place
            return place % half, which * 2 + place // half

        chosen = [
            (piece, placed(at, which))
            for pieces, which in ((own_core, core), (other_core, 1 - core))
            for at, piece in pieces
        ]
        return assemble(
            [piece for piece, _ in chosen],
            [place for _, place in chosen],
            (outer_weight if is_outer else inner_weight).shape,
            earlier,
            after=after,
            flops=1,
        )[0]

    early = len(turns) + 1

    def core_swaps(pieces):
        return [(at, swap(piece, "core", 1, "piece_core")) for at, piece in pieces]

    others = []
    for pieces in (outer_pieces, inner_pieces):
        (held,) = touch([pieces[0][1]], [arrived])
        others.append(core_swaps([(pieces[0][0], held), *pieces[1:early]]))
    totals = []
    for is_outer, own_core, other_core in zip(
        (True, False), (outer_pieces, inner_pieces), others
    ):
        totals.append(
            whole_sum(own_core[:early], other_core, is_outer, [], [arrived] + totals[-1:])
        )
    late = []
    for pieces in (outer_pieces, inner_pieces):
        held = touch([piece for _, piece in pieces[early:]], totals)
        late.append([(at, piece) for (at, _), piece in zip(pieces[early:], held)])
    late_others = [core_swaps(pieces) for pieces in late]
    kept = touch([summed], [pieces[0][1] for pieces in late])[0].reshape(lines, model_width)
    got = swap(kept, "core", 1, "weight_back")
    project_grad, output_weight_grad, gains = weight_outputs(
        core, kept, got, local_cols
    )
    gains = gains + swap(gains, "head", 1, "gains")
    outer_total = whole_sum(late[0], late_others[0], True, totals[:1], [project_grad])
    inner_total = whole_sum(late[1], late_others[1], False, totals[1:], [outer_total])
    return (
        block_output,
        input_grad,
        gains[0],
        gains[1],
        project_grad,
        output_weight_grad,
        inner_total[None],
        outer_total[None],
    )


def solution(mesh):
    devices = mesh.devices
    mesh = Mesh(
        devices.reshape(devices.shape[0] // 2, 2, *devices.shape[1:]), ("x", "core", "expert", "head")
    )
    in_specs = (
        P(("x", "core", "expert", "head"), None),
        P(("x", "core", "expert", "head"), None),
        P(("x", "core", "expert", "head")),
        P(("x", "core", "expert", "head")),
        P(),
        P(),
        P(),
        P(None, None, "head"),
        P("head", None),
        P("expert", None, None),
        P("expert", None, None),
    )
    out_specs = (
        P(("x", "core", "expert", "head"), None),
        P(("x", "core", "expert", "head"), None),
        P(),
        P(),
        P(None, None, "head"),
        P("head", None),
        P("expert", None, None),
        P("expert", None, None),
    )
    return jax.shard_map(
        on_device, mesh=mesh, in_specs=in_specs, out_specs=out_specs, check_vma=False
    )
```

```python
import functools

import jax
import jax.numpy as jnp
from jax import lax
from jax.experimental import pallas as pl
from jax.experimental.pallas import tpu as pltpu
from jax.sharding import Mesh
from jax.sharding import PartitionSpec as P

HEAD_DIM = 64
BF = jnp.bfloat16
F32 = jnp.float32


def swap(values, axis, bit, name):
    size = lax.axis_size(axis)
    with jax.named_scope(name):
        return lax.ppermute(values, axis, [(i, i ^ bit) for i in range(size)])


def bits_of(axis, low=1):
    size = lax.axis_size(axis)
    found = []
    while low < size:
        found.append((axis, low))
        low *= 2
    return found


def side(axis, bit):
    return (lax.axis_index(axis) // bit) % 2


PAIR = 2 * HEAD_DIM
ATTEND_FLOPS = 20 * 10**9
BACK_FLOPS = 300 * 10**9
ATTBACK_FLOPS = 50 * 10**9
FIRST_FLOPS = 300 * 10**9
HIDE = -1000000000.0
VMEM_LIMIT = 64 * 1024 * 1024


def dot(left, right):
    return jnp.dot(left, right, preferred_element_type=F32)


def dot_nt(left, right):
    return lax.dot_general(left, right, (((1,), (1,)), ((), ())), preferred_element_type=F32)


def norm_parts(values):
    center = values - jnp.mean(values, axis=-1, keepdims=True)
    scale = lax.rsqrt(jnp.mean(center * center, axis=-1, keepdims=True) + 1e-05)
    return center * scale, scale


def norm_back(grad, normed, scale):
    along = jnp.mean(grad * normed, axis=-1, keepdims=True)
    return scale * (grad - jnp.mean(grad, axis=-1, keepdims=True) - normed * along)


def shaped(shape, dtype):
    return jax.ShapeDtypeStruct(shape, dtype)


def call(kernel, operands, after=(), alias=(), prefetch=(), flops=1, **options):
    extra = [*alias, *after]
    anywhere = pl.BlockSpec(memory_space=pl.ANY)
    options["in_specs"] = [*options["in_specs"], *[anywhere] * len(extra)]
    first = len(prefetch) + len(operands)
    fixed, skip = len(operands), len(extra)

    def body(*refs):
        cut = len(prefetch) + fixed
        kernel(*refs[:cut], *refs[cut + skip :])

    if prefetch:
        specs = {name: options.pop(name) for name in ("grid", "in_specs", "out_specs")}
        specs["scratch_shapes"] = options.pop("scratch_shapes", ())
        options["grid_spec"] = pltpu.PrefetchScalarGridSpec(
            num_scalar_prefetch=len(prefetch), **specs
        )
    return pl.pallas_call(
        body,
        input_output_aliases={first + i: i for i in range(len(alias))},
        compiler_params=pltpu.CompilerParams(vmem_limit_bytes=VMEM_LIMIT),
        cost_estimate=pl.CostEstimate(flops=flops, bytes_accessed=1, transcendentals=0),
        **options,
    )(*prefetch, *operands, *extra)


def whole(shape):
    return pl.BlockSpec(shape, lambda *_: (0,) * len(shape))


def plain(kernel, operands, out_shape, name, after=(), scratch=(), flops=1):
    return call(
        kernel,
        operands,
        after=after,
        flops=flops,
        grid=(1,),
        in_specs=[whole(x.shape) for x in operands],
        out_specs=jax.tree.map(lambda s: whole(s.shape), out_shape),
        out_shape=out_shape,
        scratch_shapes=scratch,
        name=name,
    )


def project_kernel(which_ref, x_ref, gain_ref, weight_ref, first_ref, out_ref):
    normed, _ = norm_parts(x_ref[...].astype(F32))
    first = (normed * gain_ref[...]).astype(BF)
    first_ref[0] = first
    for c in range(3):
        out_ref[c, 0] = dot(first, weight_ref[c]).astype(BF)


def project(which, rows, gain, weight, earlier, after=(), tiles=1):
    count, width = rows.shape
    cols = weight.shape[2]
    size = count // tiles
    return call(
        project_kernel,
        [rows, gain, weight],
        after=after,
        alias=earlier,
        prefetch=[which],
        grid=(tiles,),
        in_specs=[
            pl.BlockSpec((size, width), lambda i, w: (i, 0)),
            whole((1, width)),
            whole((3, width, cols)),
        ],
        out_specs=[
            pl.BlockSpec((1, size, width), lambda i, w: (w[0], i, 0)),
            pl.BlockSpec((3, 1, size, cols), lambda i, w: (0, w[0], i, 0)),
        ],
        out_shape=[shaped((2, count, width), BF), shaped((3, 2, count, cols), BF)],
        name="project",
    )


def attend_kernel(
    which_ref, q_ref, kd_ref, vd_ref, kc_ref, vc_ref, pos_ref,
    pd_ref, pc_ref, rl_ref, context_ref, bias_d, bias_c,
):
    count = q_ref.shape[2]
    step = count // 2

    @pl.when(pl.program_id(0) == 0)
    def _():
        row = lax.broadcasted_iota(jnp.int32, (count, count), 0)
        col = lax.broadcasted_iota(jnp.int32, (count, count), 1)
        start = row - pos_ref[0]
        bias_d[...] = jnp.where((col <= row) & (col >= start), 0.0, HIDE)
        bias_c[...] = jnp.where(col >= start + count, 0.0, HIDE)

    lane = lax.broadcasted_iota(jnp.int32, (1, PAIR), 1) // HEAD_DIM

    def half(late):
        blocks = [(at, a) for at in (0, step) for a in (0, 1)]
        for a in (0, 1):
            pd_ref[0, a, :step, step:] = jnp.zeros((step, step), BF)
        scores = []
        for at, a in blocks:
            rows, keys = pl.ds(at, step), at + step
            mine = jnp.where(lane == a, q_ref[0, 0, rows, :] * 0.125, 0.0).astype(BF)
            s_d = dot_nt(mine, kd_ref[0, 0, :keys, :]) + bias_d[rows, :keys]
            s_c = dot_nt(mine, kc_ref[0, 0]) + bias_c[rows, :] if late else None
            scores.append((s_d, s_c))
        mixed, scale = {}, {}
        for (at, a), (s_d, s_c) in zip(blocks, scores):
            rows, keys = pl.ds(at, step), at + step
            top = jnp.max(s_d, axis=-1, keepdims=True)
            if late:
                top = jnp.maximum(top, jnp.max(s_c, axis=-1, keepdims=True))
            p_d = jnp.exp(s_d - top)
            total = jnp.sum(p_d, axis=-1, keepdims=True)
            p_d = p_d.astype(BF)
            pd_ref[0, a, rows, :keys] = p_d
            value = jnp.where(lane == a, vd_ref[0, 0, :keys, :], 0.0).astype(BF)
            mix = dot(p_d, value)
            if late:
                p_c = jnp.exp(s_c - top)
                total = total + jnp.sum(p_c, axis=-1, keepdims=True)
                p_c = p_c.astype(BF)
                pc_ref[0, a, rows, :] = p_c
                value = jnp.where(lane == a, vc_ref[0, 0], 0.0).astype(BF)
                mix = mix + dot(p_c, value)
            mixed[at, a], scale[at, a] = mix, 1.0 / total
        for at in (0, step):
            rows = pl.ds(at, step)
            inverse = jnp.where(lane == 0, scale[at, 0], scale[at, 1])
            rl_ref[0, rows, :] = inverse
            context_ref[rows, :] = ((mixed[at, 0] + mixed[at, 1]) * inverse).astype(BF)

    pl.when(which_ref[0] == 0)(lambda: half(False))
    pl.when(which_ref[0] == 1)(lambda: half(True))


def attend(which, projected, positions, earlier, after=(), flops=1):
    _, _, count, cols = projected.shape
    heads = cols // HEAD_DIM

    def block(part, other):
        if other:
            return pl.BlockSpec((1, 1, count, PAIR), lambda g, w: (part, 0, 0, g))
        return pl.BlockSpec((1, 1, count, PAIR), lambda g, w: (part, w[0], 0, g))

    score_spec = pl.BlockSpec((1, 2, count, count), lambda g, w: (w[0], g, 0, 0))
    return call(
        attend_kernel,
        [*[projected] * 5, positions],
        after=after,
        alias=earlier,
        prefetch=[which],
        flops=flops,
        grid=(cols // PAIR,),
        in_specs=[
            block(0, False),
            block(1, False),
            block(2, False),
            block(1, True),
            block(2, True),
            pl.BlockSpec((1, count, 1), lambda g, w: (w[0], 0, 0)),
        ],
        out_specs=[
            score_spec,
            score_spec,
            pl.BlockSpec((1, count, PAIR), lambda g, w: (w[0], 0, g)),
            pl.BlockSpec((count, PAIR), lambda g, w: (0, g)),
        ],
        scratch_shapes=[pltpu.VMEM((count, count), F32)] * 2,
        out_shape=[
            shaped((2, heads, count, count), BF),
            shaped((2, heads, count, count), BF),
            shaped((2, count, cols), F32),
            shaped((count, cols), BF),
        ],
        name="attend",
    )


def hidden_kernel(
    x_ref, own_ref, got_ref, own_weight_ref, got_weight_ref, gain_ref, slot_ref, hidden_ref, *out_refs
):
    attended = dot(own_ref[...], own_weight_ref[...]) + dot(got_ref[...], got_weight_ref[...])
    hidden = x_ref[...].astype(F32) + attended
    hidden_ref[...] = hidden
    normed, _ = norm_parts(hidden)
    second = (normed * gain_ref[...]).astype(BF)
    send_rows(second, slot_ref, out_refs)


def send_rows(rows, slot_ref, out_refs):
    capacity = out_refs[0].shape[0]
    for k, ref in enumerate(out_refs):
        slot = lax.broadcasted_iota(jnp.int32, (capacity, rows.shape[0]), 0) + k * capacity
        place = jnp.where(slot_ref[...] == slot, 1.0, 0.0).astype(BF)
        ref[...] = dot(place, rows).astype(BF)


def hidden_rows(x, own, got, own_weight, got_weight, gain, slot_row, experts, after=()):
    count, width = x.shape
    out = [shaped((count, width), F32)] + [shaped((count // 2, width), BF)] * experts
    return plain(
        hidden_kernel,
        [x, own, got, own_weight, got_weight, gain, slot_row],
        out,
        "hidden_rows",
        after,
    )


def send_kernel(rows_ref, slot_ref, out_ref):
    send_rows(rows_ref[...], slot_ref, [out_ref.at[k] for k in range(out_ref.shape[0])])


def sent_rows(rows, slot_row, experts):
    count, width = rows.shape
    out = shaped((experts, count // 2, width), BF)
    return plain(send_kernel, [rows, slot_row], out, "sent_rows")


def taken_rows(slot_ref, block_refs):
    count, capacity = slot_ref.shape[1], block_refs[0].shape[0]
    total = 0.0
    for k, ref in enumerate(block_refs):
        slot = lax.broadcasted_iota(jnp.int32, (capacity, count), 0) + k * capacity
        place = jnp.where(slot_ref[...] == slot, 1.0, 0.0).astype(BF)
        total = total + lax.dot_general(
            place, ref[...], (((0,), (0,)), ((), ())), preferred_element_type=F32
        )
    return total


def output_kernel(hidden_ref, slot_ref, *refs):
    blocks = [refs[0].at[k] for k in range(refs[0].shape[0])]
    refs[-1][...] = (hidden_ref[...] + taken_rows(slot_ref, blocks)).astype(BF)


def output_rows(hidden, slot_row, blocks, after=()):
    return plain(
        output_kernel,
        [hidden, slot_row, blocks],
        shaped(hidden.shape, BF),
        "output_rows",
        after,
    )


def second_kernel(cot_ref, hidden_ref, gain_ref, slot_ref, own_weight_ref, got_weight_ref, *refs):
    grad_ref, low_ref, gain_grad_ref, own_ref, send_ref = refs[-5:]
    second_grad = taken_rows(slot_ref, refs[:-5])
    normed, scale = norm_parts(hidden_ref[...])
    gain_grad_ref[...] = jnp.sum(second_grad * normed, axis=0, keepdims=True)
    grad = cot_ref[...].astype(F32) + norm_back(second_grad * gain_ref[...], normed, scale)
    grad_ref[...] = grad
    low = grad.astype(BF)
    low_ref[...] = low
    send_ref[...] = dot_nt(low, got_weight_ref[...]).astype(BF)
    own_ref[...] = dot_nt(low, own_weight_ref[...]).astype(BF)


def second_back(cot, hidden, gain, slot_row, own_weight, got_weight, blocks, after=()):
    count, width = hidden.shape
    part = shaped((count, own_weight.shape[0]), BF)
    out = [
        shaped((count, width), F32),
        shaped((count, width), BF),
        shaped((1, width), F32),
        part,
        part,
    ]
    return plain(
        second_kernel,
        [cot, hidden, gain, slot_row, own_weight, got_weight, *blocks],
        out,
        "second_back",
        after,
        flops=BACK_FLOPS,
    )


def output_weight_kernel(
    core_ref, own_ref, got_ref, low_ref, own_out, kept_out, sent_out, scratch
):
    def part(ref):
        return lax.dot_general(
            ref[...], low_ref[...], (((0,), (0,)), ((), ())), preferred_element_type=F32
        ).astype(BF)

    scratch[...] = part(got_ref)
    rows = kept_out.shape[0]
    for ref, half in ((kept_out, core_ref[0]), (sent_out, 1 - core_ref[0])):
        ref[...] = scratch[pl.ds(pl.multiple_of(half * rows, rows), rows), :]
    own_out[...] = part(own_ref)


def output_weight_parts(core, own, got, low, after=()):
    cols, width = own.shape[1], low.shape[1]
    part = shaped((cols // 2, width), BF)
    out = [shaped((cols, width), BF), part, part]
    return call(
        output_weight_kernel,
        [own, got, low],
        after=after,
        prefetch=[core.reshape(1).astype(jnp.int32)],
        grid=(1,),
        in_specs=[whole(x.shape) for x in (own, got, low)],
        out_specs=[whole(o.shape) for o in out],
        out_shape=out,
        scratch_shapes=[pltpu.VMEM((cols, width), BF)],
        name="output_weight_parts",
    )


def first_kernel(x_ref, gain_ref, hidden_grad_ref, own_ref, theirs_ref, out_ref):
    grad = (own_ref[...] + theirs_ref[...].astype(F32)) * gain_ref[...]
    normed, scale = norm_parts(x_ref[...].astype(F32))
    out_ref[...] = hidden_grad_ref[...] + norm_back(grad, normed, scale)


def first_back(x, gain, hidden_grad, own, theirs, after=()):
    return plain(
        first_kernel,
        [x, gain, hidden_grad, own, theirs],
        shaped(x.shape, F32),
        "first_back",
        after,
        flops=FIRST_FLOPS,
    )


def fill(target, refs):
    rows = refs[0].shape[0]
    for i, ref in enumerate(refs):
        target[i * rows : (i + 1) * rows] = ref[...]


def expert_kernel(count, sub, place_ref, *refs):
    x_refs, cot_refs, refs = refs[:count], refs[count : 2 * count], refs[2 * count :]
    inner_ref, outer_ref, act_ref, pre_ref, out_ref, *grad_refs, x, cot, grad_acc, out_acc = refs
    at = pl.program_id(0)
    last = pl.num_programs(0) - count
    size = out_ref.shape[1]

    @pl.when(at > last)
    def _():
        rows = pl.ds(pl.multiple_of((at - last) * size, size), size)
        out_ref[0] = out_acc[rows, :].astype(BF)

    pl.when(at <= last)(
        lambda: expert_step(
            count, sub, x_refs, cot_refs, inner_ref, outer_ref, act_ref, pre_ref, out_ref,
            grad_refs, x, cot, grad_acc, out_acc, at, last,
        )
    )


def expert_step(
    count, sub, x_refs, cot_refs, inner_ref, outer_ref, act_ref, pre_ref, out_ref, grad_refs,
    x, cot, grad_acc, out_acc, at, last,
):

    @pl.when(at == 0)
    def _():
        fill(x, x_refs)
        fill(cot, [ref.at[0] for ref in cot_refs])
        grad_acc[...] = jnp.zeros_like(grad_acc)
        out_acc[...] = jnp.zeros_like(out_acc)

    def front(i):
        cols = slice(i * sub, (i + 1) * sub)
        return dot(x[...], inner_ref[:, cols]), dot_nt(cot[...], outer_ref[cols, :])

    parts = inner_ref.shape[1] // sub
    now = front(0)
    for i in range(parts):
        later = front(i + 1) if i + 1 < parts else None
        value, grad = now
        square = value * value
        half = 0.5 + 0.5 * jnp.tanh(
            value * (0.7978845608028654 + 0.035677408136300125 * square)
        )
        act = value * half
        slope = half + act * (1.0 - half) * (1.5957691216057308 + 0.21406444881780074 * square)
        cols = slice(i * sub, (i + 1) * sub)
        act_ref[:, cols] = act.astype(BF)
        pre_ref[:, cols] = (grad * slope).astype(BF)
        now = later
    grad_acc[...] += dot_nt(pre_ref[...], inner_ref[...])
    out_acc[...] += dot(act_ref[...], outer_ref[...])

    @pl.when(at == last)
    def _():
        size = out_ref.shape[1]
        out_ref[0] = out_acc[:size].astype(BF)
        for i, ref in enumerate(grad_refs):
            ref[...] = grad_acc[i * size : (i + 1) * size].astype(BF)


def expert(index, blocks, cot, places, inner, outer, earlier, after=(), tile=768, sub=256):
    count, width = blocks[0].shape
    size, units = len(blocks), inner.shape[1]
    total = count * cot.shape[0]
    tiles = units // tile

    def held(j):
        return jnp.minimum(j, tiles - 1)

    wide = pl.BlockSpec((count * size, tile), lambda j, p: (index // size, held(j)))
    out = pl.BlockSpec(
        (1, count, width), lambda j, p: (p[jnp.maximum(j - tiles + 1, 0)], 0, 0)
    )

    def placed(i):
        return pl.BlockSpec((1, count, width), lambda j, p: (p[i], 0, 0))

    return call(
        functools.partial(expert_kernel, size, sub),
        [*blocks, *[cot] * size, inner, outer],
        after=after,
        alias=earlier,
        prefetch=[jnp.stack(places).astype(jnp.int32)],
        grid=(tiles + size - 1,),
        in_specs=[whole((count, width))] * size
        + [placed(i) for i in range(size)]
        + [
            pl.BlockSpec((width, tile), lambda j, p: (0, held(j))),
            pl.BlockSpec((tile, width), lambda j, p: (held(j), 0)),
        ],
        out_specs=[wide, wide, out] + [whole((count, width))] * size,
        out_shape=[shaped((total, units), BF)] * 2
        + [shaped(cot.shape, BF)]
        + [shaped((count, width), BF)] * size,
        scratch_shapes=[pltpu.VMEM((count * size, width), BF)] * 2
        + [pltpu.VMEM((count * size, width), F32)] * 2,
        name="expert",
    )


def weight_kernel(count, which_ref, place_ref, act_ref, pre_ref, *refs):
    x_refs, (cot_ref, outer_out, inner_out, x, cot) = refs[:count], refs[count:]
    at = pl.program_id(0)
    half = pl.num_programs(0) // 2

    @pl.when(at == 0)
    def _():
        fill(cot, [cot_ref.at[place_ref[i]] for i in range(count)])
        fill(x, x_refs)

    def put(ref, left, right):
        ref[...] = lax.dot_general(
            left, right, (((0,), (0,)), ((), ())), preferred_element_type=F32
        ).astype(BF)

    pl.when(at < half)(lambda: put(outer_out, act_ref[...], cot[...]))
    pl.when(at >= half)(lambda: put(inner_out, x[...], pre_ref[...]))


def weight_parts(half, x_blocks, cot_blocks, places, act, pre, after=(), tiles=2):
    count, width = x_blocks[0].shape
    total, units = act.shape
    tile = units // 2 // tiles

    def early(j):
        return jnp.minimum(j, tiles - 1)

    def late(j):
        return jnp.maximum(j - tiles, 0)

    return call(
        functools.partial(weight_kernel, len(x_blocks)),
        [act, pre, *x_blocks, cot_blocks],
        after=after,
        prefetch=[half.reshape(1).astype(jnp.int32), jnp.stack(places).astype(jnp.int32)],
        grid=(2 * tiles,),
        in_specs=[
            pl.BlockSpec((total, tile), lambda j, w, p: (0, w[0] * tiles + early(j))),
            pl.BlockSpec((total, tile), lambda j, w, p: (0, w[0] * tiles + late(j))),
        ]
        + [whole((count, width))] * len(x_blocks)
        + [whole(cot_blocks.shape)],
        out_specs=[
            pl.BlockSpec((tile, width), lambda j, w, p: (early(j), 0)),
            pl.BlockSpec((width, tile), lambda j, w, p: (0, late(j))),
        ],
        out_shape=[shaped((units // 2, width), BF), shaped((width, units // 2), BF)],
        scratch_shapes=[pltpu.VMEM((total, width), BF)] * 2,
        name="weight_parts",
    )


def weight_sum_kernel(count, which_ref, place_ref, act_ref, pre_ref, *refs):
    x_refs, (cot_ref, outer_got, inner_got, *out_refs, x, cot) = refs[:count], refs[count:]
    at = pl.program_id(0)

    @pl.when(at == 0)
    def _():
        fill(cot, [cot_ref.at[place_ref[i]] for i in range(count)])
        fill(x, x_refs)

    def put(out_ref, got_ref, left, right):
        part = lax.dot_general(
            left, right, (((0,), (0,)), ((), ())), preferred_element_type=F32
        )
        out_ref[...] = (part + got_ref[...].astype(F32)).astype(BF)

    for i, out_ref in enumerate(out_refs):

        @pl.when(at == i)
        def _(i=i, out_ref=out_ref):
            if i < 2:
                put(out_ref, outer_got, act_ref[...], cot[...])
            else:
                put(out_ref, inner_got, x[...], pre_ref[...])


def weight_sums(
    half, outer_turn, inner_turn, x_blocks, cot_blocks, places, act, pre, outer_got, inner_got, after=()
):
    count, width = x_blocks[0].shape
    total, units = act.shape
    tile = units // 4

    def outer_at(j, w):
        return (w[1] + jnp.minimum(j, 1)) % 2

    def inner_at(j, w):
        return (w[2] + jnp.maximum(j - 2, 0)) % 2

    out = [shaped((tile, width), BF)] * 2 + [shaped((width, tile), BF)] * 2
    parts = call(
        functools.partial(weight_sum_kernel, len(x_blocks)),
        [act, pre, *x_blocks, cot_blocks, outer_got, inner_got],
        after=after,
        prefetch=[
            jnp.stack([half, outer_turn, inner_turn]).astype(jnp.int32),
            jnp.stack(places).astype(jnp.int32),
        ],
        grid=(4,),
        in_specs=[
            pl.BlockSpec((total, tile), lambda j, w, p: (0, w[0] * 2 + outer_at(j, w))),
            pl.BlockSpec((total, tile), lambda j, w, p: (0, w[0] * 2 + inner_at(j, w))),
        ]
        + [whole((count, width))] * len(x_blocks)
        + [
            whole(cot_blocks.shape),
            pl.BlockSpec((tile, width), lambda j, w, p: (outer_at(j, w), 0)),
            pl.BlockSpec((width, tile), lambda j, w, p: (0, inner_at(j, w))),
        ],
        out_specs=[whole(o.shape) for o in out],
        out_shape=out,
        scratch_shapes=[pltpu.VMEM((total, width), BF)] * 2,
        name="weight_sums",
    )
    return parts[:2], parts[2:]


def assemble_kernel(place_ref, *refs):
    *piece_refs, out_ref = refs
    for i, ref in enumerate(piece_refs):

        @pl.when(pl.program_id(0) == i)
        def _(ref=ref):
            out_ref[...] = ref[...].astype(F32)


def assemble_two_kernel(count, place_ref, *refs):
    *piece_refs, outer_ref, inner_ref = refs
    for i, ref in enumerate(piece_refs):

        @pl.when(pl.program_id(0) == i)
        def _(ref=ref, out_ref=outer_ref if i < count else inner_ref):
            out_ref[...] = ref[...].astype(F32)


def assemble_two(outer, inner, places, earlier, after=()):
    size, count = outer[0].shape, len(outer)
    table = jnp.stack([jnp.stack(place) for place in places]).astype(jnp.int32)

    def outer_at(i, t):
        held = jnp.minimum(i, count - 1)
        return t[held, 0], t[held, 1]

    def inner_at(i, t):
        held = jnp.maximum(i, count)
        return t[held, 0], t[held, 1]

    return call(
        functools.partial(assemble_two_kernel, count),
        [*outer, *inner],
        after=after,
        alias=earlier,
        prefetch=[table],
        grid=(2 * count,),
        in_specs=[whole(size)] * (2 * count),
        out_specs=[pl.BlockSpec(size, outer_at), pl.BlockSpec(size, inner_at)],
        out_shape=[shaped(x.shape, F32) for x in earlier],
        name="assemble_two",
    )


def assemble(pieces, places, shape, earlier, after=(), flops=1):
    size = pieces[0].shape
    table = jnp.stack([jnp.stack(place) for place in places]).astype(jnp.int32)
    return call(
        assemble_kernel,
        pieces,
        flops=flops,
        after=after,
        alias=earlier,
        prefetch=[table],
        grid=(len(pieces),),
        in_specs=[whole(size)] * len(pieces),
        out_specs=[pl.BlockSpec(size, lambda i, t: (t[i, 0], t[i, 1]))],
        out_shape=[shaped(shape, F32)],
        name="assemble",
    )


def add_kernel(kept_ref, got_ref, out_ref):
    out_ref[...] = (kept_ref[...].astype(F32) + got_ref[...].astype(F32)).astype(BF)


def add(kept, got):
    return plain(add_kernel, [kept, got], shaped(kept.shape, BF), "add")


def gather_sum_kernel(kept_ref, got_ref, more_ref, out_ref, tail_ref):
    rows, more = out_ref.shape[0], more_ref.shape[0]
    first = rows - more
    out_ref[:first] = (kept_ref[:first].astype(F32) + got_ref[:first].astype(F32)).astype(BF)
    last = kept_ref[first:rows].astype(F32) + got_ref[first:rows].astype(F32)
    out_ref[first:] = (last + more_ref[...].astype(F32)).astype(BF)
    tail_ref[...] = (kept_ref[rows:].astype(F32) + got_ref[rows:].astype(F32)).astype(BF)


def gather_sum(kept, got, more, rows, after=()):
    lines, width = kept.shape
    out = [shaped((rows, width), BF), shaped((lines - rows, width), BF)]
    return plain(gather_sum_kernel, [kept, got, more], out, "gather_sum", after)


def adds_kernel(count, cuts, place_ref, *refs):
    in_refs, out_refs = refs[: 2 * count], refs[2 * count :]
    for i in range(count):
        kept_ref, got_ref = in_refs[2 * i : 2 * i + 2]
        for j in range(cuts):
            ref = out_refs[cuts * i + j]
            rows = ref.shape[0]
            cut = pl.ds(pl.multiple_of(place_ref[cuts * i + j] * rows, rows), rows)
            ref[...] = (kept_ref[cut, :].astype(F32) + got_ref[cut, :].astype(F32)).astype(BF)


def adds(pairs, places, after=()):
    cuts = len(places[0])
    out = [
        shaped((kept.shape[0] // cuts, kept.shape[1]), BF) for kept, _ in pairs for _ in range(cuts)
    ]
    operands = [x for pair in pairs for x in pair]
    parts = call(
        functools.partial(adds_kernel, len(pairs), cuts),
        operands,
        after=after,
        prefetch=[jnp.stack([p for at in places for p in at]).astype(jnp.int32)],
        grid=(1,),
        in_specs=[whole(x.shape) for x in operands],
        out_specs=[whole(o.shape) for o in out],
        out_shape=out,
        name="adds",
    )
    return [parts[cuts * i : cuts * (i + 1)] for i in range(len(pairs))]


def gather_pieces(own, steps, order, flops):
    weights = {step: 1 << (len(steps) - 1 - i) for i, step in enumerate(steps)}
    place = sum(side(*step) * weight for step, weight in weights.items())
    pieces, newest = [(place, own)], [(0, place, own)]
    while newest:
        found = []
        for first, at, piece in newest:
            for i in range(first, len(order)):
                change = weights[order[i]] * (1 - 2 * side(*order[i]))
                found.append((i + 1, at + change, swap(piece, *order[i], "piece")))
        if len(pieces) == 1:
            held = touch([piece for _, _, piece in found], [], flops=flops)
            found = [(first, at, piece) for (first, at, _), piece in zip(found, held)]
        pieces += [(at, piece) for _, at, piece in found]
        newest = found
    return pieces


def total_kernel(in_ref, tail_ref, out_ref):
    count, rows = in_ref.shape[:2]
    value = sum(in_ref[i].astype(F32) for i in range(count)).astype(BF)
    for i in range(count):
        out_ref[i, :rows] = value
        out_ref[i, rows:] = tail_ref[...]


def total(blocks, tail, after=()):
    count, rows, width = blocks.shape
    out = shaped((count, rows + tail.shape[0], width), BF)
    return plain(total_kernel, [blocks, tail], out, "total", after)


def halves(step):
    mine = side(*step)
    return [1 - mine, mine]


def touch_kernel(*out_refs):
    pass


def touch(values, after, flops=1):
    return call(
        touch_kernel,
        [],
        after=after,
        alias=values,
        flops=flops,
        in_specs=[],
        out_specs=[pl.BlockSpec(memory_space=pl.ANY)] * len(values),
        out_shape=[shaped(x.shape, x.dtype) for x in values],
        name="touch",
    )


def back_kernel(
    at_ref, own_ref, other_ref, q_ref, k_ref, v_ref, pd_ref, pc_ref, own_context_ref,
    other_context_ref, rl_ref, first_ref, wp_ref, gain_ref, second_ref, own_output_ref,
    sent_ref, kept_ref, mine_ref, theirs_ref,
    acc, scaled, through, key_acc, value_acc, queries, weights, scores,
):
    group = pl.program_id(0)
    count = own_ref.shape[0]
    step = count // 2
    me, core = at_ref[0], at_ref[1]
    lane = lax.broadcasted_iota(jnp.int32, (1, PAIR), 1) // HEAD_DIM

    for ref, context, at in (
        (own_ref, own_context_ref, me),
        (other_ref, other_context_ref, 1 - me),
    ):
        grad = ref[...].astype(F32) * rl_ref[at]
        scaled[at] = grad
        through[at] = grad.astype(BF).astype(F32) * context[...].astype(F32)
    @pl.when(group == 0)
    def _():
        for h in (0, 1):
            for a in (0, 1):
                scores[h, a, :step, step:] = jnp.zeros((step, step), BF)

    for h in (0, 1):
        for at in (0, step):
            rows = pl.ds(at, step)
            low = scaled[h, rows, :].astype(BF)
            query = 0.0
            for a in (0, 1):
                mine = jnp.where(lane == a, low, 0.0).astype(BF)
                along = jnp.sum(
                    jnp.where(lane == a, through[h, rows, :], 0.0), axis=-1, keepdims=True
                )
                parts = [(pd_ref, h, h, at + step)]
                if h:
                    parts.append((pc_ref, 0, 2, count))
                for p_ref, p_at, to, keys in parts:
                    source = 0 if to == 2 else h
                    prob_grad = dot_nt(mine, v_ref[0, source, :keys, :])
                    p = p_ref[p_at, a, rows, :keys]
                    score = (p.astype(F32) * (prob_grad - along)).astype(BF)
                    scores[to, a, rows, :keys] = score
                    k = jnp.where(lane == a, k_ref[0, source, :keys, :], 0.0).astype(BF)
                    query = query + dot(score, k)
            queries[pl.ds(h * count + at, step), :] = query * 0.125
    low_t = [jnp.transpose(scaled[h]).astype(BF) for h in (0, 1)]
    q_t = [jnp.transpose(q_ref[0, h].astype(F32)).astype(BF) for h in (0, 1)]
    for a in (0, 1):
        line = slice(a * HEAD_DIM, (a + 1) * HEAD_DIM)
        key_acc[line, :count] = dot(q_t[0][line], scores[0, a]) + dot(q_t[1][line], scores[2, a])
        key_acc[line, count:] = dot(q_t[1][line], scores[1, a])
        value_acc[line, :count] = dot(low_t[0][line], pd_ref[0, a]) + dot(
            low_t[1][line], pc_ref[0, a]
        )
        value_acc[line, count:] = dot(low_t[1][line], pd_ref[1, a])

    query = queries[...]
    key_t = key_acc[...] * 0.125
    value_t = value_acc[...]
    both = jnp.concatenate(
        [query.astype(BF), jnp.transpose(key_t).astype(BF), jnp.transpose(value_t).astype(BF)],
        axis=1,
    )
    both_t = jnp.concatenate(
        [jnp.transpose(query).astype(BF), key_t.astype(BF), value_t.astype(BF)], axis=0
    )
    first = jnp.concatenate([first_ref[0], first_ref[1]], axis=0)
    weights[...] = dot(both_t, first)
    size = 3 * PAIR // 2
    groups = pl.num_programs(0)
    here = pl.ds(pl.multiple_of(group * size, size), size)
    for ref, half in ((sent_ref, 1 - core), (kept_ref, core)):
        ref[here, :] = weights[pl.ds(pl.multiple_of(half * size, size), size), :].astype(BF)
    weight = jnp.concatenate([wp_ref[0], wp_ref[1], wp_ref[2]], axis=1)
    added = dot_nt(both, weight)

    @pl.when(group == 0)
    def _():
        for h in (0, 1):
            acc[h] = added[h * count : (h + 1) * count]

    @pl.when(group > 0)
    def _():
        for h in (0, 1):
            acc[h] += added[h * count : (h + 1) * count]

    @pl.when(group == groups - 1)
    def _():
        mine_ref[...] = acc[me]
        theirs_ref[...] = acc[1 - me].astype(BF)
        gain = 0.0
        for h in (0, 1):
            gain = gain + jnp.sum(acc[h] * first_ref[h].astype(F32), axis=0, keepdims=True)
        gain = gain / gain_ref[...]
        part = own_output_ref.shape[0] // 2
        at = groups * size
        end = at + part
        for ref, half in ((sent_ref, 1 - core), (kept_ref, core)):
            cut = pl.ds(pl.multiple_of(half * part, part), part)
            ref[at:end, :] = own_output_ref[cut, :]
            value = jnp.where(half == 0, gain, second_ref[...])
            high = value.astype(BF).astype(F32)
            line = lax.broadcasted_iota(jnp.int32, (ref.shape[0] - end, value.shape[1]), 0)
            tail = jnp.where(line == 0, high, jnp.where(line == 1, value - high, 0.0))
            ref[end:, :] = tail.astype(BF)


def attend_back(
    at, own, other, projected, p_diag, p_cross, own_context, other_context, inverse, first, weight,
    gain, second, own_output, lines, after=(),
):
    _, _, count, cols = projected.shape
    width = first.shape[2]
    rows = whole((count, width))
    pair = pl.BlockSpec((count, PAIR), lambda g, w: (0, g))

    def block(part):
        return pl.BlockSpec((1, 2, count, PAIR), lambda g, w: (part, 0, 0, g))

    sent = shaped((lines, width), BF)
    out = [sent, sent, shaped((count, width), F32), shaped((count, width), BF)]
    return call(
        back_kernel,
        [
            own, other, projected, projected, projected, p_diag, p_cross, own_context,
            other_context, inverse, first, weight, gain, second, own_output,
        ],
        after=after,
        flops=ATTBACK_FLOPS,
        prefetch=[at],
        grid=(cols // PAIR,),
        in_specs=[
            pair,
            pair,
            block(0),
            block(1),
            block(2),
            pl.BlockSpec((2, 2, count, count), lambda g, w: (0, g, 0, 0)),
            pl.BlockSpec((1, 2, count, count), lambda g, w: (1, g, 0, 0)),
            pair,
            pair,
            pl.BlockSpec((2, count, PAIR), lambda g, w: (0, 0, g)),
            whole((2, count, width)),
            pl.BlockSpec((3, width, PAIR), lambda g, w: (0, 0, g)),
            whole((1, width)),
            whole((1, width)),
            whole((cols, width)),
        ],
        out_specs=[whole(o.shape) for o in out],
        scratch_shapes=[
            pltpu.VMEM((2, count, width), F32),
            pltpu.VMEM((2, count, PAIR), F32),
            pltpu.VMEM((2, count, PAIR), F32),
            pltpu.VMEM((PAIR, 2 * count), F32),
            pltpu.VMEM((PAIR, 2 * count), F32),
            pltpu.VMEM((2 * count, PAIR), F32),
            pltpu.VMEM((3 * PAIR, width), F32),
            pltpu.VMEM((3, 2, count, count), BF),
        ],
        out_shape=out,
        name="attend_back",
    )


def weight_outputs_kernel(rows, core_ref, kept_ref, got_ref, project_ref, output_ref, gains_ref):
    group, groups = pl.program_id(0), pl.num_programs(0)
    size = 3 * PAIR // 2

    def halves_of(cut, which):
        kept, got = [
            jnp.concatenate([ref[block, cut, :] for block in which], axis=0).astype(F32)
            for ref in (kept_ref, got_ref)
        ]
        low = jnp.where(core_ref[0] == 0, kept, got)
        return low, jnp.where(core_ref[0] == 0, got, kept)

    body, blocks = slice(0, rows), size // rows
    low, high = halves_of(body, [group * blocks + i for i in range(blocks)])
    flat = jnp.transpose(jnp.concatenate([low, high], axis=0))
    for c in range(3):
        project_ref[c] = flat[:, c * PAIR : (c + 1) * PAIR]

    @pl.when(group == groups - 1)
    def _():
        part, count = output_ref.shape[0] // 2, kept_ref.shape[0]
        first = groups * size // rows
        output_ref[:part], output_ref[part:] = halves_of(body, range(first, count))
        tails = halves_of(slice(rows, rows + 16), range(count))
        for i, tail in enumerate(tails):
            gains_ref[i : i + 1] = sum(
                tail[16 * b : 16 * b + 1] + tail[16 * b + 1 : 16 * b + 2] for b in range(count)
            )


def weight_outputs(core, kept, got, cols, after=()):
    _, rows, width = kept.shape
    return call(
        functools.partial(weight_outputs_kernel, rows - 16),
        [kept, got],
        after=after,
        prefetch=[core.reshape(1).astype(jnp.int32)],
        grid=(cols // PAIR,),
        in_specs=[whole(kept.shape)] * 2,
        out_specs=[
            pl.BlockSpec((3, width, PAIR), lambda g, w: (0, 0, g)),
            whole((cols, width)),
            whole((2, width)),
        ],
        out_shape=[shaped((3, width, cols), F32), shaped((cols, width), F32), shaped((2, width), F32)],
        name="weight_outputs",
    )


def on_device(
    block_input,
    output_cotangent,
    token_ids,
    positions,
    hash_table,
    first_gain,
    second_gain,
    project_weight,
    output_weight,
    expert_inner,
    expert_outer,
):
    tok_rows, model_width = block_input.shape
    local_cols = output_weight.shape[0]
    expert_count = lax.axis_size("expert")
    capacity = tok_rows // 2
    inner_weight = expert_inner[0]
    outer_weight = expert_outer[0]
    my_head = lax.axis_index("head")
    my_expert = lax.axis_index("expert")
    own_at = my_head.reshape(1).astype(jnp.int32)
    other_at = 1 - own_at
    first_gain = first_gain.reshape(1, model_width)
    second_gain = second_gain.reshape(1, model_width)

    other_input = swap(block_input, "head", 1, "rows")
    other_pos = swap(positions, "head", 1, "positions")
    seq_pos = jnp.where(
        my_head == 0, jnp.stack([positions, other_pos]), jnp.stack([other_pos, positions])
    )[:, :, None]

    chosen = jnp.take(hash_table, token_ids)
    relative = chosen ^ my_expert
    one_hot = relative[:, None] == jnp.arange(expert_count, dtype=jnp.int32)[None, :]
    rank_table = jnp.cumsum(one_hot.astype(jnp.int32), axis=0) - 1
    slot_index = relative * capacity + jnp.sum(jnp.where(one_hot, rank_table, 0), axis=1)
    slot_row = slot_index[None, :]
    absolute = slot_index + (chosen - relative) * capacity
    order = [my_expert ^ k for k in range(expert_count)]

    def exchange(blocks, name, first=0):
        return [
            swap(block, "expert", k, f"{name}{k}") if k else block
            for k, block in enumerate(blocks, first)
        ]

    def exchange_all(blocks):
        return lax.all_to_all(blocks, "expert", split_axis=0, concat_axis=0, tiled=True)

    sent = sent_rows(output_cotangent, absolute[None, :], expert_count)
    grad_blocks = exchange_all(sent)

    done = project(
        own_at, block_input, first_gain, project_weight, [], after=[sent, other_pos]
    )
    first_low, projected = project(other_at, other_input, first_gain, project_weight, done)
    other_weight = swap(touch([output_weight], [done[0]])[0], "head", 1, "output_weight")
    *done, other_context = attend(other_at, projected, seq_pos, [])
    got_context = swap(other_context, "head", 1, "context")
    p_diag, p_cross, inverse, own_context = attend(
        own_at,
        projected,
        seq_pos,
        done,
        after=[other_weight],
        flops=ATTEND_FLOPS,
    )
    hidden, *outgoing = hidden_rows(
        block_input,
        own_context,
        got_context,
        output_weight,
        other_weight,
        second_gain,
        slot_row,
        expert_count,
    )

    row_blocks = exchange(outgoing, "dispatch")
    done, returned, at = [], [], 0
    while at < expert_count:
        size = max(at, 1)
        parts = expert(
            at, row_blocks[at : at + size], grad_blocks, order[at : at + size], inner_weight,
            outer_weight, done,
        )
        done, grads = parts[:3], parts[3:]
        returned += exchange(grads, "return", at)
        at += size
    activated, pre_grad, produced = done

    core = lax.axis_index("core")
    turns = bits_of("x") + bits_of("head")
    outer_steps, inner_steps = turns, turns[::-1]
    outer_sent, inner_sent = weight_parts(
        1 - core, row_blocks, grad_blocks, order, activated, pre_grad, after=grads
    )
    outer_got = swap(outer_sent, "core", 1, "outer_core")
    inner_got = swap(inner_sent, "core", 1, "inner_core")
    token = touch([jnp.zeros((8, 128), F32)], [inner_sent], flops=BACK_FLOPS)
    outer_parts, inner_parts = weight_sums(
        core, 1 - side(*outer_steps[0]), 1 - side(*inner_steps[0]), row_blocks, grad_blocks, order,
        activated, pre_grad, outer_got, inner_got, after=token,
    )

    hidden_grad, hidden_low, second_gain_part, own_grad, grad_sent = second_back(
        output_cotangent,
        hidden,
        second_gain,
        slot_row,
        output_weight,
        other_weight,
        returned,
        after=[inner_parts[0]],
    )
    other_grad = swap(grad_sent, "head", 1, "context_grad")
    def pairs_of(outer, inner, i):
        return [
            (outer[1], swap(outer[0], *outer_steps[i], f"outer{i}")),
            (inner[1], swap(inner[0], *inner_steps[i], f"inner{i}")),
        ]

    own_output, output_kept, output_sent = output_weight_parts(
        core, own_context, got_context, hidden_low, after=[grad_sent]
    )
    output_sent = add(output_kept, swap(output_sent, "core", 1, "output_core"))
    combined = exchange_all(touch([produced], [output_sent])[0])
    got_output = swap(output_sent, "head", 1, "output_grad")

    groups = local_cols // PAIR
    end = 2 * local_cols
    lines = end + 16
    sent, kept, mine, theirs = attend_back(
        jnp.stack([my_head, core]).astype(jnp.int32), own_grad, other_grad, projected, p_diag,
        p_cross, own_context, other_context, inverse, first_low, project_weight, first_gain,
        second_gain_part, own_output, lines, after=[inner_parts[0]],
    )
    at = 3 * local_cols // 2
    for i in range(len(turns) - 1):
        outer_parts, inner_parts = adds(
            pairs_of(outer_parts, inner_parts, i),
            [halves(outer_steps[i + 1]), halves(inner_steps[i + 1])],
            after=[kept],
        )
    more = touch([got_output], outer_parts, flops=BACK_FLOPS)
    got = swap(sent, "core", 1, "weight")
    summed, tail = gather_sum(kept, got, more[0], end, after=more)
    crowd = ("x", "expert")
    summed = summed.reshape(-1, end // lax.axis_size(crowd), model_width)
    arrived = lax.all_to_all(summed, crowd, split_axis=0, concat_axis=0, tiled=True)
    theirs = swap(theirs, "head", 1, "theirs")
    block_output = output_rows(hidden, absolute[None, :], combined, after=[summed])
    input_grad = first_back(
        block_input, first_gain, hidden_grad, mine, theirs, after=[block_output]
    )
    (outer_own,), (inner_own,) = adds(
        pairs_of(outer_parts, inner_parts, -1), [[0 * core]] * 2, after=[input_grad]
    )
    outer_pieces = gather_pieces(outer_own, outer_steps, outer_steps[::-1], BACK_FLOPS)
    inner_pieces = gather_pieces(inner_own, inner_steps, inner_steps[::-1], 1)
    arrived = total(arrived, tail, after=[outer_own, inner_own])
    summed = lax.all_to_all(arrived, crowd, split_axis=0, concat_axis=0, tiled=True)

    def chosen_pieces(own_core, other_core, is_outer):
        half = 1 << (len(turns) - 1)

        def placed(place, which):
            if is_outer:
                return which * 2 * half + place, 0 * place
            return place % half, which * 2 + place // half

        return [
            (piece, placed(at, which))
            for pieces, which in ((own_core, core), (other_core, 1 - core))
            for at, piece in pieces
        ]

    early = len(turns) + 1

    def core_swaps(pieces):
        return [(at, swap(piece, "core", 1, "piece_core")) for at, piece in pieces]

    others = []
    for pieces in (outer_pieces, inner_pieces):
        (held,) = touch([pieces[0][1]], [arrived])
        others.append(core_swaps([(pieces[0][0], held), *pieces[1:early]]))
    totals = []
    for is_outer, own_core, other_core in zip(
        (True, False), (outer_pieces, inner_pieces), others
    ):
        chosen = chosen_pieces(own_core[:early], other_core, is_outer)
        totals += assemble(
            [piece for piece, _ in chosen],
            [place for _, place in chosen],
            (outer_weight if is_outer else inner_weight).shape,
            [],
            after=[arrived] + totals[-1:],
        )
    late = []
    for pieces in (outer_pieces, inner_pieces):
        held = touch([piece for _, piece in pieces[early:]], totals)
        late.append([(at, piece) for (at, _), piece in zip(pieces[early:], held)])
    late_others = [core_swaps(pieces) for pieces in late]
    (kept,) = touch([summed], [pieces[0][1] for pieces in late])
    got = swap(kept, "core", 1, "weight_back")
    project_grad, output_weight_grad, gains = weight_outputs(
        core, kept, got, local_cols
    )
    gains = gains + swap(gains, "head", 1, "gains")
    outer_late, inner_late = [
        chosen_pieces(own_core, other_core, is_outer)
        for own_core, other_core, is_outer in zip(late, late_others, (True, False))
    ]
    outer_total, inner_total = assemble_two(
        [piece for piece, _ in outer_late],
        [piece for piece, _ in inner_late],
        [place for _, place in outer_late + inner_late],
        totals,
        after=[project_grad],
    )
    return (
        block_output,
        input_grad,
        gains[0],
        gains[1],
        project_grad,
        output_weight_grad,
        inner_total[None],
        outer_total[None],
    )


def solution(mesh):
    devices = mesh.devices
    mesh = Mesh(
        devices.reshape(devices.shape[0] // 2, 2, *devices.shape[1:]), ("x", "core", "expert", "head")
    )
    in_specs = (
        P(("x", "core", "expert", "head"), None),
        P(("x", "core", "expert", "head"), None),
        P(("x", "core", "expert", "head")),
        P(("x", "core", "expert", "head")),
        P(),
        P(),
        P(),
        P(None, None, "head"),
        P("head", None),
        P("expert", None, None),
        P("expert", None, None),
    )
    out_specs = (
        P(("x", "core", "expert", "head"), None),
        P(("x", "core", "expert", "head"), None),
        P(),
        P(),
        P(None, None, "head"),
        P("head", None),
        P("expert", None, None),
        P("expert", None, None),
    )
    return jax.shard_map(
        on_device, mesh=mesh, in_specs=in_specs, out_specs=out_specs, check_vma=False
    )
```

```python
import functools

import jax
import jax.numpy as jnp
from jax import lax
from jax.experimental import pallas as pl
from jax.experimental.pallas import tpu as pltpu
from jax.sharding import Mesh
from jax.sharding import PartitionSpec as P

HEAD_DIM = 64
BF = jnp.bfloat16
F32 = jnp.float32


def swap(values, axis, bit, name):
    size = lax.axis_size(axis)
    with jax.named_scope(name):
        return lax.ppermute(values, axis, [(i, i ^ bit) for i in range(size)])


def bits_of(axis, low=1):
    size = lax.axis_size(axis)
    found = []
    while low < size:
        found.append((axis, low))
        low *= 2
    return found


def side(axis, bit):
    return (lax.axis_index(axis) // bit) % 2


PAIR = 2 * HEAD_DIM
CORE, OTHER_CORE, NONE, OUTER_TURN, INNER_TURN, ORDER = 2, 3, 4, 5, 6, 7
EXPERT_FLOPS = 2 * 10**9
ATTEND_FLOPS = 20 * 10**9
BACK_FLOPS = 300 * 10**9
ATTBACK_FLOPS = 50 * 10**9
FIRST_FLOPS = 300 * 10**9
HIDE = -1000000000.0
VMEM_LIMIT = 64 * 1024 * 1024


def dot(left, right):
    return jnp.dot(left, right, preferred_element_type=F32)


def dot_nt(left, right):
    return lax.dot_general(left, right, (((1,), (1,)), ((), ())), preferred_element_type=F32)


def norm_parts(values):
    center = values - jnp.mean(values, axis=-1, keepdims=True)
    scale = lax.rsqrt(jnp.mean(center * center, axis=-1, keepdims=True) + 1e-05)
    return center * scale, scale


def norm_back(grad, normed, scale):
    along = jnp.mean(grad * normed, axis=-1, keepdims=True)
    return scale * (grad - jnp.mean(grad, axis=-1, keepdims=True) - normed * along)


def shaped(shape, dtype):
    return jax.ShapeDtypeStruct(shape, dtype)


def call(kernel, operands, after=(), alias=(), prefetch=(), flops=1, **options):
    extra = [*alias, *after]
    anywhere = pl.BlockSpec(memory_space=pl.ANY)
    options["in_specs"] = [*options["in_specs"], *[anywhere] * len(extra)]
    first = len(prefetch) + len(operands)
    fixed, skip = len(operands), len(extra)

    def body(*refs):
        cut = len(prefetch) + fixed
        kernel(*refs[:cut], *refs[cut + skip :])

    if prefetch:
        specs = {name: options.pop(name) for name in ("grid", "in_specs", "out_specs")}
        specs["scratch_shapes"] = options.pop("scratch_shapes", ())
        options["grid_spec"] = pltpu.PrefetchScalarGridSpec(
            num_scalar_prefetch=len(prefetch), **specs
        )
    return pl.pallas_call(
        body,
        input_output_aliases={first + i: i for i in range(len(alias))},
        compiler_params=pltpu.CompilerParams(vmem_limit_bytes=VMEM_LIMIT),
        cost_estimate=pl.CostEstimate(flops=flops, bytes_accessed=1, transcendentals=0),
        **options,
    )(*prefetch, *operands, *extra)


def whole(shape):
    return pl.BlockSpec(shape, lambda *_: (0,) * len(shape))


def plain(kernel, operands, out_shape, name, after=(), scratch=(), flops=1):
    return call(
        kernel,
        operands,
        after=after,
        flops=flops,
        grid=(1,),
        in_specs=[whole(x.shape) for x in operands],
        out_specs=jax.tree.map(lambda s: whole(s.shape), out_shape),
        out_shape=out_shape,
        scratch_shapes=scratch,
        name=name,
    )


def project_kernel(which_ref, x_ref, gain_ref, weight_ref, first_ref, out_ref):
    normed, _ = norm_parts(x_ref[...].astype(F32))
    first = (normed * gain_ref[...]).astype(BF)
    first_ref[0] = first
    for c in range(3):
        out_ref[c, 0] = dot(first, weight_ref[c]).astype(BF)


def project(which, rows, gain, weight, earlier, after=(), tiles=1):
    count, width = rows.shape
    cols = weight.shape[2]
    size = count // tiles
    return call(
        project_kernel,
        [rows, gain, weight],
        after=after,
        alias=earlier,
        prefetch=[which],
        grid=(tiles,),
        in_specs=[
            pl.BlockSpec((size, width), lambda i, w: (i, 0)),
            whole((1, width)),
            whole((3, width, cols)),
        ],
        out_specs=[
            pl.BlockSpec((1, size, width), lambda i, w: (w[0], i, 0)),
            pl.BlockSpec((3, 1, size, cols), lambda i, w: (0, w[0], i, 0)),
        ],
        out_shape=[shaped((2, count, width), BF), shaped((3, 2, count, cols), BF)],
        name="project",
    )


def attend_kernel(
    which_ref, q_ref, kd_ref, vd_ref, kc_ref, vc_ref, pos_ref,
    pd_ref, pc_ref, rl_ref, context_ref, bias_d, bias_c,
):
    count = q_ref.shape[2]
    step = count // 2

    @pl.when(pl.program_id(0) == 0)
    def _():
        row = lax.broadcasted_iota(jnp.int32, (count, count), 0)
        col = lax.broadcasted_iota(jnp.int32, (count, count), 1)
        spread = jnp.broadcast_to(pos_ref[...].astype(F32), (8, count))
        start = row - jnp.transpose(spread)[:, :1].astype(jnp.int32)
        bias_d[...] = jnp.where((col <= row) & (col >= start), 0.0, HIDE)
        bias_c[...] = jnp.where(col >= start + count, 0.0, HIDE)

    lane = lax.broadcasted_iota(jnp.int32, (1, PAIR), 1) // HEAD_DIM

    def half(late):
        blocks = [(at, a) for at in (0, step) for a in (0, 1)]
        for a in (0, 1):
            pd_ref[0, a, :step, step:] = jnp.zeros((step, step), BF)
        scores = []
        for at, a in blocks:
            rows, keys = pl.ds(at, step), at + step
            mine = jnp.where(lane == a, q_ref[0, 0, rows, :] * 0.125, 0.0).astype(BF)
            s_d = dot_nt(mine, kd_ref[0, 0, :keys, :]) + bias_d[rows, :keys]
            s_c = dot_nt(mine, kc_ref[0, 0]) + bias_c[rows, :] if late else None
            scores.append((s_d, s_c))
        mixed, scale = {}, {}
        for (at, a), (s_d, s_c) in zip(blocks, scores):
            rows, keys = pl.ds(at, step), at + step
            top = jnp.max(s_d, axis=-1, keepdims=True)
            if late:
                top = jnp.maximum(top, jnp.max(s_c, axis=-1, keepdims=True))
            p_d = jnp.exp(s_d - top)
            total = jnp.sum(p_d, axis=-1, keepdims=True)
            p_d = p_d.astype(BF)
            pd_ref[0, a, rows, :keys] = p_d
            value = jnp.where(lane == a, vd_ref[0, 0, :keys, :], 0.0).astype(BF)
            mix = dot(p_d, value)
            if late:
                p_c = jnp.exp(s_c - top)
                total = total + jnp.sum(p_c, axis=-1, keepdims=True)
                p_c = p_c.astype(BF)
                pc_ref[0, a, rows, :] = p_c
                value = jnp.where(lane == a, vc_ref[0, 0], 0.0).astype(BF)
                mix = mix + dot(p_c, value)
            mixed[at, a], scale[at, a] = mix, 1.0 / total
        for at in (0, step):
            rows = pl.ds(at, step)
            inverse = jnp.where(lane == 0, scale[at, 0], scale[at, 1])
            rl_ref[0, rows, :] = inverse
            context_ref[rows, :] = ((mixed[at, 0] + mixed[at, 1]) * inverse).astype(BF)

    pl.when(which_ref[0] == 0)(lambda: half(False))
    pl.when(which_ref[0] == 1)(lambda: half(True))


def attend(which, projected, positions, earlier, after=(), flops=1):
    _, _, count, cols = projected.shape
    heads = cols // HEAD_DIM

    def block(part, other):
        if other:
            return pl.BlockSpec((1, 1, count, PAIR), lambda g, w: (part, 0, 0, g))
        return pl.BlockSpec((1, 1, count, PAIR), lambda g, w: (part, w[0], 0, g))

    score_spec = pl.BlockSpec((1, 2, count, count), lambda g, w: (w[0], g, 0, 0))
    return call(
        attend_kernel,
        [*[projected] * 5, positions],
        after=after,
        alias=earlier,
        prefetch=[which],
        flops=flops,
        grid=(cols // PAIR,),
        in_specs=[
            block(0, False),
            block(1, False),
            block(2, False),
            block(1, True),
            block(2, True),
            whole((1, count)),
        ],
        out_specs=[
            score_spec,
            score_spec,
            pl.BlockSpec((1, count, PAIR), lambda g, w: (w[0], 0, g)),
            pl.BlockSpec((count, PAIR), lambda g, w: (0, g)),
        ],
        scratch_shapes=[pltpu.VMEM((count, count), F32)] * 2,
        out_shape=[
            shaped((2, heads, count, count), BF),
            shaped((2, heads, count, count), BF),
            shaped((2, count, cols), F32),
            shaped((count, cols), BF),
        ],
        name="attend",
    )


def hidden_kernel(
    x_ref, own_ref, got_ref, own_weight_ref, got_weight_ref, gain_ref, slot_ref, hidden_ref, *out_refs
):
    attended = dot(own_ref[...], own_weight_ref[...]) + dot(got_ref[...], got_weight_ref[...])
    hidden = x_ref[...].astype(F32) + attended
    hidden_ref[...] = hidden
    normed, _ = norm_parts(hidden)
    second = (normed * gain_ref[...]).astype(BF)
    send_rows(second, slot_ref, out_refs)


def send_rows(rows, slot_ref, out_refs):
    capacity = out_refs[0].shape[0]
    for k, ref in enumerate(out_refs):
        slot = lax.broadcasted_iota(jnp.int32, (capacity, rows.shape[0]), 0) + k * capacity
        place = jnp.where(slot_ref[...] == slot, 1.0, 0.0).astype(BF)
        ref[...] = dot(place, rows).astype(BF)


def hidden_rows(x, own, got, own_weight, got_weight, gain, slot_row, experts, after=()):
    count, width = x.shape
    out = [shaped((count, width), F32)] + [shaped((count // 2, width), BF)] * experts
    return plain(
        hidden_kernel,
        [x, own, got, own_weight, got_weight, gain, slot_row],
        out,
        "hidden_rows",
        after,
    )


def send_kernel(rows_ref, slot_ref, weight_ref, out_ref, weight_out):
    send_rows(rows_ref[...], slot_ref, [out_ref.at[k] for k in range(out_ref.shape[0])])
    weight_out[...] = weight_ref[...]


def sent_rows(rows, slot_row, weight, experts, after=()):
    count, width = rows.shape
    out = [shaped((experts, count // 2, width), BF), shaped(weight.shape, BF)]
    return plain(send_kernel, [rows, slot_row, weight], out, "sent_rows", after)


def taken_rows(slot_ref, block_refs):
    count, capacity = slot_ref.shape[1], block_refs[0].shape[0]
    total = 0.0
    for k, ref in enumerate(block_refs):
        slot = lax.broadcasted_iota(jnp.int32, (capacity, count), 0) + k * capacity
        place = jnp.where(slot_ref[...] == slot, 1.0, 0.0).astype(BF)
        total = total + lax.dot_general(
            place, ref[...], (((0,), (0,)), ((), ())), preferred_element_type=F32
        )
    return total


def output_kernel(hidden_ref, slot_ref, *refs):
    blocks = [refs[0].at[k] for k in range(refs[0].shape[0])]
    refs[-1][...] = (hidden_ref[...] + taken_rows(slot_ref, blocks)).astype(BF)


def output_rows(hidden, slot_row, blocks, after=()):
    return plain(
        output_kernel,
        [hidden, slot_row, blocks],
        shaped(hidden.shape, BF),
        "output_rows",
        after,
    )


def second_kernel(cot_ref, hidden_ref, gain_ref, slot_ref, own_weight_ref, got_weight_ref, *refs):
    grad_ref, low_ref, gain_grad_ref, own_ref, send_ref = refs[-5:]
    second_grad = taken_rows(slot_ref, refs[:-5])
    normed, scale = norm_parts(hidden_ref[...])
    gain_grad_ref[...] = jnp.sum(second_grad * normed, axis=0, keepdims=True)
    grad = cot_ref[...].astype(F32) + norm_back(second_grad * gain_ref[...], normed, scale)
    grad_ref[...] = grad
    low = grad.astype(BF)
    low_ref[...] = low
    send_ref[...] = dot_nt(low, got_weight_ref[...]).astype(BF)
    own_ref[...] = dot_nt(low, own_weight_ref[...]).astype(BF)


def second_back(cot, hidden, gain, slot_row, own_weight, got_weight, blocks, after=()):
    count, width = hidden.shape
    part = shaped((count, own_weight.shape[0]), BF)
    out = [
        shaped((count, width), F32),
        shaped((count, width), BF),
        shaped((1, width), F32),
        part,
        part,
    ]
    return plain(
        second_kernel,
        [cot, hidden, gain, slot_row, own_weight, got_weight, *blocks],
        out,
        "second_back",
        after,
        flops=BACK_FLOPS,
    )


def output_weight_kernel(
    core_ref, own_ref, got_ref, low_ref, own_out, kept_out, sent_out, scratch
):
    def part(ref):
        return lax.dot_general(
            ref[...], low_ref[...], (((0,), (0,)), ((), ())), preferred_element_type=F32
        ).astype(BF)

    scratch[...] = part(got_ref)
    rows = kept_out.shape[0]
    for ref, half in ((kept_out, core_ref[0]), (sent_out, 1 - core_ref[0])):
        ref[...] = scratch[pl.ds(pl.multiple_of(half * rows, rows), rows), :]
    own_out[...] = part(own_ref)


def output_weight_parts(core, own, got, low, after=()):
    cols, width = own.shape[1], low.shape[1]
    part = shaped((cols // 2, width), BF)
    out = [shaped((cols, width), BF), part, part]
    return call(
        output_weight_kernel,
        [own, got, low],
        after=after,
        prefetch=[core],
        grid=(1,),
        in_specs=[whole(x.shape) for x in (own, got, low)],
        out_specs=[whole(o.shape) for o in out],
        out_shape=out,
        scratch_shapes=[pltpu.VMEM((cols, width), BF)],
        name="output_weight_parts",
    )


def first_kernel(x_ref, gain_ref, hidden_grad_ref, own_ref, theirs_ref, out_ref):
    grad = (own_ref[...] + theirs_ref[...].astype(F32)) * gain_ref[...]
    normed, scale = norm_parts(x_ref[...].astype(F32))
    out_ref[...] = hidden_grad_ref[...] + norm_back(grad, normed, scale)


def first_back(x, gain, hidden_grad, own, theirs, after=()):
    return plain(
        first_kernel,
        [x, gain, hidden_grad, own, theirs],
        shaped(x.shape, F32),
        "first_back",
        after,
        flops=FIRST_FLOPS,
    )


def fill(target, refs):
    rows = refs[0].shape[0]
    for i, ref in enumerate(refs):
        target[i * rows : (i + 1) * rows] = ref[...]


def expert_kernel(count, sub, place_ref, *refs):
    x_refs, cot_refs, refs = refs[:count], refs[count : 2 * count], refs[2 * count :]
    inner_ref, outer_ref, act_ref, pre_ref, out_ref, *grad_refs, x, cot, grad_acc, out_acc = refs
    at = pl.program_id(0)
    last = pl.num_programs(0) - count
    size = out_ref.shape[1]

    @pl.when(at > last)
    def _():
        rows = pl.ds(pl.multiple_of((at - last) * size, size), size)
        out_ref[0] = out_acc[rows, :].astype(BF)

    pl.when(at <= last)(
        lambda: expert_step(
            count, sub, x_refs, cot_refs, inner_ref, outer_ref, act_ref, pre_ref, out_ref,
            grad_refs, x, cot, grad_acc, out_acc, at, last,
        )
    )


def expert_step(
    count, sub, x_refs, cot_refs, inner_ref, outer_ref, act_ref, pre_ref, out_ref, grad_refs,
    x, cot, grad_acc, out_acc, at, last,
):

    @pl.when(at == 0)
    def _():
        fill(x, x_refs)
        fill(cot, [ref.at[0] for ref in cot_refs])
        grad_acc[...] = jnp.zeros_like(grad_acc)
        out_acc[...] = jnp.zeros_like(out_acc)

    def front(i):
        cols = slice(i * sub, (i + 1) * sub)
        return dot(x[...], inner_ref[:, cols]), dot_nt(cot[...], outer_ref[cols, :])

    parts = inner_ref.shape[1] // sub
    now = front(0)
    for i in range(parts):
        later = front(i + 1) if i + 1 < parts else None
        value, grad = now
        square = value * value
        half = 0.5 + 0.5 * jnp.tanh(
            value * (0.7978845608028654 + 0.035677408136300125 * square)
        )
        act = value * half
        slope = half + act * (1.0 - half) * (1.5957691216057308 + 0.21406444881780074 * square)
        cols = slice(i * sub, (i + 1) * sub)
        act_ref[:, cols] = act.astype(BF)
        pre_ref[:, cols] = (grad * slope).astype(BF)
        now = later
    grad_acc[...] += dot_nt(pre_ref[...], inner_ref[...])
    out_acc[...] += dot(act_ref[...], outer_ref[...])

    @pl.when(at == last)
    def _():
        size = out_ref.shape[1]
        out_ref[0] = out_acc[:size].astype(BF)
        for i, ref in enumerate(grad_refs):
            ref[...] = grad_acc[i * size : (i + 1) * size].astype(BF)


def expert(place, index, blocks, cot, inner, outer, earlier, after=(), tile=768, sub=256):
    count, width = blocks[0].shape
    size, units = len(blocks), inner.shape[1]
    total = count * cot.shape[0]
    tiles = units // tile

    def held(j):
        return jnp.minimum(j, tiles - 1)

    wide = pl.BlockSpec((count * size, tile), lambda j, p: (index // size, held(j)))
    out = pl.BlockSpec(
        (1, count, width), lambda j, p: (p[jnp.maximum(j - tiles + 1, 0)], 0, 0)
    )

    def placed(i):
        return pl.BlockSpec((1, count, width), lambda j, p: (p[i], 0, 0))

    return call(
        functools.partial(expert_kernel, size, sub),
        [*blocks, *[cot] * size, inner, outer],
        after=after,
        flops=EXPERT_FLOPS,
        alias=earlier,
        prefetch=[place],
        grid=(tiles + size - 1,),
        in_specs=[whole((count, width))] * size
        + [placed(i) for i in range(size)]
        + [
            pl.BlockSpec((width, tile), lambda j, p: (0, held(j))),
            pl.BlockSpec((tile, width), lambda j, p: (held(j), 0)),
        ],
        out_specs=[wide, wide, out] + [whole((count, width))] * size,
        out_shape=[shaped((total, units), BF)] * 2
        + [shaped(cot.shape, BF)]
        + [shaped((count, width), BF)] * size,
        scratch_shapes=[pltpu.VMEM((count * size, width), BF)] * 2
        + [pltpu.VMEM((count * size, width), F32)] * 2,
        name="expert",
    )


def weight_kernel(is_outer, count, added, info_ref, wide_ref, *refs):
    row_count = 1 if is_outer else count
    row_refs, refs = refs[:row_count], refs[row_count:]
    if is_outer:
        row_refs = [row_refs[0].at[info_ref[ORDER + i]] for i in range(count)]
    got_ref = refs[0] if added else None
    *out_refs, rows = refs[1:] if added else refs
    at = pl.program_id(0)
    pl.when(at == 0)(lambda: fill(rows, row_refs))

    def put(out_ref):
        sides = (wide_ref[...], rows[...]) if is_outer else (rows[...], wide_ref[...])
        part = lax.dot_general(*sides, (((0,), (0,)), ((), ())), preferred_element_type=F32)
        if added:
            part = part + got_ref[...].astype(F32)
        out_ref[...] = part.astype(BF)

    if added:
        for i, out_ref in enumerate(out_refs):
            pl.when(at == i)(functools.partial(put, out_ref))
    else:
        put(out_refs[0])


def weight_part(info, is_outer, half, turn, blocks, wide, got=None, after=()):
    total, units = wide.shape
    width, added, tile = blocks[0].shape[1], got is not None, units // 4
    count = len(blocks) if not is_outer else blocks.shape[0]
    if is_outer:
        row_specs, blocks = [whole(blocks.shape)], [blocks]
    else:
        row_specs = [whole(block.shape) for block in blocks]

    def at(j):
        return (j, 0) if is_outer else (0, j)

    def place(j, w):
        return (w[turn] + j) % 2

    def shape(units):
        return (units, width) if is_outer else (width, units)

    block = pl.BlockSpec(shape(tile), lambda j, w: at(place(j, w)))
    if added:
        out, out_specs = [shaped(shape(tile), BF)] * 2, [whole(shape(tile))] * 2
    else:
        out, out_specs = [shaped(shape(2 * tile), BF)], [block]
    return call(
        functools.partial(weight_kernel, is_outer, count, added),
        [wide, *blocks] + ([got] if added else []),
        after=after,
        prefetch=[info],
        grid=(2,),
        in_specs=[pl.BlockSpec((total, tile), lambda j, w: (0, w[half] * 2 + place(j, w)))]
        + row_specs
        + ([block] if added else []),
        out_specs=out_specs,
        out_shape=out,
        scratch_shapes=[pltpu.VMEM((total, width), BF)],
        name="weight_part",
    )


def assemble_kernel(counts, info_ref, *refs):
    piece_refs, out_refs = refs[: sum(counts)], refs[sum(counts) :]
    targets = [out for out, count in zip(out_refs, counts) for _ in range(count)]
    for i, (ref, out_ref) in enumerate(zip(piece_refs, targets)):

        @pl.when(pl.program_id(0) == i)
        def _(ref=ref, out_ref=out_ref):
            out_ref[...] = ref[...].astype(F32)


def assemble(info, start, groups, shapes, earlier, after=()):
    counts = [len(pieces) for pieces in groups]
    pieces = [piece for group in groups for piece in group]
    size = pieces[0].shape

    def spec(first, count):
        def at(i, t):
            held = start + 2 * jnp.clip(i, first, first + count - 1)
            return t[held], t[held + 1]

        return pl.BlockSpec(size, at)

    firsts = [sum(counts[:i]) for i in range(len(counts))]
    return call(
        functools.partial(assemble_kernel, counts),
        pieces,
        after=after,
        alias=earlier,
        prefetch=[info],
        grid=(len(pieces),),
        in_specs=[whole(size)] * len(pieces),
        out_specs=[spec(first, count) for first, count in zip(firsts, counts)],
        out_shape=[shaped(shape, F32) for shape in shapes],
        name="assemble",
    )


def add_kernel(kept_ref, got_ref, out_ref):
    out_ref[...] = (kept_ref[...].astype(F32) + got_ref[...].astype(F32)).astype(BF)


def add(kept, got):
    return plain(add_kernel, [kept, got], shaped(kept.shape, BF), "add")


def gather_sum_kernel(kept_ref, got_ref, more_ref, out_ref, tail_ref):
    rows, more = out_ref.shape[0], more_ref.shape[0]
    first = rows - more
    out_ref[:first] = (kept_ref[:first].astype(F32) + got_ref[:first].astype(F32)).astype(BF)
    last = kept_ref[first:rows].astype(F32) + got_ref[first:rows].astype(F32)
    out_ref[first:] = (last + more_ref[...].astype(F32)).astype(BF)
    tail_ref[...] = (kept_ref[rows:].astype(F32) + got_ref[rows:].astype(F32)).astype(BF)


def gather_sum(kept, got, more, rows, after=()):
    lines, width = kept.shape
    out = [shaped((rows, width), BF), shaped((lines - rows, width), BF)]
    return plain(gather_sum_kernel, [kept, got, more], out, "gather_sum", after)


def adds_kernel(start, count, cuts, info_ref, *refs):
    in_refs, out_refs = refs[: 2 * count], refs[2 * count :]
    for i in range(count):
        kept_ref, got_ref = in_refs[2 * i : 2 * i + 2]
        for j in range(cuts):
            ref = out_refs[cuts * i + j]
            rows = ref.shape[0]
            at = info_ref[start + cuts * i + j] if cuts > 1 else 0
            cut = pl.ds(pl.multiple_of(at * rows, rows), rows)
            ref[...] = (kept_ref[cut, :].astype(F32) + got_ref[cut, :].astype(F32)).astype(BF)


def adds(info, start, pairs, cuts, after=()):
    out = [
        shaped((kept.shape[0] // cuts, kept.shape[1]), BF) for kept, _ in pairs for _ in range(cuts)
    ]
    operands = [x for pair in pairs for x in pair]
    parts = call(
        functools.partial(adds_kernel, start, len(pairs), cuts),
        operands,
        after=after,
        prefetch=[info],
        grid=(1,),
        in_specs=[whole(x.shape) for x in operands],
        out_specs=[whole(o.shape) for o in out],
        out_shape=out,
        name="adds",
    )
    return [parts[cuts * i : cuts * (i + 1)] for i in range(len(pairs))]


def piece_places(steps, order):
    weights = {step: 1 << (len(steps) - 1 - i) for i, step in enumerate(steps)}
    place = sum(side(*step) * weight for step, weight in weights.items())
    places, newest = [place], [(0, place)]
    while newest:
        newest = [
            (i + 1, at + weights[order[i]] * (1 - 2 * side(*order[i])))
            for first, at in newest
            for i in range(first, len(order))
        ]
        places += [at for _, at in newest]
    return places


def gather_pieces(own, steps, order, flops):
    pieces, newest = [own], [(0, own)]
    while newest:
        found = [
            (i + 1, swap(piece, *order[i], "piece"))
            for first, piece in newest
            for i in range(first, len(order))
        ]
        if len(pieces) == 1:
            held = touch([piece for _, piece in found], [], flops=flops)
            found = [(first, piece) for (first, _), piece in zip(found, held)]
        pieces += [piece for _, piece in found]
        newest = found
    return list(zip(piece_places(steps, order), pieces))


def total_kernel(in_ref, tail_ref, got_ref, out_ref):
    count, rows = in_ref.shape[:2]
    value = sum(in_ref[i].astype(F32) for i in range(count)).astype(BF)
    tail = sum(ref[i : i + 1].astype(F32) for ref in (tail_ref, got_ref) for i in (0, 1))
    high = tail.astype(BF).astype(F32)
    line = lax.broadcasted_iota(jnp.int32, tail_ref.shape, 0)
    tail = jnp.where(line == 0, high, jnp.where(line == 1, tail - high, 0.0)).astype(BF)
    for i in range(count):
        out_ref[i, :rows] = value
        out_ref[i, rows:] = tail


def total(blocks, tail, got, after=()):
    count, rows, width = blocks.shape
    out = shaped((count, rows + tail.shape[0], width), BF)
    return plain(total_kernel, [blocks, tail, got], out, "total", after)


def halves(step):
    mine = side(*step)
    return [1 - mine, mine]


def touch_kernel(*out_refs):
    pass


def touch(values, after, flops=1):
    return call(
        touch_kernel,
        [],
        after=after,
        alias=values,
        flops=flops,
        in_specs=[],
        out_specs=[pl.BlockSpec(memory_space=pl.ANY)] * len(values),
        out_shape=[shaped(x.shape, x.dtype) for x in values],
        name="touch",
    )


def back_kernel(
    at_ref, own_ref, other_ref, q_ref, k_ref, v_ref, pd_ref, pc_ref, own_context_ref,
    other_context_ref, rl_ref, first_ref, wp_ref, gain_ref, second_ref, own_output_ref,
    sent_ref, kept_ref, mine_ref, theirs_ref,
    acc, scaled, through, key_acc, value_acc, queries, weights, scores,
):
    group = pl.program_id(0)
    count = own_ref.shape[0]
    step = count // 2
    me, core = at_ref[0], at_ref[CORE]
    lane = lax.broadcasted_iota(jnp.int32, (1, PAIR), 1) // HEAD_DIM

    for ref, context, at in (
        (own_ref, own_context_ref, me),
        (other_ref, other_context_ref, 1 - me),
    ):
        grad = ref[...].astype(F32) * rl_ref[at]
        scaled[at] = grad
        through[at] = grad.astype(BF).astype(F32) * context[...].astype(F32)
    @pl.when(group == 0)
    def _():
        for h in (0, 1):
            for a in (0, 1):
                scores[h, a, :step, step:] = jnp.zeros((step, step), BF)

    for h in (0, 1):
        for at in (0, step):
            rows = pl.ds(at, step)
            low = scaled[h, rows, :].astype(BF)
            query = 0.0
            for a in (0, 1):
                mine = jnp.where(lane == a, low, 0.0).astype(BF)
                along = jnp.sum(
                    jnp.where(lane == a, through[h, rows, :], 0.0), axis=-1, keepdims=True
                )
                parts = [(pd_ref, h, h, at + step)]
                if h:
                    parts.append((pc_ref, 0, 2, count))
                for p_ref, p_at, to, keys in parts:
                    source = 0 if to == 2 else h
                    prob_grad = dot_nt(mine, v_ref[0, source, :keys, :])
                    p = p_ref[p_at, a, rows, :keys]
                    score = (p.astype(F32) * (prob_grad - along)).astype(BF)
                    scores[to, a, rows, :keys] = score
                    k = jnp.where(lane == a, k_ref[0, source, :keys, :], 0.0).astype(BF)
                    query = query + dot(score, k)
            queries[pl.ds(h * count + at, step), :] = query * 0.125
    low_t = [jnp.transpose(scaled[h]).astype(BF) for h in (0, 1)]
    q_t = [jnp.transpose(q_ref[0, h].astype(F32)).astype(BF) for h in (0, 1)]
    for a in (0, 1):
        line = slice(a * HEAD_DIM, (a + 1) * HEAD_DIM)
        key_acc[line, :count] = dot(q_t[0][line], scores[0, a]) + dot(q_t[1][line], scores[2, a])
        key_acc[line, count:] = dot(q_t[1][line], scores[1, a])
        value_acc[line, :count] = dot(low_t[0][line], pd_ref[0, a]) + dot(
            low_t[1][line], pc_ref[0, a]
        )
        value_acc[line, count:] = dot(low_t[1][line], pd_ref[1, a])

    query = queries[...]
    key_t = key_acc[...] * 0.125
    value_t = value_acc[...]
    both = jnp.concatenate(
        [query.astype(BF), jnp.transpose(key_t).astype(BF), jnp.transpose(value_t).astype(BF)],
        axis=1,
    )
    both_t = jnp.concatenate(
        [jnp.transpose(query).astype(BF), key_t.astype(BF), value_t.astype(BF)], axis=0
    )
    first = jnp.concatenate([first_ref[0], first_ref[1]], axis=0)
    weights[...] = dot(both_t, first)
    size = 3 * PAIR // 2
    groups = pl.num_programs(0)
    here = pl.ds(pl.multiple_of(group * size, size), size)
    for ref, half in ((sent_ref, 1 - core), (kept_ref, core)):
        ref[here, :] = weights[pl.ds(pl.multiple_of(half * size, size), size), :].astype(BF)
    weight = jnp.concatenate([wp_ref[0], wp_ref[1], wp_ref[2]], axis=1)
    added = dot_nt(both, weight)

    @pl.when(group == 0)
    def _():
        for h in (0, 1):
            acc[h] = added[h * count : (h + 1) * count]

    @pl.when(group > 0)
    def _():
        for h in (0, 1):
            acc[h] += added[h * count : (h + 1) * count]

    @pl.when(group == groups - 1)
    def _():
        mine_ref[...] = acc[me]
        theirs_ref[...] = acc[1 - me].astype(BF)
        gain = 0.0
        for h in (0, 1):
            gain = gain + jnp.sum(acc[h] * first_ref[h].astype(F32), axis=0, keepdims=True)
        gain = gain / gain_ref[...]
        part = own_output_ref.shape[0] // 2
        at = groups * size
        end = at + part
        for ref, half in ((sent_ref, 1 - core), (kept_ref, core)):
            cut = pl.ds(pl.multiple_of(half * part, part), part)
            ref[at:end, :] = own_output_ref[cut, :]
            value = jnp.where(half == 0, gain, second_ref[...])
            high = value.astype(BF).astype(F32)
            line = lax.broadcasted_iota(jnp.int32, (ref.shape[0] - end, value.shape[1]), 0)
            tail = jnp.where(line == 0, high, jnp.where(line == 1, value - high, 0.0))
            ref[end:, :] = tail.astype(BF)


def attend_back(
    at, own, other, projected, p_diag, p_cross, own_context, other_context, inverse, first, weight,
    gain, second, own_output, lines, after=(),
):
    _, _, count, cols = projected.shape
    width = first.shape[2]
    rows = whole((count, width))
    pair = pl.BlockSpec((count, PAIR), lambda g, w: (0, g))

    def block(part):
        return pl.BlockSpec((1, 2, count, PAIR), lambda g, w: (part, 0, 0, g))

    sent = shaped((lines, width), BF)
    out = [sent, sent, shaped((count, width), F32), shaped((count, width), BF)]
    return call(
        back_kernel,
        [
            own, other, projected, projected, projected, p_diag, p_cross, own_context,
            other_context, inverse, first, weight, gain, second, own_output,
        ],
        after=after,
        flops=ATTBACK_FLOPS,
        prefetch=[at],
        grid=(cols // PAIR,),
        in_specs=[
            pair,
            pair,
            block(0),
            block(1),
            block(2),
            pl.BlockSpec((2, 2, count, count), lambda g, w: (0, g, 0, 0)),
            pl.BlockSpec((1, 2, count, count), lambda g, w: (1, g, 0, 0)),
            pair,
            pair,
            pl.BlockSpec((2, count, PAIR), lambda g, w: (0, 0, g)),
            whole((2, count, width)),
            pl.BlockSpec((3, width, PAIR), lambda g, w: (0, 0, g)),
            whole((1, width)),
            whole((1, width)),
            whole((cols, width)),
        ],
        out_specs=[whole(o.shape) for o in out],
        scratch_shapes=[
            pltpu.VMEM((2, count, width), F32),
            pltpu.VMEM((2, count, PAIR), F32),
            pltpu.VMEM((2, count, PAIR), F32),
            pltpu.VMEM((PAIR, 2 * count), F32),
            pltpu.VMEM((PAIR, 2 * count), F32),
            pltpu.VMEM((2 * count, PAIR), F32),
            pltpu.VMEM((3 * PAIR, width), F32),
            pltpu.VMEM((3, 2, count, count), BF),
        ],
        out_shape=out,
        name="attend_back",
    )


def weight_outputs_kernel(rows, core_ref, kept_ref, got_ref, project_ref, output_ref, gains_ref):
    group, groups = pl.program_id(0), pl.num_programs(0)
    size = 3 * PAIR // 2

    def halves_of(cut, which):
        kept, got = [
            jnp.concatenate([ref[block, cut, :] for block in which], axis=0).astype(F32)
            for ref in (kept_ref, got_ref)
        ]
        low = jnp.where(core_ref[0] == 0, kept, got)
        return low, jnp.where(core_ref[0] == 0, got, kept)

    body, blocks = slice(0, rows), size // rows
    low, high = halves_of(body, [group * blocks + i for i in range(blocks)])
    flat = jnp.transpose(jnp.concatenate([low, high], axis=0))
    for c in range(3):
        project_ref[c] = flat[:, c * PAIR : (c + 1) * PAIR]

    @pl.when(group == groups - 1)
    def _():
        part, count = output_ref.shape[0] // 2, kept_ref.shape[0]
        first = groups * size // rows
        output_ref[:part], output_ref[part:] = halves_of(body, range(first, count))
        tails = halves_of(slice(rows, rows + 16), range(count))
        for i, tail in enumerate(tails):
            gains_ref[i : i + 1] = sum(
                tail[16 * b : 16 * b + 1] + tail[16 * b + 1 : 16 * b + 2] for b in range(count)
            )


def weight_outputs(core, kept, got, cols, after=()):
    _, rows, width = kept.shape
    return call(
        functools.partial(weight_outputs_kernel, rows - 16),
        [kept, got],
        after=after,
        prefetch=[core],
        grid=(cols // PAIR,),
        in_specs=[whole(kept.shape)] * 2,
        out_specs=[
            pl.BlockSpec((3, width, PAIR), lambda g, w: (0, 0, g)),
            whole((cols, width)),
            whole((2, width)),
        ],
        out_shape=[shaped((3, width, cols), F32), shaped((cols, width), F32), shaped((2, width), F32)],
        name="weight_outputs",
    )


def on_device(
    block_input,
    output_cotangent,
    token_ids,
    positions,
    hash_table,
    first_gain,
    second_gain,
    project_weight,
    output_weight,
    expert_inner,
    expert_outer,
):
    tok_rows, model_width = block_input.shape
    local_cols = output_weight.shape[0]
    expert_count = lax.axis_size("expert")
    capacity = tok_rows // 2
    inner_weight = expert_inner[0]
    outer_weight = expert_outer[0]
    my_head = lax.axis_index("head")
    my_expert = lax.axis_index("expert")
    core = lax.axis_index("core")
    turns = bits_of("x") + bits_of("head")
    outer_steps, inner_steps = turns, turns[::-1]
    order = [my_expert ^ k for k in range(expert_count)]

    early = len(turns) + 1
    entries = [
        my_head, 1 - my_head, core, 1 - core, 0 * core,
        1 - side(*outer_steps[0]), 1 - side(*inner_steps[0]), *order,
    ]
    adds_at = [len(entries) + 4 * i for i in range(len(turns) - 1)]
    for i in range(1, len(turns)):
        entries += [*halves(outer_steps[i]), *halves(inner_steps[i])]
    half = 1 << (len(turns) - 1)

    def placed(place, which, is_outer):
        if is_outer:
            return [which * 2 * half + place, 0 * place]
        return [place % half, which * 2 + place // half]

    piece_at = []
    for chosen in (slice(early), slice(early, None)):
        for steps, is_outer in ((outer_steps, True), (inner_steps, False)):
            piece_at.append(len(entries))
            for which in (core, 1 - core):
                for place in piece_places(steps, steps[::-1])[chosen]:
                    entries += placed(place, which, is_outer)
    info = jnp.stack(entries).astype(jnp.int32)
    own_at, core_at = my_head.reshape(1).astype(jnp.int32), core.reshape(1).astype(jnp.int32)
    other_at = 1 - own_at
    first_gain = first_gain.reshape(1, model_width)
    second_gain = second_gain.reshape(1, model_width)

    other_input = swap(block_input, "head", 1, "rows")
    other_pos = swap(positions, "head", 1, "positions")

    chosen = jnp.take(hash_table, token_ids)
    relative = chosen ^ my_expert
    one_hot = relative[:, None] == jnp.arange(expert_count, dtype=jnp.int32)[None, :]
    rank_table = jnp.cumsum(one_hot.astype(jnp.int32), axis=0) - 1
    slot_index = relative * capacity + jnp.sum(jnp.where(one_hot, rank_table, 0), axis=1)
    slot_row = slot_index[None, :]
    absolute = slot_index + (chosen - relative) * capacity

    def exchange(blocks, name, first=0):
        return [
            swap(block, "expert", k, f"{name}{k}") if k else block
            for k, block in enumerate(blocks, first)
        ]

    def exchange_all(blocks):
        return lax.all_to_all(blocks, "expert", split_axis=0, concat_axis=0, tiled=True)

    done = project(own_at, block_input, first_gain, project_weight, [])
    sent, weight_sent = sent_rows(
        output_cotangent, absolute[None, :], output_weight, expert_count, after=[done[0], other_pos]
    )
    grad_blocks = exchange_all(sent)
    first_low, projected = project(other_at, other_input, first_gain, project_weight, done)
    other_weight = swap(weight_sent, "head", 1, "output_weight")
    *done, other_context = attend(other_at, projected, other_pos[None, :], [])
    got_context = swap(other_context, "head", 1, "context")
    p_diag, p_cross, inverse, own_context = attend(
        own_at,
        projected,
        positions[None, :],
        done,
        after=[other_weight],
        flops=ATTEND_FLOPS,
    )
    hidden, *outgoing = hidden_rows(
        block_input,
        own_context,
        got_context,
        output_weight,
        other_weight,
        second_gain,
        slot_row,
        expert_count,
    )

    row_blocks = exchange(outgoing, "dispatch")
    done, returned, at = [], [], 0
    while at < expert_count:
        size = 1
        parts = expert(
            order[at].reshape(1).astype(jnp.int32), at, row_blocks[at : at + size], grad_blocks if at else sent, inner_weight,
            outer_weight, done,
        )
        done, grads = parts[:3], parts[3:]
        returned += exchange(grads, "return", at)
        at += size
    activated, pre_grad, produced = done

    (outer_sent,) = weight_part(info, True, OTHER_CORE, NONE, grad_blocks, activated, after=grads)
    outer_got = swap(outer_sent, "core", 1, "outer_core")
    (inner_sent,) = weight_part(
        info, False, OTHER_CORE, NONE, row_blocks, pre_grad, after=[outer_sent]
    )
    inner_got = swap(inner_sent, "core", 1, "inner_core")
    token = touch([jnp.zeros((8, 128), F32)], [inner_sent], flops=BACK_FLOPS)
    outer_parts = weight_part(
        info, True, CORE, OUTER_TURN, grad_blocks, activated, outer_got, after=token
    )
    inner_parts = weight_part(
        info, False, CORE, INNER_TURN, row_blocks, pre_grad, inner_got, after=[outer_parts[0]]
    )

    hidden_grad, hidden_low, second_gain_part, own_grad, grad_sent = second_back(
        output_cotangent,
        hidden,
        second_gain,
        slot_row,
        output_weight,
        other_weight,
        returned,
        after=[inner_parts[0]],
    )
    other_grad = swap(grad_sent, "head", 1, "context_grad")
    def pairs_of(outer, inner, i):
        return [
            (outer[1], swap(outer[0], *outer_steps[i], f"outer{i}")),
            (inner[1], swap(inner[0], *inner_steps[i], f"inner{i}")),
        ]

    own_output, output_kept, output_sent = output_weight_parts(
        core_at, own_context, got_context, hidden_low, after=[grad_sent]
    )
    output_sent = add(output_kept, swap(output_sent, "core", 1, "output_core"))
    combined = exchange_all(touch([produced], [output_sent])[0])
    got_output = swap(output_sent, "head", 1, "output_grad")

    groups = local_cols // PAIR
    end = 2 * local_cols
    lines = end + 16
    sent, kept, mine, theirs = attend_back(
        info, own_grad, other_grad, projected, p_diag,
        p_cross, own_context, other_context, inverse, first_low, project_weight, first_gain,
        second_gain_part, own_output, lines, after=[inner_parts[0]],
    )
    at = 3 * local_cols // 2
    for i in range(len(turns) - 1):
        outer_parts, inner_parts = adds(
            info, adds_at[i], pairs_of(outer_parts, inner_parts, i), 2, after=[kept]
        )
    more = touch([got_output], outer_parts, flops=BACK_FLOPS)
    got = swap(sent, "core", 1, "weight")
    summed, tail = gather_sum(kept, got, more[0], end, after=more)
    crowd = ("x", "expert")
    summed = summed.reshape(-1, end // lax.axis_size(crowd), model_width)
    arrived = lax.all_to_all(summed, crowd, split_axis=0, concat_axis=0, tiled=True)
    theirs = swap(theirs, "head", 1, "theirs")
    block_output = output_rows(hidden, absolute[None, :], combined, after=[summed])
    input_grad = first_back(
        block_input, first_gain, hidden_grad, mine, theirs, after=[block_output]
    )
    got_tail = swap(tail, "head", 1, "gains")
    (outer_own,), (inner_own,) = adds(
        info, 0, pairs_of(outer_parts, inner_parts, -1), 1, after=[input_grad, got_tail]
    )
    outer_pieces = gather_pieces(outer_own, outer_steps, outer_steps[::-1], BACK_FLOPS)
    inner_pieces = gather_pieces(inner_own, inner_steps, inner_steps[::-1], 1)
    arrived = total(
        arrived, tail, got_tail, after=[outer_own, inner_own]
    )
    summed = lax.all_to_all(arrived, crowd, split_axis=0, concat_axis=0, tiled=True)

    def core_swaps(pieces):
        return [(at, swap(piece, "core", 1, "piece_core")) for at, piece in pieces]

    others = []
    for pieces in (outer_pieces, inner_pieces):
        (held,) = touch([pieces[0][1]], [arrived])
        others.append(core_swaps([(pieces[0][0], held), *pieces[1:early]]))
    shapes = [outer_weight.shape, inner_weight.shape]
    totals = []
    for i, pieces in enumerate((outer_pieces, inner_pieces)):
        chosen = [piece for _, piece in pieces[:early] + others[i]]
        totals += assemble(
            info, piece_at[i], [chosen], shapes[i : i + 1], [], after=[arrived] + totals[-1:]
        )
    late = []
    for pieces in (outer_pieces, inner_pieces):
        held = touch([piece for _, piece in pieces[early:]], totals)
        late.append([(at, piece) for (at, _), piece in zip(pieces[early:], held)])
    late_others = [core_swaps(pieces) for pieces in late]
    (kept,) = touch([summed], [pieces[0][1] for pieces in late])
    got = swap(kept, "core", 1, "weight_back")
    project_grad, output_weight_grad, gains = weight_outputs(core_at, kept, got, local_cols)
    chosen = [
        [piece for _, piece in own + other] for own, other in zip(late, late_others)
    ]
    outer_total, inner_total = assemble(
        info, piece_at[2], chosen, shapes, totals, after=[project_grad]
    )
    return (
        block_output,
        input_grad,
        gains[0],
        gains[1],
        project_grad,
        output_weight_grad,
        inner_total[None],
        outer_total[None],
    )


def solution(mesh):
    devices = mesh.devices
    mesh = Mesh(
        devices.reshape(devices.shape[0] // 2, 2, *devices.shape[1:]), ("x", "core", "expert", "head")
    )
    in_specs = (
        P(("x", "core", "expert", "head"), None),
        P(("x", "core", "expert", "head"), None),
        P(("x", "core", "expert", "head")),
        P(("x", "core", "expert", "head")),
        P(),
        P(),
        P(),
        P(None, None, "head"),
        P("head", None),
        P("expert", None, None),
        P("expert", None, None),
    )
    out_specs = (
        P(("x", "core", "expert", "head"), None),
        P(("x", "core", "expert", "head"), None),
        P(),
        P(),
        P(None, None, "head"),
        P("head", None),
        P("expert", None, None),
        P("expert", None, None),
    )
    return jax.shard_map(
        on_device, mesh=mesh, in_specs=in_specs, out_specs=out_specs, check_vma=False
    )
```

```python
import functools

import jax
import jax.numpy as jnp
from jax import lax
from jax.experimental import pallas as pl
from jax.experimental.pallas import tpu as pltpu
from jax.sharding import Mesh
from jax.sharding import PartitionSpec as P

HEAD_DIM = 64
BF = jnp.bfloat16
F32 = jnp.float32


def swap(values, axis, bit, name):
    size = lax.axis_size(axis)
    with jax.named_scope(name):
        return lax.ppermute(values, axis, [(i, i ^ bit) for i in range(size)])


def bits_of(axis, low=1):
    size = lax.axis_size(axis)
    found = []
    while low < size:
        found.append((axis, low))
        low *= 2
    return found


def side(axis, bit):
    return (lax.axis_index(axis) // bit) % 2


PAIR = 2 * HEAD_DIM
CORE, OTHER_CORE, NONE, OUTER_TURN, INNER_TURN, ORDER = 2, 3, 4, 5, 6, 7
EXPERT_FLOPS = 2 * 10**9
ATTEND_FLOPS = 20 * 10**9
BACK_FLOPS = 300 * 10**9
ATTBACK_FLOPS = 50 * 10**9
FIRST_FLOPS = 300 * 10**9
HIDE = -1000000000.0
VMEM_LIMIT = 64 * 1024 * 1024


def dot(left, right):
    return jnp.dot(left, right, preferred_element_type=F32)


def dot_nt(left, right):
    return lax.dot_general(left, right, (((1,), (1,)), ((), ())), preferred_element_type=F32)


def norm_parts(values):
    center = values - jnp.mean(values, axis=-1, keepdims=True)
    scale = lax.rsqrt(jnp.mean(center * center, axis=-1, keepdims=True) + 1e-05)
    return center * scale, scale


def norm_back(grad, normed, scale):
    along = jnp.mean(grad * normed, axis=-1, keepdims=True)
    return scale * (grad - jnp.mean(grad, axis=-1, keepdims=True) - normed * along)


def shaped(shape, dtype):
    return jax.ShapeDtypeStruct(shape, dtype)


def call(kernel, operands, after=(), alias=(), prefetch=(), flops=1, **options):
    extra = [*alias, *after]
    anywhere = pl.BlockSpec(memory_space=pl.ANY)
    options["in_specs"] = [*options["in_specs"], *[anywhere] * len(extra)]
    first = len(prefetch) + len(operands)
    fixed, skip = len(operands), len(extra)

    def body(*refs):
        cut = len(prefetch) + fixed
        kernel(*refs[:cut], *refs[cut + skip :])

    if prefetch:
        specs = {name: options.pop(name) for name in ("grid", "in_specs", "out_specs")}
        specs["scratch_shapes"] = options.pop("scratch_shapes", ())
        options["grid_spec"] = pltpu.PrefetchScalarGridSpec(
            num_scalar_prefetch=len(prefetch), **specs
        )
    return pl.pallas_call(
        body,
        input_output_aliases={first + i: i for i in range(len(alias))},
        compiler_params=pltpu.CompilerParams(vmem_limit_bytes=VMEM_LIMIT),
        cost_estimate=pl.CostEstimate(flops=flops, bytes_accessed=1, transcendentals=0),
        **options,
    )(*prefetch, *operands, *extra)


def whole(shape):
    return pl.BlockSpec(shape, lambda *_: (0,) * len(shape))


def plain(kernel, operands, out_shape, name, after=(), scratch=(), flops=1):
    return call(
        kernel,
        operands,
        after=after,
        flops=flops,
        grid=(1,),
        in_specs=[whole(x.shape) for x in operands],
        out_specs=jax.tree.map(lambda s: whole(s.shape), out_shape),
        out_shape=out_shape,
        scratch_shapes=scratch,
        name=name,
    )


def project_kernel(which_ref, x_ref, gain_ref, weight_ref, first_ref, out_ref):
    normed, _ = norm_parts(x_ref[...].astype(F32))
    first = (normed * gain_ref[...]).astype(BF)
    first_ref[0] = first
    for c in range(3):
        out_ref[c, 0] = dot(first, weight_ref[c]).astype(BF)


def project(which, rows, gain, weight, earlier, after=(), tiles=1):
    count, width = rows.shape
    cols = weight.shape[2]
    size = count // tiles
    return call(
        project_kernel,
        [rows, gain, weight],
        after=after,
        alias=earlier,
        prefetch=[which],
        grid=(tiles,),
        in_specs=[
            pl.BlockSpec((size, width), lambda i, w: (i, 0)),
            whole((1, width)),
            whole((3, width, cols)),
        ],
        out_specs=[
            pl.BlockSpec((1, size, width), lambda i, w: (w[0], i, 0)),
            pl.BlockSpec((3, 1, size, cols), lambda i, w: (0, w[0], i, 0)),
        ],
        out_shape=[shaped((2, count, width), BF), shaped((3, 2, count, cols), BF)],
        name="project",
    )


def attend_kernel(
    which_ref, q_ref, kd_ref, vd_ref, kc_ref, vc_ref, pos_ref,
    pd_ref, pc_ref, rl_ref, context_ref, bias_d, bias_c,
):
    count = q_ref.shape[2]
    step = count // 2

    @pl.when(pl.program_id(0) == 0)
    def _():
        row = lax.broadcasted_iota(jnp.int32, (count, count), 0)
        col = lax.broadcasted_iota(jnp.int32, (count, count), 1)
        spread = jnp.broadcast_to(pos_ref[...].astype(F32), (8, count))
        start = row - jnp.transpose(spread)[:, :1].astype(jnp.int32)
        bias_d[...] = jnp.where((col <= row) & (col >= start), 0.0, HIDE)
        bias_c[...] = jnp.where(col >= start + count, 0.0, HIDE)

    lane = lax.broadcasted_iota(jnp.int32, (1, PAIR), 1) // HEAD_DIM

    def half(late):
        blocks = [(at, a) for at in (0, step) for a in (0, 1)]
        for a in (0, 1):
            pd_ref[0, a, :step, step:] = jnp.zeros((step, step), BF)
        scores = []
        for at, a in blocks:
            rows, keys = pl.ds(at, step), at + step
            mine = jnp.where(lane == a, q_ref[0, 0, rows, :] * 0.125, 0.0).astype(BF)
            s_d = dot_nt(mine, kd_ref[0, 0, :keys, :]) + bias_d[rows, :keys]
            s_c = dot_nt(mine, kc_ref[0, 0]) + bias_c[rows, :] if late else None
            scores.append((s_d, s_c))
        mixed, scale = {}, {}
        for (at, a), (s_d, s_c) in zip(blocks, scores):
            rows, keys = pl.ds(at, step), at + step
            top = jnp.max(s_d, axis=-1, keepdims=True)
            if late:
                top = jnp.maximum(top, jnp.max(s_c, axis=-1, keepdims=True))
            p_d = jnp.exp(s_d - top)
            total = jnp.sum(p_d, axis=-1, keepdims=True)
            p_d = p_d.astype(BF)
            pd_ref[0, a, rows, :keys] = p_d
            value = jnp.where(lane == a, vd_ref[0, 0, :keys, :], 0.0).astype(BF)
            mix = dot(p_d, value)
            if late:
                p_c = jnp.exp(s_c - top)
                total = total + jnp.sum(p_c, axis=-1, keepdims=True)
                p_c = p_c.astype(BF)
                pc_ref[0, a, rows, :] = p_c
                value = jnp.where(lane == a, vc_ref[0, 0], 0.0).astype(BF)
                mix = mix + dot(p_c, value)
            mixed[at, a], scale[at, a] = mix, 1.0 / total
        for at in (0, step):
            rows = pl.ds(at, step)
            inverse = jnp.where(lane == 0, scale[at, 0], scale[at, 1])
            rl_ref[0, rows, :] = inverse
            context_ref[rows, :] = ((mixed[at, 0] + mixed[at, 1]) * inverse).astype(BF)

    pl.when(which_ref[0] == 0)(lambda: half(False))
    pl.when(which_ref[0] == 1)(lambda: half(True))


def attend(which, projected, positions, earlier, after=(), flops=1):
    _, _, count, cols = projected.shape
    heads = cols // HEAD_DIM

    def block(part, other):
        if other:
            return pl.BlockSpec((1, 1, count, PAIR), lambda g, w: (part, 0, 0, g))
        return pl.BlockSpec((1, 1, count, PAIR), lambda g, w: (part, w[0], 0, g))

    score_spec = pl.BlockSpec((1, 2, count, count), lambda g, w: (w[0], g, 0, 0))
    return call(
        attend_kernel,
        [*[projected] * 5, positions],
        after=after,
        alias=earlier,
        prefetch=[which],
        flops=flops,
        grid=(cols // PAIR,),
        in_specs=[
            block(0, False),
            block(1, False),
            block(2, False),
            block(1, True),
            block(2, True),
            whole((1, count)),
        ],
        out_specs=[
            score_spec,
            score_spec,
            pl.BlockSpec((1, count, PAIR), lambda g, w: (w[0], 0, g)),
            pl.BlockSpec((count, PAIR), lambda g, w: (0, g)),
        ],
        scratch_shapes=[pltpu.VMEM((count, count), F32)] * 2,
        out_shape=[
            shaped((2, heads, count, count), BF),
            shaped((2, heads, count, count), BF),
            shaped((2, count, cols), F32),
            shaped((count, cols), BF),
        ],
        name="attend",
    )


def hidden_kernel(
    x_ref, own_ref, got_ref, own_weight_ref, got_weight_ref, gain_ref, slot_ref, hidden_ref, *out_refs
):
    attended = dot(own_ref[...], own_weight_ref[...]) + dot(got_ref[...], got_weight_ref[...])
    hidden = x_ref[...].astype(F32) + attended
    hidden_ref[...] = hidden
    normed, _ = norm_parts(hidden)
    second = (normed * gain_ref[...]).astype(BF)
    send_rows(second, slot_ref, out_refs)


def send_rows(rows, slot_ref, out_refs):
    capacity = out_refs[0].shape[0]
    for k, ref in enumerate(out_refs):
        slot = lax.broadcasted_iota(jnp.int32, (capacity, rows.shape[0]), 0) + k * capacity
        place = jnp.where(slot_ref[...] == slot, 1.0, 0.0).astype(BF)
        ref[...] = dot(place, rows).astype(BF)


def hidden_rows(x, own, got, own_weight, got_weight, gain, slot_row, experts, after=()):
    count, width = x.shape
    out = [shaped((count, width), F32)] + [shaped((count // 2, width), BF)] * experts
    return plain(
        hidden_kernel,
        [x, own, got, own_weight, got_weight, gain, slot_row],
        out,
        "hidden_rows",
        after,
    )


def send_kernel(rows_ref, slot_ref, weight_ref, out_ref, weight_out):
    send_rows(rows_ref[...], slot_ref, [out_ref.at[k] for k in range(out_ref.shape[0])])
    weight_out[...] = weight_ref[...]


def sent_rows(rows, slot_row, weight, experts, after=()):
    count, width = rows.shape
    out = [shaped((experts, count // 2, width), BF), shaped(weight.shape, BF)]
    return plain(send_kernel, [rows, slot_row, weight], out, "sent_rows", after)


def taken_rows(slot_ref, block_refs):
    count, capacity = slot_ref.shape[1], block_refs[0].shape[0]
    total = 0.0
    for k, ref in enumerate(block_refs):
        slot = lax.broadcasted_iota(jnp.int32, (capacity, count), 0) + k * capacity
        place = jnp.where(slot_ref[...] == slot, 1.0, 0.0).astype(BF)
        total = total + lax.dot_general(
            place, ref[...], (((0,), (0,)), ((), ())), preferred_element_type=F32
        )
    return total


def output_kernel(hidden_ref, slot_ref, *refs):
    blocks = [refs[0].at[k] for k in range(refs[0].shape[0])]
    refs[-1][...] = (hidden_ref[...] + taken_rows(slot_ref, blocks)).astype(BF)


def output_rows(hidden, slot_row, blocks, after=()):
    return plain(
        output_kernel,
        [hidden, slot_row, blocks],
        shaped(hidden.shape, BF),
        "output_rows",
        after,
        flops=FIRST_FLOPS,
    )


def second_kernel(cot_ref, hidden_ref, gain_ref, slot_ref, own_weight_ref, got_weight_ref, *refs):
    grad_ref, low_ref, gain_grad_ref, own_ref, send_ref = refs[-5:]
    second_grad = taken_rows(slot_ref, refs[:-5])
    normed, scale = norm_parts(hidden_ref[...])
    gain_grad_ref[...] = jnp.sum(second_grad * normed, axis=0, keepdims=True)
    grad = cot_ref[...].astype(F32) + norm_back(second_grad * gain_ref[...], normed, scale)
    grad_ref[...] = grad
    low = grad.astype(BF)
    low_ref[...] = low
    send_ref[...] = dot_nt(low, got_weight_ref[...]).astype(BF)
    own_ref[...] = dot_nt(low, own_weight_ref[...]).astype(BF)


def second_back(cot, hidden, gain, slot_row, own_weight, got_weight, blocks, after=()):
    count, width = hidden.shape
    part = shaped((count, own_weight.shape[0]), BF)
    out = [
        shaped((count, width), F32),
        shaped((count, width), BF),
        shaped((1, width), F32),
        part,
        part,
    ]
    return plain(
        second_kernel,
        [cot, hidden, gain, slot_row, own_weight, got_weight, *blocks],
        out,
        "second_back",
        after,
        flops=BACK_FLOPS,
    )


def output_weight_kernel(
    core_ref, own_ref, got_ref, low_ref, own_out, kept_out, sent_out, scratch
):
    def part(ref):
        return lax.dot_general(
            ref[...], low_ref[...], (((0,), (0,)), ((), ())), preferred_element_type=F32
        ).astype(BF)

    scratch[...] = part(got_ref)
    rows = kept_out.shape[0]
    for ref, half in ((kept_out, core_ref[0]), (sent_out, 1 - core_ref[0])):
        ref[...] = scratch[pl.ds(pl.multiple_of(half * rows, rows), rows), :]
    own_out[...] = part(own_ref)


def output_weight_parts(core, own, got, low, after=()):
    cols, width = own.shape[1], low.shape[1]
    part = shaped((cols // 2, width), BF)
    out = [shaped((cols, width), BF), part, part]
    return call(
        output_weight_kernel,
        [own, got, low],
        after=after,
        prefetch=[core],
        grid=(1,),
        in_specs=[whole(x.shape) for x in (own, got, low)],
        out_specs=[whole(o.shape) for o in out],
        out_shape=out,
        scratch_shapes=[pltpu.VMEM((cols, width), BF)],
        name="output_weight_parts",
    )


def first_kernel(x_ref, gain_ref, hidden_grad_ref, own_ref, theirs_ref, out_ref):
    grad = (own_ref[...] + theirs_ref[...].astype(F32)) * gain_ref[...]
    normed, scale = norm_parts(x_ref[...].astype(F32))
    out_ref[...] = hidden_grad_ref[...] + norm_back(grad, normed, scale)


def first_back(x, gain, hidden_grad, own, theirs, after=()):
    return plain(
        first_kernel,
        [x, gain, hidden_grad, own, theirs],
        shaped(x.shape, F32),
        "first_back",
        after,
    )


def fill(target, refs):
    rows = refs[0].shape[0]
    for i, ref in enumerate(refs):
        target[i * rows : (i + 1) * rows] = ref[...]


def expert_kernel(count, sub, place_ref, *refs):
    x_refs, cot_refs, refs = refs[:count], refs[count : 2 * count], refs[2 * count :]
    inner_ref, outer_ref, act_ref, pre_ref, out_ref, *grad_refs, x, cot, grad_acc, out_acc = refs
    at = pl.program_id(0)
    last = pl.num_programs(0) - count
    size = out_ref.shape[1]

    @pl.when(at > last)
    def _():
        rows = pl.ds(pl.multiple_of((at - last) * size, size), size)
        out_ref[0] = out_acc[rows, :].astype(BF)

    pl.when(at <= last)(
        lambda: expert_step(
            count, sub, x_refs, cot_refs, inner_ref, outer_ref, act_ref, pre_ref, out_ref,
            grad_refs, x, cot, grad_acc, out_acc, at, last,
        )
    )


def expert_step(
    count, sub, x_refs, cot_refs, inner_ref, outer_ref, act_ref, pre_ref, out_ref, grad_refs,
    x, cot, grad_acc, out_acc, at, last,
):

    @pl.when(at == 0)
    def _():
        fill(x, x_refs)
        fill(cot, [ref.at[0] for ref in cot_refs])
        grad_acc[...] = jnp.zeros_like(grad_acc)
        out_acc[...] = jnp.zeros_like(out_acc)

    def front(i):
        cols = slice(i * sub, (i + 1) * sub)
        return dot(x[...], inner_ref[:, cols]), dot_nt(cot[...], outer_ref[cols, :])

    parts = inner_ref.shape[1] // sub
    now = front(0)
    for i in range(parts):
        later = front(i + 1) if i + 1 < parts else None
        value, grad = now
        square = value * value
        half = 0.5 + 0.5 * jnp.tanh(
            value * (0.7978845608028654 + 0.035677408136300125 * square)
        )
        act = value * half
        slope = half + act * (1.0 - half) * (1.5957691216057308 + 0.21406444881780074 * square)
        cols = slice(i * sub, (i + 1) * sub)
        act_ref[:, cols] = act.astype(BF)
        pre_ref[:, cols] = (grad * slope).astype(BF)
        now = later
    grad_acc[...] += dot_nt(pre_ref[...], inner_ref[...])
    out_acc[...] += dot(act_ref[...], outer_ref[...])

    @pl.when(at == last)
    def _():
        size = out_ref.shape[1]
        out_ref[0] = out_acc[:size].astype(BF)
        for i, ref in enumerate(grad_refs):
            ref[...] = grad_acc[i * size : (i + 1) * size].astype(BF)


def expert(place, index, blocks, cot, inner, outer, earlier, after=(), tile=1536, sub=256):
    count, width = blocks[0].shape
    size, units = len(blocks), inner.shape[1]
    total = count * cot.shape[0]
    tiles = units // tile

    def held(j):
        return jnp.minimum(j, tiles - 1)

    wide = pl.BlockSpec((count * size, tile), lambda j, p: (index // size, held(j)))
    out = pl.BlockSpec(
        (1, count, width), lambda j, p: (p[jnp.maximum(j - tiles + 1, 0)], 0, 0)
    )

    def placed(i):
        return pl.BlockSpec((1, count, width), lambda j, p: (p[i], 0, 0))

    return call(
        functools.partial(expert_kernel, size, sub),
        [*blocks, *[cot] * size, inner, outer],
        after=after,
        flops=EXPERT_FLOPS,
        alias=earlier,
        prefetch=[place],
        grid=(tiles + size - 1,),
        in_specs=[whole((count, width))] * size
        + [placed(i) for i in range(size)]
        + [
            pl.BlockSpec((width, tile), lambda j, p: (0, held(j))),
            pl.BlockSpec((tile, width), lambda j, p: (held(j), 0)),
        ],
        out_specs=[wide, wide, out] + [whole((count, width))] * size,
        out_shape=[shaped((total, units), BF)] * 2
        + [shaped(cot.shape, BF)]
        + [shaped((count, width), BF)] * size,
        scratch_shapes=[pltpu.VMEM((count * size, width), BF)] * 2
        + [pltpu.VMEM((count * size, width), F32)] * 2,
        name="expert",
    )


def weight_kernel(is_outer, count, added, info_ref, wide_ref, *refs):
    row_count = 1 if is_outer else count
    row_refs, refs = refs[:row_count], refs[row_count:]
    if is_outer:
        row_refs = [row_refs[0].at[info_ref[ORDER + i]] for i in range(count)]
    got_ref = refs[0] if added else None
    *out_refs, rows = refs[1:] if added else refs
    at = pl.program_id(0)
    pl.when(at == 0)(lambda: fill(rows, row_refs))

    def put(out_ref):
        sides = (wide_ref[...], rows[...]) if is_outer else (rows[...], wide_ref[...])
        part = lax.dot_general(*sides, (((0,), (0,)), ((), ())), preferred_element_type=F32)
        if added:
            part = part + got_ref[...].astype(F32)
        out_ref[...] = part.astype(BF)

    if added:
        for i, out_ref in enumerate(out_refs):
            pl.when(at == i)(functools.partial(put, out_ref))
    else:
        put(out_refs[0])


def weight_part(info, is_outer, half, turn, blocks, wide, got=None, after=()):
    total, units = wide.shape
    width, added, tile = blocks[0].shape[1], got is not None, units // 4
    count = len(blocks) if not is_outer else blocks.shape[0]
    if is_outer:
        row_specs, blocks = [whole(blocks.shape)], [blocks]
    else:
        row_specs = [whole(block.shape) for block in blocks]

    def at(j):
        return (j, 0) if is_outer else (0, j)

    def place(j, w):
        return (w[turn] + j) % 2

    def shape(units):
        return (units, width) if is_outer else (width, units)

    block = pl.BlockSpec(shape(tile), lambda j, w: at(place(j, w)))
    if added:
        out, out_specs = [shaped(shape(tile), BF)] * 2, [whole(shape(tile))] * 2
    else:
        out, out_specs = [shaped(shape(2 * tile), BF)], [block]
    return call(
        functools.partial(weight_kernel, is_outer, count, added),
        [wide, *blocks] + ([got] if added else []),
        after=after,
        prefetch=[info],
        grid=(2,),
        in_specs=[pl.BlockSpec((total, tile), lambda j, w: (0, w[half] * 2 + place(j, w)))]
        + row_specs
        + ([block] if added else []),
        out_specs=out_specs,
        out_shape=out,
        scratch_shapes=[pltpu.VMEM((total, width), BF)],
        name="weight_part",
    )


def assemble_kernel(counts, info_ref, *refs):
    piece_refs, out_refs = refs[: sum(counts)], refs[sum(counts) :]
    targets = [out for out, count in zip(out_refs, counts) for _ in range(count)]
    for i, (ref, out_ref) in enumerate(zip(piece_refs, targets)):

        @pl.when(pl.program_id(0) == i)
        def _(ref=ref, out_ref=out_ref):
            out_ref[...] = ref[...].astype(F32)


def assemble(info, start, groups, shapes, earlier, after=()):
    counts = [len(pieces) for pieces in groups]
    pieces = [piece for group in groups for piece in group]
    size = pieces[0].shape

    def spec(first, count):
        def at(i, t):
            held = start + 2 * jnp.clip(i, first, first + count - 1)
            return t[held], t[held + 1]

        return pl.BlockSpec(size, at)

    firsts = [sum(counts[:i]) for i in range(len(counts))]
    return call(
        functools.partial(assemble_kernel, counts),
        pieces,
        after=after,
        alias=earlier,
        prefetch=[info],
        grid=(len(pieces),),
        in_specs=[whole(size)] * len(pieces),
        out_specs=[spec(first, count) for first, count in zip(firsts, counts)],
        out_shape=[shaped(shape, F32) for shape in shapes],
        name="assemble",
    )


def add_kernel(kept_ref, got_ref, out_ref):
    out_ref[...] = (kept_ref[...].astype(F32) + got_ref[...].astype(F32)).astype(BF)


def add(kept, got):
    return plain(add_kernel, [kept, got], shaped(kept.shape, BF), "add")


def gather_sum_kernel(kept_ref, got_ref, more_ref, out_ref, tail_ref):
    rows, more = out_ref.shape[0], more_ref.shape[0]
    first = rows - more
    out_ref[:first] = (kept_ref[:first].astype(F32) + got_ref[:first].astype(F32)).astype(BF)
    last = kept_ref[first:rows].astype(F32) + got_ref[first:rows].astype(F32)
    out_ref[first:] = (last + more_ref[...].astype(F32)).astype(BF)
    tail_ref[...] = (kept_ref[rows:].astype(F32) + got_ref[rows:].astype(F32)).astype(BF)


def gather_sum(kept, got, more, rows, after=()):
    lines, width = kept.shape
    out = [shaped((rows, width), BF), shaped((lines - rows, width), BF)]
    return plain(gather_sum_kernel, [kept, got, more], out, "gather_sum", after)


def adds_kernel(start, count, cuts, whole_sum, info_ref, *refs):
    in_refs, out_refs = refs[: 2 * count], refs[2 * count :]
    for i in range(count):
        kept_ref, got_ref = in_refs[2 * i : 2 * i + 2]
        for j in range(cuts):
            ref = out_refs[cuts * i + j]
            rows = ref.shape[0]
            at = 0 if whole_sum else info_ref[start + cuts * i + j]
            cut = pl.ds(pl.multiple_of(at * rows, rows), rows)
            ref[...] = (kept_ref[cut, :].astype(F32) + got_ref[cut, :].astype(F32)).astype(BF)


def adds(info, start, pairs, cuts, whole_sum=False, after=()):
    out = [
        shaped((kept.shape[0] // (1 if whole_sum else cuts), kept.shape[1]), BF)
        for kept, _ in pairs
        for _ in range(cuts)
    ]
    operands = [x for pair in pairs for x in pair]
    parts = call(
        functools.partial(adds_kernel, start, len(pairs), cuts, whole_sum),
        operands,
        after=after,
        prefetch=[info],
        grid=(1,),
        in_specs=[whole(x.shape) for x in operands],
        out_specs=[whole(o.shape) for o in out],
        out_shape=out,
        name="adds",
    )
    return [parts[cuts * i : cuts * (i + 1)] for i in range(len(pairs))]


def piece_places(steps, order):
    weights = {step: 1 << (len(steps) - 1 - i) for i, step in enumerate(steps)}
    place = sum(side(*step) * weight for step, weight in weights.items())
    places, newest = [place], [(0, place)]
    while newest:
        newest = [
            (i + 1, at + weights[order[i]] * (1 - 2 * side(*order[i])))
            for first, at in newest
            for i in range(first, len(order))
        ]
        places += [at for _, at in newest]
    return places


def gather_pieces(own, steps, order, flops, after):
    pieces, newest = [own], [(0, own)]
    while newest:
        found = [
            (i + 1, swap(piece, *order[i], "piece"))
            for first, piece in newest
            for i in range(first, len(order))
        ]
        if len(pieces) == 1:
            held = touch([piece for _, piece in found], after, flops=flops)
            found = [(first, piece) for (first, _), piece in zip(found, held)]
        pieces += [piece for _, piece in found]
        newest = found
    return list(zip(piece_places(steps, order), pieces))


def total_kernel(in_ref, tail_ref, got_ref, out_ref):
    count, rows = in_ref.shape[:2]
    value = sum(in_ref[i].astype(F32) for i in range(count)).astype(BF)
    tail = sum(ref[i : i + 1].astype(F32) for ref in (tail_ref, got_ref) for i in (0, 1))
    high = tail.astype(BF).astype(F32)
    line = lax.broadcasted_iota(jnp.int32, tail_ref.shape, 0)
    tail = jnp.where(line == 0, high, jnp.where(line == 1, tail - high, 0.0)).astype(BF)
    for i in range(count):
        out_ref[i, :rows] = value
        out_ref[i, rows:] = tail


def total(blocks, tail, got, after=()):
    count, rows, width = blocks.shape
    out = shaped((count, rows + tail.shape[0], width), BF)
    return plain(total_kernel, [blocks, tail, got], out, "total", after)


def halves(step):
    mine = side(*step)
    return [1 - mine, mine]


def touch_kernel(*out_refs):
    pass


def touch(values, after, flops=1):
    return call(
        touch_kernel,
        [],
        after=after,
        alias=values,
        flops=flops,
        in_specs=[],
        out_specs=[pl.BlockSpec(memory_space=pl.ANY)] * len(values),
        out_shape=[shaped(x.shape, x.dtype) for x in values],
        name="touch",
    )


def back_kernel(
    at_ref, own_ref, other_ref, q_ref, k_ref, v_ref, pd_ref, pc_ref, own_context_ref,
    other_context_ref, rl_ref, first_ref, wp_ref, gain_ref, second_ref, own_output_ref,
    sent_ref, kept_ref, mine_ref, theirs_ref,
    acc, scaled, through, key_acc, value_acc, queries, weights, scores,
):
    group = pl.program_id(0)
    count = own_ref.shape[0]
    step = count // 2
    me, core = at_ref[0], at_ref[CORE]
    lane = lax.broadcasted_iota(jnp.int32, (1, PAIR), 1) // HEAD_DIM

    for ref, context, at in (
        (own_ref, own_context_ref, me),
        (other_ref, other_context_ref, 1 - me),
    ):
        grad = ref[...].astype(F32) * rl_ref[at]
        scaled[at] = grad
        through[at] = grad.astype(BF).astype(F32) * context[...].astype(F32)
    @pl.when(group == 0)
    def _():
        for h in (0, 1):
            for a in (0, 1):
                scores[h, a, :step, step:] = jnp.zeros((step, step), BF)

    for h in (0, 1):
        for at in (0, step):
            rows = pl.ds(at, step)
            low = scaled[h, rows, :].astype(BF)
            query = 0.0
            for a in (0, 1):
                mine = jnp.where(lane == a, low, 0.0).astype(BF)
                along = jnp.sum(
                    jnp.where(lane == a, through[h, rows, :], 0.0), axis=-1, keepdims=True
                )
                parts = [(pd_ref, h, h, at + step)]
                if h:
                    parts.append((pc_ref, 0, 2, count))
                for p_ref, p_at, to, keys in parts:
                    source = 0 if to == 2 else h
                    prob_grad = dot_nt(mine, v_ref[0, source, :keys, :])
                    p = p_ref[p_at, a, rows, :keys]
                    score = (p.astype(F32) * (prob_grad - along)).astype(BF)
                    scores[to, a, rows, :keys] = score
                    k = jnp.where(lane == a, k_ref[0, source, :keys, :], 0.0).astype(BF)
                    query = query + dot(score, k)
            queries[pl.ds(h * count + at, step), :] = query * 0.125
    low_t = [jnp.transpose(scaled[h]).astype(BF) for h in (0, 1)]
    q_t = [jnp.transpose(q_ref[0, h].astype(F32)).astype(BF) for h in (0, 1)]
    for a in (0, 1):
        line = slice(a * HEAD_DIM, (a + 1) * HEAD_DIM)
        key_acc[line, :count] = dot(q_t[0][line], scores[0, a]) + dot(q_t[1][line], scores[2, a])
        key_acc[line, count:] = dot(q_t[1][line], scores[1, a])
        value_acc[line, :count] = dot(low_t[0][line], pd_ref[0, a]) + dot(
            low_t[1][line], pc_ref[0, a]
        )
        value_acc[line, count:] = dot(low_t[1][line], pd_ref[1, a])

    query = queries[...]
    key_t = key_acc[...] * 0.125
    value_t = value_acc[...]
    both = jnp.concatenate(
        [query.astype(BF), jnp.transpose(key_t).astype(BF), jnp.transpose(value_t).astype(BF)],
        axis=1,
    )
    both_t = jnp.concatenate(
        [jnp.transpose(query).astype(BF), key_t.astype(BF), value_t.astype(BF)], axis=0
    )
    first = jnp.concatenate([first_ref[0], first_ref[1]], axis=0)
    weights[...] = dot(both_t, first)
    size = 3 * PAIR // 2
    groups = pl.num_programs(0)
    here = pl.ds(pl.multiple_of(group * size, size), size)
    for ref, half in ((sent_ref, 1 - core), (kept_ref, core)):
        ref[here, :] = weights[pl.ds(pl.multiple_of(half * size, size), size), :].astype(BF)
    weight = jnp.concatenate([wp_ref[0], wp_ref[1], wp_ref[2]], axis=1)
    added = dot_nt(both, weight)

    @pl.when(group == 0)
    def _():
        for h in (0, 1):
            acc[h] = added[h * count : (h + 1) * count]

    @pl.when(group > 0)
    def _():
        for h in (0, 1):
            acc[h] += added[h * count : (h + 1) * count]

    @pl.when(group == groups - 1)
    def _():
        mine_ref[...] = acc[me]
        theirs_ref[...] = acc[1 - me].astype(BF)
        gain = 0.0
        for h in (0, 1):
            gain = gain + jnp.sum(acc[h] * first_ref[h].astype(F32), axis=0, keepdims=True)
        gain = gain / gain_ref[...]
        part = own_output_ref.shape[0] // 2
        at = groups * size
        end = at + part
        for ref, half in ((sent_ref, 1 - core), (kept_ref, core)):
            cut = pl.ds(pl.multiple_of(half * part, part), part)
            ref[at:end, :] = own_output_ref[cut, :]
            value = jnp.where(half == 0, gain, second_ref[...])
            high = value.astype(BF).astype(F32)
            line = lax.broadcasted_iota(jnp.int32, (ref.shape[0] - end, value.shape[1]), 0)
            tail = jnp.where(line == 0, high, jnp.where(line == 1, value - high, 0.0))
            ref[end:, :] = tail.astype(BF)


def attend_back(
    at, own, other, projected, p_diag, p_cross, own_context, other_context, inverse, first, weight,
    gain, second, own_output, lines, after=(),
):
    _, _, count, cols = projected.shape
    width = first.shape[2]
    rows = whole((count, width))
    pair = pl.BlockSpec((count, PAIR), lambda g, w: (0, g))

    def block(part):
        return pl.BlockSpec((1, 2, count, PAIR), lambda g, w: (part, 0, 0, g))

    sent = shaped((lines, width), BF)
    out = [sent, sent, shaped((count, width), F32), shaped((count, width), BF)]
    return call(
        back_kernel,
        [
            own, other, projected, projected, projected, p_diag, p_cross, own_context,
            other_context, inverse, first, weight, gain, second, own_output,
        ],
        after=after,
        flops=ATTBACK_FLOPS,
        prefetch=[at],
        grid=(cols // PAIR,),
        in_specs=[
            pair,
            pair,
            block(0),
            block(1),
            block(2),
            pl.BlockSpec((2, 2, count, count), lambda g, w: (0, g, 0, 0)),
            pl.BlockSpec((1, 2, count, count), lambda g, w: (1, g, 0, 0)),
            pair,
            pair,
            pl.BlockSpec((2, count, PAIR), lambda g, w: (0, 0, g)),
            whole((2, count, width)),
            pl.BlockSpec((3, width, PAIR), lambda g, w: (0, 0, g)),
            whole((1, width)),
            whole((1, width)),
            whole((cols, width)),
        ],
        out_specs=[whole(o.shape) for o in out],
        scratch_shapes=[
            pltpu.VMEM((2, count, width), F32),
            pltpu.VMEM((2, count, PAIR), F32),
            pltpu.VMEM((2, count, PAIR), F32),
            pltpu.VMEM((PAIR, 2 * count), F32),
            pltpu.VMEM((PAIR, 2 * count), F32),
            pltpu.VMEM((2 * count, PAIR), F32),
            pltpu.VMEM((3 * PAIR, width), F32),
            pltpu.VMEM((3, 2, count, count), BF),
        ],
        out_shape=out,
        name="attend_back",
    )


def weight_outputs_kernel(rows, core_ref, kept_ref, got_ref, project_ref, output_ref, gains_ref):
    group, groups = pl.program_id(0), pl.num_programs(0)
    size = 3 * PAIR // 2

    def halves_of(cut, which):
        kept, got = [
            jnp.concatenate([ref[block, cut, :] for block in which], axis=0).astype(F32)
            for ref in (kept_ref, got_ref)
        ]
        low = jnp.where(core_ref[0] == 0, kept, got)
        return low, jnp.where(core_ref[0] == 0, got, kept)

    body, blocks = slice(0, rows), size // rows
    low, high = halves_of(body, [group * blocks + i for i in range(blocks)])
    flat = jnp.transpose(jnp.concatenate([low, high], axis=0))
    for c in range(3):
        project_ref[c] = flat[:, c * PAIR : (c + 1) * PAIR]

    @pl.when(group == groups - 1)
    def _():
        part, count = output_ref.shape[0] // 2, kept_ref.shape[0]
        first = groups * size // rows
        output_ref[:part], output_ref[part:] = halves_of(body, range(first, count))
        tails = halves_of(slice(rows, rows + 16), range(count))
        for i, tail in enumerate(tails):
            gains_ref[i : i + 1] = sum(
                tail[16 * b : 16 * b + 1] + tail[16 * b + 1 : 16 * b + 2] for b in range(count)
            )


def weight_outputs(core, kept, got, cols, after=()):
    _, rows, width = kept.shape
    return call(
        functools.partial(weight_outputs_kernel, rows - 16),
        [kept, got],
        after=after,
        prefetch=[core],
        grid=(cols // PAIR,),
        in_specs=[whole(kept.shape)] * 2,
        out_specs=[
            pl.BlockSpec((3, width, PAIR), lambda g, w: (0, 0, g)),
            whole((cols, width)),
            whole((2, width)),
        ],
        out_shape=[shaped((3, width, cols), F32), shaped((cols, width), F32), shaped((2, width), F32)],
        name="weight_outputs",
    )


def on_device(
    block_input,
    output_cotangent,
    token_ids,
    positions,
    hash_table,
    first_gain,
    second_gain,
    project_weight,
    output_weight,
    expert_inner,
    expert_outer,
):
    tok_rows, model_width = block_input.shape
    local_cols = output_weight.shape[0]
    expert_count = lax.axis_size("expert")
    capacity = tok_rows // 2
    inner_weight = expert_inner[0]
    outer_weight = expert_outer[0]
    my_head = lax.axis_index("head")
    my_expert = lax.axis_index("expert")
    core = lax.axis_index("core")
    turns = bits_of("x") + bits_of("head")
    outer_steps, inner_steps = turns, turns[::-1]
    order = [my_expert ^ k for k in range(expert_count)]

    early = len(turns) + 1
    entries = [
        my_head, 1 - my_head, core, 1 - core, 0 * core,
        1 - side(*outer_steps[0]), 1 - side(*inner_steps[0]), *order,
    ]
    adds_at = [len(entries) + 4 * i for i in range(len(turns) - 1)]
    for i in range(1, len(turns)):
        entries += [*halves(outer_steps[i]), *halves(inner_steps[i])]
    half = 1 << (len(turns) - 1)

    def placed(place, which, is_outer):
        if is_outer:
            return [which * 2 * half + place, 0 * place]
        return [place % half, which * 2 + place // half]

    piece_at = []
    for chosen in (slice(early), slice(early, None)):
        for steps, is_outer in ((outer_steps, True), (inner_steps, False)):
            piece_at.append(len(entries))
            for which in (core, 1 - core):
                for place in piece_places(steps, steps[::-1])[chosen]:
                    entries += placed(place, which, is_outer)
    info = jnp.stack(entries).astype(jnp.int32)
    own_at, core_at = my_head.reshape(1).astype(jnp.int32), core.reshape(1).astype(jnp.int32)
    other_at = 1 - own_at
    first_gain = first_gain.reshape(1, model_width)
    second_gain = second_gain.reshape(1, model_width)

    other_input = swap(block_input, "head", 1, "rows")
    other_pos = swap(positions, "head", 1, "positions")

    chosen = jnp.take(hash_table, token_ids)
    relative = chosen ^ my_expert
    one_hot = relative[:, None] == jnp.arange(expert_count, dtype=jnp.int32)[None, :]
    rank_table = jnp.cumsum(one_hot.astype(jnp.int32), axis=0) - 1
    slot_index = relative * capacity + jnp.sum(jnp.where(one_hot, rank_table, 0), axis=1)
    slot_row = slot_index[None, :]
    absolute = slot_index + (chosen - relative) * capacity

    def exchange(blocks, name, first=0):
        return [
            swap(block, "expert", k, f"{name}{k}") if k else block
            for k, block in enumerate(blocks, first)
        ]

    def exchange_all(blocks):
        return lax.all_to_all(blocks, "expert", split_axis=0, concat_axis=0, tiled=True)

    done = project(own_at, block_input, first_gain, project_weight, [])
    sent, weight_sent = sent_rows(
        output_cotangent, absolute[None, :], output_weight, expert_count, after=[done[0], other_pos]
    )
    grad_blocks = exchange_all(sent)
    first_low, projected = project(other_at, other_input, first_gain, project_weight, done)
    other_weight = swap(weight_sent, "head", 1, "output_weight")
    *done, other_context = attend(other_at, projected, other_pos[None, :], [])
    got_context = swap(other_context, "head", 1, "context")
    p_diag, p_cross, inverse, own_context = attend(
        own_at,
        projected,
        positions[None, :],
        done,
        after=[other_weight],
        flops=ATTEND_FLOPS,
    )
    hidden, *outgoing = hidden_rows(
        block_input,
        own_context,
        got_context,
        output_weight,
        other_weight,
        second_gain,
        slot_row,
        expert_count,
    )

    row_blocks = exchange(outgoing, "dispatch")
    done, returned, at = [], [], 0
    while at < expert_count:
        size = 1
        parts = expert(
            order[at].reshape(1).astype(jnp.int32), at, row_blocks[at : at + size], grad_blocks if at else sent, inner_weight,
            outer_weight, done,
        )
        done, grads = parts[:3], parts[3:]
        returned += exchange(grads, "return", at)
        at += size
    activated, pre_grad, produced = done

    (outer_sent,) = weight_part(info, True, OTHER_CORE, NONE, grad_blocks, activated, after=grads)
    outer_got = swap(outer_sent, "core", 1, "outer_core")
    (inner_sent,) = weight_part(
        info, False, OTHER_CORE, NONE, row_blocks, pre_grad, after=[outer_sent]
    )
    inner_got = swap(inner_sent, "core", 1, "inner_core")
    token = touch([jnp.zeros((8, 128), F32)], [inner_sent], flops=BACK_FLOPS)
    outer_parts = weight_part(
        info, True, CORE, OUTER_TURN, grad_blocks, activated, outer_got, after=token
    )
    inner_parts = weight_part(
        info, False, CORE, INNER_TURN, row_blocks, pre_grad, inner_got, after=[outer_parts[0]]
    )

    hidden_grad, hidden_low, second_gain_part, own_grad, grad_sent = second_back(
        output_cotangent,
        hidden,
        second_gain,
        slot_row,
        output_weight,
        other_weight,
        returned,
        after=[inner_parts[0]],
    )
    other_grad = swap(grad_sent, "head", 1, "context_grad")
    def pairs_of(outer, inner, i):
        return [
            (outer[1], swap(outer[0], *outer_steps[i], f"outer{i}")),
            (inner[1], swap(inner[0], *inner_steps[i], f"inner{i}")),
        ]

    own_output, output_kept, output_sent = output_weight_parts(
        core_at, own_context, got_context, hidden_low, after=[grad_sent]
    )
    output_sent = add(output_kept, swap(output_sent, "core", 1, "output_core"))
    combined = exchange_all(touch([produced], [output_sent])[0])
    got_output = swap(output_sent, "head", 1, "output_grad")

    groups = local_cols // PAIR
    end = 2 * local_cols
    lines = end + 16
    sent, kept, mine, theirs = attend_back(
        info, own_grad, other_grad, projected, p_diag,
        p_cross, own_context, other_context, inverse, first_low, project_weight, first_gain,
        second_gain_part, own_output, lines, after=[inner_parts[0]],
    )
    at = 3 * local_cols // 2
    for i in range(len(turns) - 1):
        outer_parts, inner_parts = adds(
            info, adds_at[i], pairs_of(outer_parts, inner_parts, i), 2, after=[kept]
        )
    more = touch([got_output], outer_parts, flops=BACK_FLOPS)
    got = swap(sent, "core", 1, "weight")
    summed, tail = gather_sum(kept, got, more[0], end, after=more)
    crowd = ("x", "expert")
    summed = summed.reshape(-1, end // lax.axis_size(crowd), model_width)
    arrived = lax.all_to_all(summed, crowd, split_axis=0, concat_axis=0, tiled=True)
    block_output = output_rows(hidden, absolute[None, :], combined, after=[summed])
    got_tail = swap(tail, "head", 1, "gains")
    theirs = swap(touch([theirs], [got_tail])[0], "head", 1, "theirs")
    (outer_own, outer_copy), (inner_own, inner_copy) = adds(
        info, 0, pairs_of(outer_parts, inner_parts, -1), 2, True, after=[block_output, got_tail]
    )
    arrived = total(
        arrived, tail, got_tail, after=[outer_own, inner_own]
    )
    input_grad = first_back(
        block_input, first_gain, hidden_grad, mine, theirs, after=[arrived]
    )
    outer_pieces = gather_pieces(outer_own, outer_steps, outer_steps[::-1], BACK_FLOPS, [input_grad])
    inner_pieces = gather_pieces(inner_own, inner_steps, inner_steps[::-1], 1, [input_grad])
    summed = lax.all_to_all(arrived, crowd, split_axis=0, concat_axis=0, tiled=True)

    def core_swaps(pieces):
        return [(at, swap(piece, "core", 1, "piece_core")) for at, piece in pieces]

    others = []
    for pieces, own in ((outer_pieces, outer_copy), (inner_pieces, inner_copy)):
        (held,) = touch([own], [arrived])
        others.append(core_swaps([(pieces[0][0], held), *pieces[1:early]]))
    shapes = [outer_weight.shape, inner_weight.shape]
    totals = []
    for i, pieces in enumerate((outer_pieces, inner_pieces)):
        chosen = [piece for _, piece in pieces[:early] + others[i]]
        totals += assemble(
            info, piece_at[i], [chosen], shapes[i : i + 1], [], after=[arrived] + totals[-1:]
        )
    late = []
    for pieces in (outer_pieces, inner_pieces):
        held = touch([piece for _, piece in pieces[early:]], totals)
        late.append([(at, piece) for (at, _), piece in zip(pieces[early:], held)])
    late_others = [core_swaps(pieces) for pieces in late]
    (kept,) = touch([summed], [pieces[0][1] for pieces in late])
    got = swap(kept, "core", 1, "weight_back")
    project_grad, output_weight_grad, gains = weight_outputs(core_at, kept, got, local_cols)
    chosen = [
        [piece for _, piece in own + other] for own, other in zip(late, late_others)
    ]
    outer_total, inner_total = assemble(
        info, piece_at[2], chosen, shapes, totals, after=[project_grad]
    )
    return (
        block_output,
        input_grad,
        gains[0],
        gains[1],
        project_grad,
        output_weight_grad,
        inner_total[None],
        outer_total[None],
    )


def solution(mesh):
    devices = mesh.devices
    mesh = Mesh(
        devices.reshape(devices.shape[0] // 2, 2, *devices.shape[1:]), ("x", "core", "expert", "head")
    )
    in_specs = (
        P(("x", "core", "expert", "head"), None),
        P(("x", "core", "expert", "head"), None),
        P(("x", "core", "expert", "head")),
        P(("x", "core", "expert", "head")),
        P(),
        P(),
        P(),
        P(None, None, "head"),
        P("head", None),
        P("expert", None, None),
        P("expert", None, None),
    )
    out_specs = (
        P(("x", "core", "expert", "head"), None),
        P(("x", "core", "expert", "head"), None),
        P(),
        P(),
        P(None, None, "head"),
        P("head", None),
        P("expert", None, None),
        P("expert", None, None),
    )
    return jax.shard_map(
        on_device, mesh=mesh, in_specs=in_specs, out_specs=out_specs, check_vma=False
    )
```

```python
import functools

import jax
import jax.numpy as jnp
from jax import lax
from jax.experimental import pallas as pl
from jax.experimental.pallas import tpu as pltpu
from jax.sharding import Mesh
from jax.sharding import PartitionSpec as P

HEAD_DIM = 64
BF = jnp.bfloat16
F32 = jnp.float32


def swap(values, axis, bit, name):
    size = lax.axis_size(axis)
    with jax.named_scope(name):
        return lax.ppermute(values, axis, [(i, i ^ bit) for i in range(size)])


def bits_of(axis, low=1):
    size = lax.axis_size(axis)
    found = []
    while low < size:
        found.append((axis, low))
        low *= 2
    return found


def side(axis, bit):
    return (lax.axis_index(axis) // bit) % 2


PAIR = 2 * HEAD_DIM
CORE, OTHER_CORE, NONE, OUTER_TURN, INNER_TURN, ORDER = 2, 3, 4, 5, 6, 7
EXPERT_FLOPS = 2 * 10**9
ATTEND_FLOPS = 20 * 10**9
BACK_FLOPS = 300 * 10**9
ATTBACK_FLOPS = 50 * 10**9
FIRST_FLOPS = 300 * 10**9
HIDE = -1000000000.0
VMEM_LIMIT = 64 * 1024 * 1024


def dot(left, right):
    return jnp.dot(left, right, preferred_element_type=F32)


def dot_nt(left, right):
    return lax.dot_general(left, right, (((1,), (1,)), ((), ())), preferred_element_type=F32)


def row_of(ref):
    return ref[...].reshape(1, ref.shape[0])


def norm_parts(values):
    center = values - jnp.mean(values, axis=-1, keepdims=True)
    scale = lax.rsqrt(jnp.mean(center * center, axis=-1, keepdims=True) + 1e-05)
    return center * scale, scale


def norm_back(grad, normed, scale):
    along = jnp.mean(grad * normed, axis=-1, keepdims=True)
    return scale * (grad - jnp.mean(grad, axis=-1, keepdims=True) - normed * along)


def shaped(shape, dtype):
    return jax.ShapeDtypeStruct(shape, dtype)


def call(kernel, operands, after=(), alias=(), prefetch=(), flops=1, **options):
    extra = [*alias, *after]
    anywhere = pl.BlockSpec(memory_space=pl.ANY)
    options["in_specs"] = [*options["in_specs"], *[anywhere] * len(extra)]
    first = len(prefetch) + len(operands)
    fixed, skip = len(operands), len(extra)

    def body(*refs):
        cut = len(prefetch) + fixed
        kernel(*refs[:cut], *refs[cut + skip :])

    if prefetch:
        specs = {name: options.pop(name) for name in ("grid", "in_specs", "out_specs")}
        specs["scratch_shapes"] = options.pop("scratch_shapes", ())
        options["grid_spec"] = pltpu.PrefetchScalarGridSpec(
            num_scalar_prefetch=len(prefetch), **specs
        )
    return pl.pallas_call(
        body,
        input_output_aliases={first + i: i for i in range(len(alias))},
        compiler_params=pltpu.CompilerParams(vmem_limit_bytes=VMEM_LIMIT),
        cost_estimate=pl.CostEstimate(flops=flops, bytes_accessed=1, transcendentals=0),
        **options,
    )(*prefetch, *operands, *extra)


def whole(shape):
    return pl.BlockSpec(shape, lambda *_: (0,) * len(shape))


def plain(kernel, operands, out_shape, name, after=(), scratch=(), flops=1):
    return call(
        kernel,
        operands,
        after=after,
        flops=flops,
        grid=(1,),
        in_specs=[whole(x.shape) for x in operands],
        out_specs=jax.tree.map(lambda s: whole(s.shape), out_shape),
        out_shape=out_shape,
        scratch_shapes=scratch,
        name=name,
    )


def project_kernel(which_ref, x_ref, gain_ref, weight_ref, first_ref, out_ref):
    normed, _ = norm_parts(x_ref[...].astype(F32))
    first = (normed * row_of(gain_ref)).astype(BF)
    first_ref[0] = first
    for c in range(3):
        out_ref[c, 0] = dot(first, weight_ref[c]).astype(BF)


def project(which, rows, gain, weight, earlier, after=(), tiles=1):
    count, width = rows.shape
    cols = weight.shape[2]
    size = count // tiles
    return call(
        project_kernel,
        [rows, gain, weight],
        after=after,
        alias=earlier,
        prefetch=[which],
        grid=(tiles,),
        in_specs=[
            pl.BlockSpec((size, width), lambda i, w: (i, 0)),
            whole((width,)),
            whole((3, width, cols)),
        ],
        out_specs=[
            pl.BlockSpec((1, size, width), lambda i, w: (w[0], i, 0)),
            pl.BlockSpec((3, 1, size, cols), lambda i, w: (0, w[0], i, 0)),
        ],
        out_shape=[shaped((2, count, width), BF), shaped((3, 2, count, cols), BF)],
        name="project",
    )


def attend_kernel(
    which_ref, q_ref, kd_ref, vd_ref, kc_ref, vc_ref, pos_ref,
    pd_ref, pc_ref, rl_ref, context_ref, bias_d, bias_c,
):
    count = q_ref.shape[2]
    step = count // 2

    @pl.when(pl.program_id(0) == 0)
    def _():
        row = lax.broadcasted_iota(jnp.int32, (count, count), 0)
        col = lax.broadcasted_iota(jnp.int32, (count, count), 1)
        spread = jnp.broadcast_to(pos_ref[...].astype(F32), (8, count))
        start = row - jnp.transpose(spread)[:, :1].astype(jnp.int32)
        bias_d[...] = jnp.where((col <= row) & (col >= start), 0.0, HIDE)
        bias_c[...] = jnp.where(col >= start + count, 0.0, HIDE)

    lane = lax.broadcasted_iota(jnp.int32, (1, PAIR), 1) // HEAD_DIM

    def half(late):
        blocks = [(at, a) for at in (0, step) for a in (0, 1)]
        for a in (0, 1):
            pd_ref[0, a, :step, step:] = jnp.zeros((step, step), BF)
        scores = []
        for at, a in blocks:
            rows, keys = pl.ds(at, step), at + step
            mine = jnp.where(lane == a, q_ref[0, 0, rows, :] * 0.125, 0.0).astype(BF)
            s_d = dot_nt(mine, kd_ref[0, 0, :keys, :]) + bias_d[rows, :keys]
            s_c = dot_nt(mine, kc_ref[0, 0]) + bias_c[rows, :] if late else None
            scores.append((s_d, s_c))
        mixed, scale = {}, {}
        for (at, a), (s_d, s_c) in zip(blocks, scores):
            rows, keys = pl.ds(at, step), at + step
            top = jnp.max(s_d, axis=-1, keepdims=True)
            if late:
                top = jnp.maximum(top, jnp.max(s_c, axis=-1, keepdims=True))
            p_d = jnp.exp(s_d - top)
            total = jnp.sum(p_d, axis=-1, keepdims=True)
            p_d = p_d.astype(BF)
            pd_ref[0, a, rows, :keys] = p_d
            value = jnp.where(lane == a, vd_ref[0, 0, :keys, :], 0.0).astype(BF)
            mix = dot(p_d, value)
            if late:
                p_c = jnp.exp(s_c - top)
                total = total + jnp.sum(p_c, axis=-1, keepdims=True)
                p_c = p_c.astype(BF)
                pc_ref[0, a, rows, :] = p_c
                value = jnp.where(lane == a, vc_ref[0, 0], 0.0).astype(BF)
                mix = mix + dot(p_c, value)
            mixed[at, a], scale[at, a] = mix, 1.0 / total
        for at in (0, step):
            rows = pl.ds(at, step)
            inverse = jnp.where(lane == 0, scale[at, 0], scale[at, 1])
            rl_ref[0, rows, :] = inverse
            context_ref[rows, :] = ((mixed[at, 0] + mixed[at, 1]) * inverse).astype(BF)

    pl.when(which_ref[0] == 0)(lambda: half(False))
    pl.when(which_ref[0] == 1)(lambda: half(True))


def attend(which, projected, positions, earlier, after=(), flops=1):
    _, _, count, cols = projected.shape
    heads = cols // HEAD_DIM

    def block(part, other):
        if other:
            return pl.BlockSpec((1, 1, count, PAIR), lambda g, w: (part, 0, 0, g))
        return pl.BlockSpec((1, 1, count, PAIR), lambda g, w: (part, w[0], 0, g))

    score_spec = pl.BlockSpec((1, 2, count, count), lambda g, w: (w[0], g, 0, 0))
    return call(
        attend_kernel,
        [*[projected] * 5, positions],
        after=after,
        alias=earlier,
        prefetch=[which],
        flops=flops,
        grid=(cols // PAIR,),
        in_specs=[
            block(0, False),
            block(1, False),
            block(2, False),
            block(1, True),
            block(2, True),
            whole((1, count)),
        ],
        out_specs=[
            score_spec,
            score_spec,
            pl.BlockSpec((1, count, PAIR), lambda g, w: (w[0], 0, g)),
            pl.BlockSpec((count, PAIR), lambda g, w: (0, g)),
        ],
        scratch_shapes=[pltpu.VMEM((count, count), F32)] * 2,
        out_shape=[
            shaped((2, heads, count, count), BF),
            shaped((2, heads, count, count), BF),
            shaped((2, count, cols), F32),
            shaped((count, cols), BF),
        ],
        name="attend",
    )


def hidden_kernel(
    x_ref, own_ref, got_ref, own_weight_ref, got_weight_ref, gain_ref, slot_ref, hidden_ref, *out_refs
):
    attended = dot(own_ref[...], own_weight_ref[...]) + dot(got_ref[...], got_weight_ref[...])
    hidden = x_ref[...].astype(F32) + attended
    hidden_ref[...] = hidden
    normed, _ = norm_parts(hidden)
    second = (normed * row_of(gain_ref)).astype(BF)
    send_rows(second, slot_ref, out_refs)


def send_rows(rows, slot_ref, out_refs):
    capacity = out_refs[0].shape[0]
    for k, ref in enumerate(out_refs):
        slot = lax.broadcasted_iota(jnp.int32, (capacity, rows.shape[0]), 0) + k * capacity
        place = jnp.where(slot_ref[...] == slot, 1.0, 0.0).astype(BF)
        ref[...] = dot(place, rows).astype(BF)


def hidden_rows(x, own, got, own_weight, got_weight, gain, slot_row, experts, after=()):
    count, width = x.shape
    out = [shaped((count, width), F32)] + [shaped((count // 2, width), BF)] * experts
    return plain(
        hidden_kernel,
        [x, own, got, own_weight, got_weight, gain, slot_row],
        out,
        "hidden_rows",
        after,
    )


def send_kernel(rows_ref, slot_ref, weight_ref, out_ref, weight_out):
    send_rows(rows_ref[...], slot_ref, [out_ref.at[k] for k in range(out_ref.shape[0])])
    weight_out[...] = weight_ref[...]


def sent_rows(rows, slot_row, weight, experts, after=()):
    count, width = rows.shape
    out = [shaped((experts, count // 2, width), BF), shaped(weight.shape, BF)]
    return plain(send_kernel, [rows, slot_row, weight], out, "sent_rows", after)


def taken_rows(slot_ref, block_refs):
    count, capacity = slot_ref.shape[1], block_refs[0].shape[0]
    total = 0.0
    for k, ref in enumerate(block_refs):
        slot = lax.broadcasted_iota(jnp.int32, (capacity, count), 0) + k * capacity
        place = jnp.where(slot_ref[...] == slot, 1.0, 0.0).astype(BF)
        total = total + lax.dot_general(
            place, ref[...], (((0,), (0,)), ((), ())), preferred_element_type=F32
        )
    return total


def output_kernel(hidden_ref, slot_ref, *refs):
    blocks = [refs[0].at[k] for k in range(refs[0].shape[0])]
    refs[-1][...] = (hidden_ref[...] + taken_rows(slot_ref, blocks)).astype(BF)


def output_rows(hidden, slot_row, blocks, after=()):
    return plain(
        output_kernel,
        [hidden, slot_row, blocks],
        shaped(hidden.shape, BF),
        "output_rows",
        after,
        flops=FIRST_FLOPS,
    )


def second_kernel(cot_ref, hidden_ref, gain_ref, slot_ref, own_weight_ref, got_weight_ref, *refs):
    grad_ref, low_ref, gain_grad_ref, own_ref, send_ref = refs[-5:]
    second_grad = taken_rows(slot_ref, refs[:-5])
    normed, scale = norm_parts(hidden_ref[...])
    gain_grad_ref[...] = jnp.sum(second_grad * normed, axis=0, keepdims=True)
    grad = cot_ref[...].astype(F32) + norm_back(second_grad * row_of(gain_ref), normed, scale)
    grad_ref[...] = grad
    low = grad.astype(BF)
    low_ref[...] = low
    send_ref[...] = dot_nt(low, got_weight_ref[...]).astype(BF)
    own_ref[...] = dot_nt(low, own_weight_ref[...]).astype(BF)


def second_back(cot, hidden, gain, slot_row, own_weight, got_weight, blocks, after=()):
    count, width = hidden.shape
    part = shaped((count, own_weight.shape[0]), BF)
    out = [
        shaped((count, width), F32),
        shaped((count, width), BF),
        shaped((1, width), F32),
        part,
        part,
    ]
    return plain(
        second_kernel,
        [cot, hidden, gain, slot_row, own_weight, got_weight, *blocks],
        out,
        "second_back",
        after,
        flops=BACK_FLOPS,
    )


def output_weight_kernel(
    core_ref, own_ref, got_ref, low_ref, own_out, kept_out, sent_out, scratch
):
    def part(ref):
        return lax.dot_general(
            ref[...], low_ref[...], (((0,), (0,)), ((), ())), preferred_element_type=F32
        ).astype(BF)

    scratch[...] = part(got_ref)
    rows = kept_out.shape[0]
    for ref, half in ((kept_out, core_ref[0]), (sent_out, 1 - core_ref[0])):
        ref[...] = scratch[pl.ds(pl.multiple_of(half * rows, rows), rows), :]
    own_out[...] = part(own_ref)


def output_weight_parts(core, own, got, low, after=()):
    cols, width = own.shape[1], low.shape[1]
    part = shaped((cols // 2, width), BF)
    out = [shaped((cols, width), BF), part, part]
    return call(
        output_weight_kernel,
        [own, got, low],
        after=after,
        prefetch=[core],
        grid=(1,),
        in_specs=[whole(x.shape) for x in (own, got, low)],
        out_specs=[whole(o.shape) for o in out],
        out_shape=out,
        scratch_shapes=[pltpu.VMEM((cols, width), BF)],
        name="output_weight_parts",
    )


def first_kernel(x_ref, gain_ref, hidden_grad_ref, own_ref, theirs_ref, out_ref):
    grad = (own_ref[...] + theirs_ref[...].astype(F32)) * row_of(gain_ref)
    normed, scale = norm_parts(x_ref[...].astype(F32))
    out_ref[...] = hidden_grad_ref[...] + norm_back(grad, normed, scale)


def first_back(x, gain, hidden_grad, own, theirs, after=()):
    return plain(
        first_kernel,
        [x, gain, hidden_grad, own, theirs],
        shaped(x.shape, F32),
        "first_back",
        after,
    )


def fill(target, refs):
    rows = refs[0].shape[0]
    for i, ref in enumerate(refs):
        target[i * rows : (i + 1) * rows] = ref[...]


def expert_kernel(count, sub, place_ref, *refs):
    x_refs, cot_refs, refs = refs[:count], refs[count : 2 * count], refs[2 * count :]
    inner_ref, outer_ref, act_ref, pre_ref, out_ref, *grad_refs, x, cot, grad_acc, out_acc = refs
    at = pl.program_id(0)
    last = pl.num_programs(0) - count
    size = out_ref.shape[1]

    @pl.when(at > last)
    def _():
        rows = pl.ds(pl.multiple_of((at - last) * size, size), size)
        out_ref[0] = out_acc[rows, :].astype(BF)

    pl.when(at <= last)(
        lambda: expert_step(
            count, sub, x_refs, cot_refs, inner_ref, outer_ref, act_ref, pre_ref, out_ref,
            grad_refs, x, cot, grad_acc, out_acc, at, last,
        )
    )


def expert_step(
    count, sub, x_refs, cot_refs, inner_ref, outer_ref, act_ref, pre_ref, out_ref, grad_refs,
    x, cot, grad_acc, out_acc, at, last,
):

    @pl.when(at == 0)
    def _():
        fill(x, x_refs)
        fill(cot, [ref.at[0] for ref in cot_refs])
        grad_acc[...] = jnp.zeros_like(grad_acc)
        out_acc[...] = jnp.zeros_like(out_acc)

    def front(i):
        cols = slice(i * sub, (i + 1) * sub)
        return dot(x[...], inner_ref[:, cols]), dot_nt(cot[...], outer_ref[cols, :])

    parts = inner_ref.shape[1] // sub
    now = front(0)
    for i in range(parts):
        later = front(i + 1) if i + 1 < parts else None
        value, grad = now
        square = value * value
        half = 0.5 + 0.5 * jnp.tanh(
            value * (0.7978845608028654 + 0.035677408136300125 * square)
        )
        act = value * half
        slope = half + act * (1.0 - half) * (1.5957691216057308 + 0.21406444881780074 * square)
        cols = slice(i * sub, (i + 1) * sub)
        act_ref[:, cols] = act.astype(BF)
        pre_ref[:, cols] = (grad * slope).astype(BF)
        now = later
    grad_acc[...] += dot_nt(pre_ref[...], inner_ref[...])
    out_acc[...] += dot(act_ref[...], outer_ref[...])

    @pl.when(at == last)
    def _():
        size = out_ref.shape[1]
        out_ref[0] = out_acc[:size].astype(BF)
        for i, ref in enumerate(grad_refs):
            ref[...] = grad_acc[i * size : (i + 1) * size].astype(BF)


def expert(place, index, blocks, cot, inner, outer, earlier, after=(), tile=1536, sub=256):
    count, width = blocks[0].shape
    size, units = len(blocks), inner.shape[1]
    total = count * cot.shape[0]
    tiles = units // tile

    def held(j):
        return jnp.minimum(j, tiles - 1)

    wide = pl.BlockSpec((count * size, tile), lambda j, p: (index // size, held(j)))
    out = pl.BlockSpec(
        (1, count, width), lambda j, p: (p[jnp.maximum(j - tiles + 1, 0)], 0, 0)
    )

    def placed(i):
        return pl.BlockSpec((1, count, width), lambda j, p: (p[i], 0, 0))

    return call(
        functools.partial(expert_kernel, size, sub),
        [*blocks, *[cot] * size, inner, outer],
        after=after,
        flops=EXPERT_FLOPS,
        alias=earlier,
        prefetch=[place],
        grid=(tiles + size - 1,),
        in_specs=[whole((count, width))] * size
        + [placed(i) for i in range(size)]
        + [
            pl.BlockSpec((width, tile), lambda j, p: (0, held(j))),
            pl.BlockSpec((tile, width), lambda j, p: (held(j), 0)),
        ],
        out_specs=[wide, wide, out] + [whole((count, width))] * size,
        out_shape=[shaped((total, units), BF)] * 2
        + [shaped(cot.shape, BF)]
        + [shaped((count, width), BF)] * size,
        scratch_shapes=[pltpu.VMEM((count * size, width), BF)] * 2
        + [pltpu.VMEM((count * size, width), F32)] * 2,
        name="expert",
    )


def weight_kernel(is_outer, count, added, info_ref, wide_ref, *refs):
    row_count = 1 if is_outer else count
    row_refs, refs = refs[:row_count], refs[row_count:]
    if is_outer:
        row_refs = [row_refs[0].at[info_ref[ORDER + i]] for i in range(count)]
    got_ref = refs[0] if added else None
    *out_refs, rows = refs[1:] if added else refs
    at = pl.program_id(0)
    pl.when(at == 0)(lambda: fill(rows, row_refs))

    def put(out_ref):
        sides = (wide_ref[...], rows[...]) if is_outer else (rows[...], wide_ref[...])
        part = lax.dot_general(*sides, (((0,), (0,)), ((), ())), preferred_element_type=F32)
        if added:
            part = part + got_ref[...].astype(F32)
        out_ref[...] = part.astype(BF)

    if added:
        for i, out_ref in enumerate(out_refs):
            pl.when(at == i)(functools.partial(put, out_ref))
    else:
        put(out_refs[0])


def weight_part(info, is_outer, half, turn, blocks, wide, got=None, after=()):
    total, units = wide.shape
    width, added, tile = blocks[0].shape[1], got is not None, units // 4
    count = len(blocks) if not is_outer else blocks.shape[0]
    if is_outer:
        row_specs, blocks = [whole(blocks.shape)], [blocks]
    else:
        row_specs = [whole(block.shape) for block in blocks]

    def at(j):
        return (j, 0) if is_outer else (0, j)

    def place(j, w):
        return (w[turn] + j) % 2

    def shape(units):
        return (units, width) if is_outer else (width, units)

    block = pl.BlockSpec(shape(tile), lambda j, w: at(place(j, w)))
    if added:
        out, out_specs = [shaped(shape(tile), BF)] * 2, [whole(shape(tile))] * 2
    else:
        out, out_specs = [shaped(shape(2 * tile), BF)], [block]
    return call(
        functools.partial(weight_kernel, is_outer, count, added),
        [wide, *blocks] + ([got] if added else []),
        after=after,
        prefetch=[info],
        grid=(2,),
        in_specs=[pl.BlockSpec((total, tile), lambda j, w: (0, w[half] * 2 + place(j, w)))]
        + row_specs
        + ([block] if added else []),
        out_specs=out_specs,
        out_shape=out,
        scratch_shapes=[pltpu.VMEM((total, width), BF)],
        name="weight_part",
    )


def assemble_kernel(counts, info_ref, *refs):
    piece_refs, out_refs = refs[: sum(counts)], refs[sum(counts) :]
    targets = [out for out, count in zip(out_refs, counts) for _ in range(count)]
    for i, (ref, out_ref) in enumerate(zip(piece_refs, targets)):

        @pl.when(pl.program_id(0) == i)
        def _(ref=ref, out_ref=out_ref):
            out_ref[...] = ref[...].astype(F32)


def assemble(info, start, groups, shapes, earlier, after=()):
    counts = [len(pieces) for pieces in groups]
    pieces = [piece for group in groups for piece in group]
    size = pieces[0].shape

    def spec(first, count):
        def at(i, t):
            held = start + 2 * jnp.clip(i, first, first + count - 1)
            return t[held], t[held + 1]

        return pl.BlockSpec(size, at)

    firsts = [sum(counts[:i]) for i in range(len(counts))]
    return call(
        functools.partial(assemble_kernel, counts),
        pieces,
        after=after,
        alias=earlier,
        prefetch=[info],
        grid=(len(pieces),),
        in_specs=[whole(size)] * len(pieces),
        out_specs=[spec(first, count) for first, count in zip(firsts, counts)],
        out_shape=[shaped(shape, F32) for shape in shapes],
        name="assemble",
    )


def add_kernel(kept_ref, got_ref, out_ref):
    out_ref[...] = (kept_ref[...].astype(F32) + got_ref[...].astype(F32)).astype(BF)


def add(kept, got):
    return plain(add_kernel, [kept, got], shaped(kept.shape, BF), "add")


def gather_sum_kernel(kept_ref, got_ref, more_ref, out_ref, tail_ref):
    rows, more = out_ref.shape[0], more_ref.shape[0]
    first = rows - more
    out_ref[:first] = (kept_ref[:first].astype(F32) + got_ref[:first].astype(F32)).astype(BF)
    last = kept_ref[first:rows].astype(F32) + got_ref[first:rows].astype(F32)
    out_ref[first:] = (last + more_ref[...].astype(F32)).astype(BF)
    tail_ref[...] = (kept_ref[rows:].astype(F32) + got_ref[rows:].astype(F32)).astype(BF)


def gather_sum(kept, got, more, rows, after=()):
    lines, width = kept.shape
    out = [shaped((rows, width), BF), shaped((lines - rows, width), BF)]
    return plain(gather_sum_kernel, [kept, got, more], out, "gather_sum", after)


def adds_kernel(start, count, cuts, whole_sum, info_ref, *refs):
    in_refs, out_refs = refs[: 2 * count], refs[2 * count :]
    for i in range(count):
        kept_ref, got_ref = in_refs[2 * i : 2 * i + 2]
        for j in range(cuts):
            ref = out_refs[cuts * i + j]
            rows = ref.shape[0]
            at = 0 if whole_sum else info_ref[start + cuts * i + j]
            cut = pl.ds(pl.multiple_of(at * rows, rows), rows)
            ref[...] = (kept_ref[cut, :].astype(F32) + got_ref[cut, :].astype(F32)).astype(BF)


def adds(info, start, pairs, cuts, whole_sum=False, after=()):
    out = [
        shaped((kept.shape[0] // (1 if whole_sum else cuts), kept.shape[1]), BF)
        for kept, _ in pairs
        for _ in range(cuts)
    ]
    operands = [x for pair in pairs for x in pair]
    parts = call(
        functools.partial(adds_kernel, start, len(pairs), cuts, whole_sum),
        operands,
        after=after,
        prefetch=[info],
        grid=(1,),
        in_specs=[whole(x.shape) for x in operands],
        out_specs=[whole(o.shape) for o in out],
        out_shape=out,
        name="adds",
    )
    return [parts[cuts * i : cuts * (i + 1)] for i in range(len(pairs))]


def piece_places(steps, order):
    weights = {step: 1 << (len(steps) - 1 - i) for i, step in enumerate(steps)}
    place = sum(side(*step) * weight for step, weight in weights.items())
    places, newest = [place], [(0, place)]
    while newest:
        newest = [
            (i + 1, at + weights[order[i]] * (1 - 2 * side(*order[i])))
            for first, at in newest
            for i in range(first, len(order))
        ]
        places += [at for _, at in newest]
    return places


def gather_pieces(own, steps, order, flops, after):
    pieces, newest = [own], [(0, own)]
    while newest:
        found = [
            (i + 1, swap(piece, *order[i], "piece"))
            for first, piece in newest
            for i in range(first, len(order))
        ]
        if len(pieces) == 1:
            held = touch([piece for _, piece in found], after, flops=flops)
            found = [(first, piece) for (first, _), piece in zip(found, held)]
        pieces += [piece for _, piece in found]
        newest = found
    return list(zip(piece_places(steps, order), pieces))


def total_kernel(in_ref, tail_ref, got_ref, out_ref):
    count, rows = in_ref.shape[:2]
    value = sum(in_ref[i].astype(F32) for i in range(count)).astype(BF)
    tail = sum(ref[i : i + 1].astype(F32) for ref in (tail_ref, got_ref) for i in (0, 1))
    high = tail.astype(BF).astype(F32)
    line = lax.broadcasted_iota(jnp.int32, tail_ref.shape, 0)
    tail = jnp.where(line == 0, high, jnp.where(line == 1, tail - high, 0.0)).astype(BF)
    for i in range(count):
        out_ref[i, :rows] = value
        out_ref[i, rows:] = tail


def total(blocks, tail, got, after=()):
    count, rows, width = blocks.shape
    out = shaped((count, rows + tail.shape[0], width), BF)
    return plain(total_kernel, [blocks, tail, got], out, "total", after)


def halves(step):
    mine = side(*step)
    return [1 - mine, mine]


def touch_kernel(*out_refs):
    pass


def touch(values, after, flops=1):
    return call(
        touch_kernel,
        [],
        after=after,
        alias=values,
        flops=flops,
        in_specs=[],
        out_specs=[pl.BlockSpec(memory_space=pl.ANY)] * len(values),
        out_shape=[shaped(x.shape, x.dtype) for x in values],
        name="touch",
    )


def back_kernel(
    at_ref, own_ref, other_ref, q_ref, k_ref, v_ref, pd_ref, pc_ref, own_context_ref,
    other_context_ref, rl_ref, first_ref, wp_ref, gain_ref, second_ref, own_output_ref,
    sent_ref, kept_ref, mine_ref, theirs_ref,
    acc, scaled, through, key_acc, value_acc, queries, weights, scores,
):
    group = pl.program_id(0)
    count = own_ref.shape[0]
    step = count // 2
    me, core = at_ref[0], at_ref[CORE]
    lane = lax.broadcasted_iota(jnp.int32, (1, PAIR), 1) // HEAD_DIM

    for ref, context, at in (
        (own_ref, own_context_ref, me),
        (other_ref, other_context_ref, 1 - me),
    ):
        grad = ref[...].astype(F32) * rl_ref[at]
        scaled[at] = grad
        through[at] = grad.astype(BF).astype(F32) * context[...].astype(F32)
    @pl.when(group == 0)
    def _():
        for h in (0, 1):
            for a in (0, 1):
                scores[h, a, :step, step:] = jnp.zeros((step, step), BF)

    for h in (0, 1):
        for at in (0, step):
            rows = pl.ds(at, step)
            low = scaled[h, rows, :].astype(BF)
            query = 0.0
            for a in (0, 1):
                mine = jnp.where(lane == a, low, 0.0).astype(BF)
                along = jnp.sum(
                    jnp.where(lane == a, through[h, rows, :], 0.0), axis=-1, keepdims=True
                )
                parts = [(pd_ref, h, h, at + step)]
                if h:
                    parts.append((pc_ref, 0, 2, count))
                for p_ref, p_at, to, keys in parts:
                    source = 0 if to == 2 else h
                    prob_grad = dot_nt(mine, v_ref[0, source, :keys, :])
                    p = p_ref[p_at, a, rows, :keys]
                    score = (p.astype(F32) * (prob_grad - along)).astype(BF)
                    scores[to, a, rows, :keys] = score
                    k = jnp.where(lane == a, k_ref[0, source, :keys, :], 0.0).astype(BF)
                    query = query + dot(score, k)
            queries[pl.ds(h * count + at, step), :] = query * 0.125
    low_t = [jnp.transpose(scaled[h]).astype(BF) for h in (0, 1)]
    q_t = [jnp.transpose(q_ref[0, h].astype(F32)).astype(BF) for h in (0, 1)]
    for a in (0, 1):
        line = slice(a * HEAD_DIM, (a + 1) * HEAD_DIM)
        key_acc[line, :count] = dot(q_t[0][line], scores[0, a]) + dot(q_t[1][line], scores[2, a])
        key_acc[line, count:] = dot(q_t[1][line], scores[1, a])
        value_acc[line, :count] = dot(low_t[0][line], pd_ref[0, a]) + dot(
            low_t[1][line], pc_ref[0, a]
        )
        value_acc[line, count:] = dot(low_t[1][line], pd_ref[1, a])

    query = queries[...]
    key_t = key_acc[...] * 0.125
    value_t = value_acc[...]
    both = jnp.concatenate(
        [query.astype(BF), jnp.transpose(key_t).astype(BF), jnp.transpose(value_t).astype(BF)],
        axis=1,
    )
    both_t = jnp.concatenate(
        [jnp.transpose(query).astype(BF), key_t.astype(BF), value_t.astype(BF)], axis=0
    )
    first = jnp.concatenate([first_ref[0], first_ref[1]], axis=0)
    weights[...] = dot(both_t, first)
    size = 3 * PAIR // 2
    groups = pl.num_programs(0)
    here = pl.ds(pl.multiple_of(group * size, size), size)
    for ref, half in ((sent_ref, 1 - core), (kept_ref, core)):
        ref[here, :] = weights[pl.ds(pl.multiple_of(half * size, size), size), :].astype(BF)
    weight = jnp.concatenate([wp_ref[0], wp_ref[1], wp_ref[2]], axis=1)
    added = dot_nt(both, weight)

    @pl.when(group == 0)
    def _():
        for h in (0, 1):
            acc[h] = added[h * count : (h + 1) * count]

    @pl.when(group > 0)
    def _():
        for h in (0, 1):
            acc[h] += added[h * count : (h + 1) * count]

    @pl.when(group == groups - 1)
    def _():
        mine_ref[...] = acc[me]
        theirs_ref[...] = acc[1 - me].astype(BF)
        gain = 0.0
        for h in (0, 1):
            gain = gain + jnp.sum(acc[h] * first_ref[h].astype(F32), axis=0, keepdims=True)
        gain = gain / row_of(gain_ref)
        part = own_output_ref.shape[0] // 2
        at = groups * size
        end = at + part
        for ref, half in ((sent_ref, 1 - core), (kept_ref, core)):
            cut = pl.ds(pl.multiple_of(half * part, part), part)
            ref[at:end, :] = own_output_ref[cut, :]
            value = jnp.where(half == 0, gain, second_ref[...])
            high = value.astype(BF).astype(F32)
            line = lax.broadcasted_iota(jnp.int32, (ref.shape[0] - end, value.shape[1]), 0)
            tail = jnp.where(line == 0, high, jnp.where(line == 1, value - high, 0.0))
            ref[end:, :] = tail.astype(BF)


def attend_back(
    at, own, other, projected, p_diag, p_cross, own_context, other_context, inverse, first, weight,
    gain, second, own_output, lines, after=(),
):
    _, _, count, cols = projected.shape
    width = first.shape[2]
    rows = whole((count, width))
    pair = pl.BlockSpec((count, PAIR), lambda g, w: (0, g))

    def block(part):
        return pl.BlockSpec((1, 2, count, PAIR), lambda g, w: (part, 0, 0, g))

    sent = shaped((lines, width), BF)
    out = [sent, sent, shaped((count, width), F32), shaped((count, width), BF)]
    return call(
        back_kernel,
        [
            own, other, projected, projected, projected, p_diag, p_cross, own_context,
            other_context, inverse, first, weight, gain, second, own_output,
        ],
        after=after,
        flops=ATTBACK_FLOPS,
        prefetch=[at],
        grid=(cols // PAIR,),
        in_specs=[
            pair,
            pair,
            block(0),
            block(1),
            block(2),
            pl.BlockSpec((2, 2, count, count), lambda g, w: (0, g, 0, 0)),
            pl.BlockSpec((1, 2, count, count), lambda g, w: (1, g, 0, 0)),
            pair,
            pair,
            pl.BlockSpec((2, count, PAIR), lambda g, w: (0, 0, g)),
            whole((2, count, width)),
            pl.BlockSpec((3, width, PAIR), lambda g, w: (0, 0, g)),
            whole((width,)),
            whole((1, width)),
            whole((cols, width)),
        ],
        out_specs=[whole(o.shape) for o in out],
        scratch_shapes=[
            pltpu.VMEM((2, count, width), F32),
            pltpu.VMEM((2, count, PAIR), F32),
            pltpu.VMEM((2, count, PAIR), F32),
            pltpu.VMEM((PAIR, 2 * count), F32),
            pltpu.VMEM((PAIR, 2 * count), F32),
            pltpu.VMEM((2 * count, PAIR), F32),
            pltpu.VMEM((3 * PAIR, width), F32),
            pltpu.VMEM((3, 2, count, count), BF),
        ],
        out_shape=out,
        name="attend_back",
    )


def weight_outputs_kernel(rows, core_ref, kept_ref, got_ref, project_ref, output_ref, *gain_refs):
    group, groups = pl.program_id(0), pl.num_programs(0)
    size = 3 * PAIR // 2

    def halves_of(cut, which):
        kept, got = [
            jnp.concatenate([ref[block, cut, :] for block in which], axis=0).astype(F32)
            for ref in (kept_ref, got_ref)
        ]
        low = jnp.where(core_ref[0] == 0, kept, got)
        return low, jnp.where(core_ref[0] == 0, got, kept)

    body, blocks = slice(0, rows), size // rows
    low, high = halves_of(body, [group * blocks + i for i in range(blocks)])
    flat = jnp.transpose(jnp.concatenate([low, high], axis=0))
    for c in range(3):
        project_ref[c] = flat[:, c * PAIR : (c + 1) * PAIR]

    @pl.when(group == groups - 1)
    def _():
        part, count = output_ref.shape[0] // 2, kept_ref.shape[0]
        first = groups * size // rows
        output_ref[:part], output_ref[part:] = halves_of(body, range(first, count))
        tails = halves_of(slice(rows, rows + 16), range(count))
        for i, tail in enumerate(tails):
            gain_refs[i][...] = sum(
                tail[16 * b : 16 * b + 1] + tail[16 * b + 1 : 16 * b + 2] for b in range(count)
            )[0]


def weight_outputs(core, kept, got, cols, after=()):
    _, rows, width = kept.shape
    return call(
        functools.partial(weight_outputs_kernel, rows - 16),
        [kept, got],
        after=after,
        prefetch=[core],
        grid=(cols // PAIR,),
        in_specs=[whole(kept.shape)] * 2,
        out_specs=[
            pl.BlockSpec((3, width, PAIR), lambda g, w: (0, 0, g)),
            whole((cols, width)),
            whole((width,)),
            whole((width,)),
        ],
        out_shape=[shaped((3, width, cols), F32), shaped((cols, width), F32)]
        + [shaped((width,), F32)] * 2,
        name="weight_outputs",
    )


def on_device(
    block_input,
    output_cotangent,
    token_ids,
    positions,
    hash_table,
    first_gain,
    second_gain,
    project_weight,
    output_weight,
    expert_inner,
    expert_outer,
):
    tok_rows, model_width = block_input.shape
    local_cols = output_weight.shape[0]
    expert_count = lax.axis_size("expert")
    capacity = tok_rows // 2
    inner_weight = expert_inner[0]
    outer_weight = expert_outer[0]
    my_head = lax.axis_index("head")
    my_expert = lax.axis_index("expert")
    core = lax.axis_index("core")
    turns = bits_of("x") + bits_of("head")
    outer_steps, inner_steps = turns, turns[::-1]
    order = [my_expert ^ k for k in range(expert_count)]

    early = len(turns) + 1
    entries = [
        my_head, 1 - my_head, core, 1 - core, 0 * core,
        1 - side(*outer_steps[0]), 1 - side(*inner_steps[0]), *order,
    ]
    adds_at = [len(entries) + 4 * i for i in range(len(turns) - 1)]
    for i in range(1, len(turns)):
        entries += [*halves(outer_steps[i]), *halves(inner_steps[i])]
    half = 1 << (len(turns) - 1)

    def placed(place, which, is_outer):
        if is_outer:
            return [which * 2 * half + place, 0 * place]
        return [place % half, which * 2 + place // half]

    piece_at = []
    for chosen in (slice(early), slice(early, None)):
        for steps, is_outer in ((outer_steps, True), (inner_steps, False)):
            piece_at.append(len(entries))
            for which in (core, 1 - core):
                for place in piece_places(steps, steps[::-1])[chosen]:
                    entries += placed(place, which, is_outer)
    info = jnp.stack(entries).astype(jnp.int32)
    own_at, core_at = my_head.reshape(1).astype(jnp.int32), core.reshape(1).astype(jnp.int32)
    other_at = 1 - own_at

    other_input = swap(block_input, "head", 1, "rows")
    other_pos = swap(positions, "head", 1, "positions")

    chosen = jnp.take(hash_table, token_ids)
    relative = chosen ^ my_expert
    one_hot = relative[:, None] == jnp.arange(expert_count, dtype=jnp.int32)[None, :]
    rank_table = jnp.cumsum(one_hot.astype(jnp.int32), axis=0) - 1
    slot_index = relative * capacity + jnp.sum(jnp.where(one_hot, rank_table, 0), axis=1)
    slot_row = slot_index[None, :]
    absolute = slot_index + (chosen - relative) * capacity

    def exchange(blocks, name, first=0):
        return [
            swap(block, "expert", k, f"{name}{k}") if k else block
            for k, block in enumerate(blocks, first)
        ]

    def exchange_all(blocks):
        return lax.all_to_all(blocks, "expert", split_axis=0, concat_axis=0, tiled=True)

    done = project(own_at, block_input, first_gain, project_weight, [])
    sent, weight_sent = sent_rows(
        output_cotangent, absolute[None, :], output_weight, expert_count, after=[done[0], other_pos]
    )
    grad_blocks = exchange_all(sent)
    first_low, projected = project(other_at, other_input, first_gain, project_weight, done)
    other_weight = swap(weight_sent, "head", 1, "output_weight")
    *done, other_context = attend(other_at, projected, other_pos[None, :], [])
    got_context = swap(other_context, "head", 1, "context")
    p_diag, p_cross, inverse, own_context = attend(
        own_at,
        projected,
        positions[None, :],
        done,
        after=[other_weight],
        flops=ATTEND_FLOPS,
    )
    hidden, *outgoing = hidden_rows(
        block_input,
        own_context,
        got_context,
        output_weight,
        other_weight,
        second_gain,
        slot_row,
        expert_count,
    )

    row_blocks = exchange(outgoing, "dispatch")
    done, returned, at = [], [], 0
    while at < expert_count:
        size = 1
        parts = expert(
            order[at].reshape(1).astype(jnp.int32), at, row_blocks[at : at + size], grad_blocks if at else sent, inner_weight,
            outer_weight, done,
        )
        done, grads = parts[:3], parts[3:]
        returned += exchange(grads, "return", at)
        at += size
    activated, pre_grad, produced = done

    (outer_sent,) = weight_part(info, True, OTHER_CORE, NONE, grad_blocks, activated, after=grads)
    outer_got = swap(outer_sent, "core", 1, "outer_core")
    (inner_sent,) = weight_part(
        info, False, OTHER_CORE, NONE, row_blocks, pre_grad, after=[outer_sent]
    )
    inner_got = swap(inner_sent, "core", 1, "inner_core")
    token = touch([jnp.zeros((8, 128), F32)], [inner_sent], flops=BACK_FLOPS)
    outer_parts = weight_part(
        info, True, CORE, OUTER_TURN, grad_blocks, activated, outer_got, after=token
    )
    inner_parts = weight_part(
        info, False, CORE, INNER_TURN, row_blocks, pre_grad, inner_got, after=[outer_parts[0]]
    )

    hidden_grad, hidden_low, second_gain_part, own_grad, grad_sent = second_back(
        output_cotangent,
        hidden,
        second_gain,
        slot_row,
        output_weight,
        other_weight,
        returned,
        after=[inner_parts[0]],
    )
    other_grad = swap(grad_sent, "head", 1, "context_grad")
    def pairs_of(outer, inner, i):
        return [
            (outer[1], swap(outer[0], *outer_steps[i], f"outer{i}")),
            (inner[1], swap(inner[0], *inner_steps[i], f"inner{i}")),
        ]

    own_output, output_kept, output_sent = output_weight_parts(
        core_at, own_context, got_context, hidden_low, after=[grad_sent]
    )
    output_sent = add(output_kept, swap(output_sent, "core", 1, "output_core"))
    combined = exchange_all(touch([produced], [output_sent])[0])
    got_output = swap(output_sent, "head", 1, "output_grad")

    groups = local_cols // PAIR
    end = 2 * local_cols
    lines = end + 16
    sent, kept, mine, theirs = attend_back(
        info, own_grad, other_grad, projected, p_diag,
        p_cross, own_context, other_context, inverse, first_low, project_weight, first_gain,
        second_gain_part, own_output, lines, after=[inner_parts[0]],
    )
    at = 3 * local_cols // 2
    for i in range(len(turns) - 1):
        outer_parts, inner_parts = adds(
            info, adds_at[i], pairs_of(outer_parts, inner_parts, i), 2, after=[kept]
        )
    more = touch([got_output], outer_parts, flops=BACK_FLOPS)
    got = swap(sent, "core", 1, "weight")
    summed, tail = gather_sum(kept, got, more[0], end, after=more)
    crowd = ("x", "expert")
    summed = summed.reshape(-1, end // lax.axis_size(crowd), model_width)
    arrived = lax.all_to_all(summed, crowd, split_axis=0, concat_axis=0, tiled=True)
    block_output = output_rows(hidden, absolute[None, :], combined, after=[summed])
    got_tail = swap(tail, "head", 1, "gains")
    theirs = swap(touch([theirs], [got_tail])[0], "head", 1, "theirs")
    (outer_own, outer_copy), (inner_own, inner_copy) = adds(
        info, 0, pairs_of(outer_parts, inner_parts, -1), 2, True, after=[block_output, got_tail]
    )
    arrived = total(
        arrived, tail, got_tail, after=[outer_own, inner_own]
    )
    input_grad = first_back(
        block_input, first_gain, hidden_grad, mine, theirs, after=[arrived]
    )
    outer_pieces = gather_pieces(outer_own, outer_steps, outer_steps[::-1], BACK_FLOPS, [input_grad])
    inner_pieces = gather_pieces(inner_own, inner_steps, inner_steps[::-1], 1, [input_grad])
    summed = lax.all_to_all(arrived, crowd, split_axis=0, concat_axis=0, tiled=True)

    def core_swaps(pieces):
        return [(at, swap(piece, "core", 1, "piece_core")) for at, piece in pieces]

    others = []
    for pieces, own in ((outer_pieces, outer_copy), (inner_pieces, inner_copy)):
        (held,) = touch([own], [arrived])
        others.append(core_swaps([(pieces[0][0], held), *pieces[1:early]]))
    shapes = [outer_weight.shape, inner_weight.shape]
    totals = []
    for i, pieces in enumerate((outer_pieces, inner_pieces)):
        chosen = [piece for _, piece in pieces[:early] + others[i]]
        totals += assemble(
            info, piece_at[i], [chosen], shapes[i : i + 1], [], after=[arrived] + totals[-1:]
        )
    late = []
    for pieces in (outer_pieces, inner_pieces):
        held = touch([piece for _, piece in pieces[early:]], totals)
        late.append([(at, piece) for (at, _), piece in zip(pieces[early:], held)])
    late_others = [core_swaps(pieces) for pieces in late]
    (kept,) = touch([summed], [pieces[0][1] for pieces in late])
    got = swap(kept, "core", 1, "weight_back")
    project_grad, output_weight_grad, first_total, second_total = weight_outputs(core_at, kept, got, local_cols)
    chosen = [
        [piece for _, piece in own + other] for own, other in zip(late, late_others)
    ]
    outer_total, inner_total = assemble(
        info, piece_at[2], chosen, shapes, totals, after=[project_grad]
    )
    return (
        block_output,
        input_grad,
        first_total,
        second_total,
        project_grad,
        output_weight_grad,
        inner_total[None],
        outer_total[None],
    )


def solution(mesh):
    devices = mesh.devices
    mesh = Mesh(
        devices.reshape(devices.shape[0] // 2, 2, *devices.shape[1:]), ("x", "core", "expert", "head")
    )
    in_specs = (
        P(("x", "core", "expert", "head"), None),
        P(("x", "core", "expert", "head"), None),
        P(("x", "core", "expert", "head")),
        P(("x", "core", "expert", "head")),
        P(),
        P(),
        P(),
        P(None, None, "head"),
        P("head", None),
        P("expert", None, None),
        P("expert", None, None),
    )
    out_specs = (
        P(("x", "core", "expert", "head"), None),
        P(("x", "core", "expert", "head"), None),
        P(),
        P(),
        P(None, None, "head"),
        P("head", None),
        P("expert", None, None),
        P("expert", None, None),
    )
    return jax.shard_map(
        on_device, mesh=mesh, in_specs=in_specs, out_specs=out_specs, check_vma=False
    )
```

```python
import functools

import jax
import jax.numpy as jnp
from jax import lax
from jax.experimental import pallas as pl
from jax.experimental.pallas import tpu as pltpu
from jax.sharding import Mesh
from jax.sharding import PartitionSpec as P

HEAD_DIM = 64
BF = jnp.bfloat16
F32 = jnp.float32


def swap(values, axis, bit, name):
    size = lax.axis_size(axis)
    with jax.named_scope(name):
        return lax.ppermute(values, axis, [(i, i ^ bit) for i in range(size)])


def bits_of(axis, low=1):
    size = lax.axis_size(axis)
    found = []
    while low < size:
        found.append((axis, low))
        low *= 2
    return found


def side(axis, bit):
    return (lax.axis_index(axis) // bit) % 2


PAIR = 2 * HEAD_DIM
CORE, OTHER_CORE, NONE, OUTER_TURN, INNER_TURN, ORDER = 2, 3, 4, 5, 6, 7
EXPERT_FLOPS = 2 * 10**9
ATTEND_FLOPS = 20 * 10**9
BACK_FLOPS = 300 * 10**9
ATTBACK_FLOPS = 50 * 10**9
FIRST_FLOPS = 300 * 10**9
HIDE = -1000000000.0
VMEM_LIMIT = 64 * 1024 * 1024


def dot(left, right):
    return jnp.dot(left, right, preferred_element_type=F32)


def dot_nt(left, right):
    return lax.dot_general(left, right, (((1,), (1,)), ((), ())), preferred_element_type=F32)


def row_of(ref):
    return ref[...].reshape(1, ref.shape[0])


def norm_parts(values):
    center = values - jnp.mean(values, axis=-1, keepdims=True)
    scale = lax.rsqrt(jnp.mean(center * center, axis=-1, keepdims=True) + 1e-05)
    return center * scale, scale


def norm_back(grad, normed, scale):
    along = jnp.mean(grad * normed, axis=-1, keepdims=True)
    return scale * (grad - jnp.mean(grad, axis=-1, keepdims=True) - normed * along)


def shaped(shape, dtype):
    return jax.ShapeDtypeStruct(shape, dtype)


def call(kernel, operands, after=(), alias=(), prefetch=(), flops=1, **options):
    extra = [*alias, *after]
    anywhere = pl.BlockSpec(memory_space=pl.ANY)
    options["in_specs"] = [*options["in_specs"], *[anywhere] * len(extra)]
    first = len(prefetch) + len(operands)
    fixed, skip = len(operands), len(extra)

    def body(*refs):
        cut = len(prefetch) + fixed
        kernel(*refs[:cut], *refs[cut + skip :])

    if prefetch:
        specs = {name: options.pop(name) for name in ("grid", "in_specs", "out_specs")}
        specs["scratch_shapes"] = options.pop("scratch_shapes", ())
        options["grid_spec"] = pltpu.PrefetchScalarGridSpec(
            num_scalar_prefetch=len(prefetch), **specs
        )
    return pl.pallas_call(
        body,
        input_output_aliases={first + i: i for i in range(len(alias))},
        compiler_params=pltpu.CompilerParams(vmem_limit_bytes=VMEM_LIMIT),
        cost_estimate=pl.CostEstimate(flops=flops, bytes_accessed=1, transcendentals=0),
        **options,
    )(*prefetch, *operands, *extra)


def whole(shape):
    return pl.BlockSpec(shape, lambda *_: (0,) * len(shape))


def plain(kernel, operands, out_shape, name, after=(), scratch=(), flops=1):
    return call(
        kernel,
        operands,
        after=after,
        flops=flops,
        grid=(1,),
        in_specs=[whole(x.shape) for x in operands],
        out_specs=jax.tree.map(lambda s: whole(s.shape), out_shape),
        out_shape=out_shape,
        scratch_shapes=scratch,
        name=name,
    )


def project_kernel(which_ref, x_ref, gain_ref, weight_ref, first_ref, out_ref):
    normed, _ = norm_parts(x_ref[...].astype(F32))
    first = (normed * row_of(gain_ref)).astype(BF)
    first_ref[0] = first
    for c in range(3):
        out_ref[c, 0] = dot(first, weight_ref[c]).astype(BF)


def project(which, rows, gain, weight, earlier, after=(), tiles=1):
    count, width = rows.shape
    cols = weight.shape[2]
    size = count // tiles
    return call(
        project_kernel,
        [rows, gain, weight],
        after=after,
        alias=earlier,
        prefetch=[which],
        grid=(tiles,),
        in_specs=[
            pl.BlockSpec((size, width), lambda i, w: (i, 0)),
            whole((width,)),
            whole((3, width, cols)),
        ],
        out_specs=[
            pl.BlockSpec((1, size, width), lambda i, w: (w[0], i, 0)),
            pl.BlockSpec((3, 1, size, cols), lambda i, w: (0, w[0], i, 0)),
        ],
        out_shape=[shaped((2, count, width), BF), shaped((3, 2, count, cols), BF)],
        name="project",
    )


def attend_kernel(
    which_ref, q_ref, kd_ref, vd_ref, kc_ref, vc_ref, pos_ref,
    pd_ref, pc_ref, rl_ref, context_ref, bias_d, bias_c,
):
    count = q_ref.shape[2]
    step = count // 2

    @pl.when(pl.program_id(0) == 0)
    def _():
        row = lax.broadcasted_iota(jnp.int32, (count, count), 0)
        col = lax.broadcasted_iota(jnp.int32, (count, count), 1)
        spread = jnp.broadcast_to(pos_ref[...].astype(F32), (8, count))
        start = row - jnp.transpose(spread)[:, :1].astype(jnp.int32)
        bias_d[...] = jnp.where((col <= row) & (col >= start), 0.0, HIDE)
        bias_c[...] = jnp.where(col >= start + count, 0.0, HIDE)

    lane = lax.broadcasted_iota(jnp.int32, (1, PAIR), 1) // HEAD_DIM

    def half(late):
        blocks = [(at, a) for at in (0, step) for a in (0, 1)]
        for a in (0, 1):
            pd_ref[0, a, :step, step:] = jnp.zeros((step, step), BF)
        scores = []
        for at, a in blocks:
            rows, keys = pl.ds(at, step), at + step
            mine = jnp.where(lane == a, q_ref[0, 0, rows, :] * 0.125, 0.0).astype(BF)
            s_d = dot_nt(mine, kd_ref[0, 0, :keys, :]) + bias_d[rows, :keys]
            s_c = dot_nt(mine, kc_ref[0, 0]) + bias_c[rows, :] if late else None
            scores.append((s_d, s_c))
        mixed, scale = {}, {}
        for (at, a), (s_d, s_c) in zip(blocks, scores):
            rows, keys = pl.ds(at, step), at + step
            top = jnp.max(s_d, axis=-1, keepdims=True)
            if late:
                top = jnp.maximum(top, jnp.max(s_c, axis=-1, keepdims=True))
            p_d = jnp.exp(s_d - top)
            total = jnp.sum(p_d, axis=-1, keepdims=True)
            p_d = p_d.astype(BF)
            pd_ref[0, a, rows, :keys] = p_d
            value = jnp.where(lane == a, vd_ref[0, 0, :keys, :], 0.0).astype(BF)
            mix = dot(p_d, value)
            if late:
                p_c = jnp.exp(s_c - top)
                total = total + jnp.sum(p_c, axis=-1, keepdims=True)
                p_c = p_c.astype(BF)
                pc_ref[0, a, rows, :] = p_c
                value = jnp.where(lane == a, vc_ref[0, 0], 0.0).astype(BF)
                mix = mix + dot(p_c, value)
            mixed[at, a], scale[at, a] = mix, 1.0 / total
        for at in (0, step):
            rows = pl.ds(at, step)
            inverse = jnp.where(lane == 0, scale[at, 0], scale[at, 1])
            rl_ref[0, rows, :] = inverse
            context_ref[rows, :] = ((mixed[at, 0] + mixed[at, 1]) * inverse).astype(BF)

    pl.when(which_ref[0] == 0)(lambda: half(False))
    pl.when(which_ref[0] == 1)(lambda: half(True))


def attend(which, projected, positions, earlier, after=(), flops=1):
    _, _, count, cols = projected.shape
    heads = cols // HEAD_DIM

    def block(part, other):
        if other:
            return pl.BlockSpec((1, 1, count, PAIR), lambda g, w: (part, 0, 0, g))
        return pl.BlockSpec((1, 1, count, PAIR), lambda g, w: (part, w[0], 0, g))

    score_spec = pl.BlockSpec((1, 2, count, count), lambda g, w: (w[0], g, 0, 0))
    return call(
        attend_kernel,
        [*[projected] * 5, positions],
        after=after,
        alias=earlier,
        prefetch=[which],
        flops=flops,
        grid=(cols // PAIR,),
        in_specs=[
            block(0, False),
            block(1, False),
            block(2, False),
            block(1, True),
            block(2, True),
            whole((1, count)),
        ],
        out_specs=[
            score_spec,
            score_spec,
            pl.BlockSpec((1, count, PAIR), lambda g, w: (w[0], 0, g)),
            pl.BlockSpec((count, PAIR), lambda g, w: (0, g)),
        ],
        scratch_shapes=[pltpu.VMEM((count, count), F32)] * 2,
        out_shape=[
            shaped((2, heads, count, count), BF),
            shaped((2, heads, count, count), BF),
            shaped((2, count, cols), F32),
            shaped((count, cols), BF),
        ],
        name="attend",
    )


def hidden_kernel(
    x_ref, own_ref, got_ref, own_weight_ref, got_weight_ref, gain_ref, slot_ref, hidden_ref, *out_refs
):
    attended = dot(own_ref[...], own_weight_ref[...]) + dot(got_ref[...], got_weight_ref[...])
    hidden = x_ref[...].astype(F32) + attended
    hidden_ref[...] = hidden
    normed, _ = norm_parts(hidden)
    second = (normed * row_of(gain_ref)).astype(BF)
    send_rows(second, slot_ref, out_refs)


def send_rows(rows, slot_ref, out_refs):
    capacity = out_refs[0].shape[0]
    for k, ref in enumerate(out_refs):
        slot = lax.broadcasted_iota(jnp.int32, (capacity, rows.shape[0]), 0) + k * capacity
        place = jnp.where(slot_ref[...] == slot, 1.0, 0.0).astype(BF)
        ref[...] = dot(place, rows).astype(BF)


def hidden_rows(x, own, got, own_weight, got_weight, gain, slot_row, experts, after=()):
    count, width = x.shape
    out = [shaped((count, width), F32)] + [shaped((count // 2, width), BF)] * experts
    return plain(
        hidden_kernel,
        [x, own, got, own_weight, got_weight, gain, slot_row],
        out,
        "hidden_rows",
        after,
    )


def send_kernel(rows_ref, slot_ref, weight_ref, out_ref, weight_out):
    send_rows(rows_ref[...], slot_ref, [out_ref.at[k] for k in range(out_ref.shape[0])])
    weight_out[...] = weight_ref[...]


def sent_rows(rows, slot_row, weight, experts, after=()):
    count, width = rows.shape
    out = [shaped((experts, count // 2, width), BF), shaped(weight.shape, BF)]
    return plain(send_kernel, [rows, slot_row, weight], out, "sent_rows", after)


def taken_rows(slot_ref, block_refs):
    count, capacity = slot_ref.shape[1], block_refs[0].shape[0]
    total = 0.0
    for k, ref in enumerate(block_refs):
        slot = lax.broadcasted_iota(jnp.int32, (capacity, count), 0) + k * capacity
        place = jnp.where(slot_ref[...] == slot, 1.0, 0.0).astype(BF)
        total = total + lax.dot_general(
            place, ref[...], (((0,), (0,)), ((), ())), preferred_element_type=F32
        )
    return total


def output_kernel(hidden_ref, slot_ref, *refs):
    blocks = [refs[0].at[k] for k in range(refs[0].shape[0])]
    refs[-1][...] = (hidden_ref[...] + taken_rows(slot_ref, blocks)).astype(BF)


def output_rows(hidden, slot_row, blocks, after=()):
    return plain(
        output_kernel,
        [hidden, slot_row, blocks],
        shaped(hidden.shape, BF),
        "output_rows",
        after,
        flops=FIRST_FLOPS,
    )


def second_kernel(cot_ref, hidden_ref, gain_ref, slot_ref, own_weight_ref, got_weight_ref, *refs):
    grad_ref, low_ref, gain_grad_ref, own_ref, send_ref = refs[-5:]
    second_grad = taken_rows(slot_ref, refs[:-5])
    normed, scale = norm_parts(hidden_ref[...])
    gain_grad_ref[...] = jnp.sum(second_grad * normed, axis=0, keepdims=True)
    grad = cot_ref[...].astype(F32) + norm_back(second_grad * row_of(gain_ref), normed, scale)
    grad_ref[...] = grad
    low = grad.astype(BF)
    low_ref[...] = low
    send_ref[...] = dot_nt(low, got_weight_ref[...]).astype(BF)
    own_ref[...] = dot_nt(low, own_weight_ref[...]).astype(BF)


def second_back(cot, hidden, gain, slot_row, own_weight, got_weight, blocks, after=()):
    count, width = hidden.shape
    part = shaped((count, own_weight.shape[0]), BF)
    out = [
        shaped((count, width), F32),
        shaped((count, width), BF),
        shaped((1, width), F32),
        part,
        part,
    ]
    return plain(
        second_kernel,
        [cot, hidden, gain, slot_row, own_weight, got_weight, *blocks],
        out,
        "second_back",
        after,
        flops=BACK_FLOPS,
    )


def output_weight_kernel(
    core_ref, own_ref, got_ref, low_ref, own_out, kept_out, sent_out, scratch
):
    def part(ref):
        return lax.dot_general(
            ref[...], low_ref[...], (((0,), (0,)), ((), ())), preferred_element_type=F32
        ).astype(BF)

    scratch[...] = part(got_ref)
    rows = kept_out.shape[0]
    for ref, half in ((kept_out, core_ref[0]), (sent_out, 1 - core_ref[0])):
        ref[...] = scratch[pl.ds(pl.multiple_of(half * rows, rows), rows), :]
    own_out[...] = part(own_ref)


def output_weight_parts(core, own, got, low, after=()):
    cols, width = own.shape[1], low.shape[1]
    part = shaped((cols // 2, width), BF)
    out = [shaped((cols, width), BF), part, part]
    return call(
        output_weight_kernel,
        [own, got, low],
        after=after,
        prefetch=[core],
        grid=(1,),
        in_specs=[whole(x.shape) for x in (own, got, low)],
        out_specs=[whole(o.shape) for o in out],
        out_shape=out,
        scratch_shapes=[pltpu.VMEM((cols, width), BF)],
        name="output_weight_parts",
    )


def first_kernel(x_ref, gain_ref, hidden_grad_ref, own_ref, theirs_ref, out_ref):
    grad = (own_ref[...] + theirs_ref[...].astype(F32)) * row_of(gain_ref)
    normed, scale = norm_parts(x_ref[...].astype(F32))
    out_ref[...] = hidden_grad_ref[...] + norm_back(grad, normed, scale)


def first_back(x, gain, hidden_grad, own, theirs, after=()):
    return plain(
        first_kernel,
        [x, gain, hidden_grad, own, theirs],
        shaped(x.shape, F32),
        "first_back",
        after,
    )


def fill(target, refs):
    rows = refs[0].shape[0]
    for i, ref in enumerate(refs):
        target[i * rows : (i + 1) * rows] = ref[...]


def expert_kernel(count, sub, place_ref, *refs):
    x_refs, cot_refs, refs = refs[:count], refs[count : 2 * count], refs[2 * count :]
    inner_ref, outer_ref, act_ref, pre_ref, out_ref, *grad_refs, x, cot, grad_acc, out_acc = refs
    at = pl.program_id(0)
    last = pl.num_programs(0) - count
    size = out_ref.shape[1]

    @pl.when(at > last)
    def _():
        rows = pl.ds(pl.multiple_of((at - last) * size, size), size)
        out_ref[0] = out_acc[rows, :].astype(BF)

    pl.when(at <= last)(
        lambda: expert_step(
            count, sub, x_refs, cot_refs, inner_ref, outer_ref, act_ref, pre_ref, out_ref,
            grad_refs, x, cot, grad_acc, out_acc, at, last,
        )
    )


def expert_step(
    count, sub, x_refs, cot_refs, inner_ref, outer_ref, act_ref, pre_ref, out_ref, grad_refs,
    x, cot, grad_acc, out_acc, at, last,
):

    @pl.when(at == 0)
    def _():
        fill(x, x_refs)
        fill(cot, [ref.at[0] for ref in cot_refs])
        grad_acc[...] = jnp.zeros_like(grad_acc)
        out_acc[...] = jnp.zeros_like(out_acc)

    def front(i):
        cols = slice(i * sub, (i + 1) * sub)
        return dot(x[...], inner_ref[:, cols]), dot_nt(cot[...], outer_ref[cols, :])

    parts = inner_ref.shape[1] // sub
    now = front(0)
    for i in range(parts):
        later = front(i + 1) if i + 1 < parts else None
        value, grad = now
        square = value * value
        half = 0.5 + 0.5 * jnp.tanh(
            value * (0.7978845608028654 + 0.035677408136300125 * square)
        )
        act = value * half
        slope = half + act * (1.0 - half) * (1.5957691216057308 + 0.21406444881780074 * square)
        cols = slice(i * sub, (i + 1) * sub)
        act_ref[:, cols] = act.astype(BF)
        pre_ref[:, cols] = (grad * slope).astype(BF)
        now = later
    grad_acc[...] += dot_nt(pre_ref[...], inner_ref[...])
    out_acc[...] += dot(act_ref[...], outer_ref[...])

    @pl.when(at == last)
    def _():
        size = out_ref.shape[1]
        out_ref[0] = out_acc[:size].astype(BF)
        for i, ref in enumerate(grad_refs):
            ref[...] = grad_acc[i * size : (i + 1) * size].astype(BF)


def expert(place, index, blocks, cot, inner, outer, earlier, after=(), tile=1536, sub=256):
    count, width = blocks[0].shape
    size, units = len(blocks), inner.shape[1]
    total = count * cot.shape[0]
    tiles = units // tile

    def held(j):
        return jnp.minimum(j, tiles - 1)

    wide = pl.BlockSpec((count * size, tile), lambda j, p: (index // size, held(j)))
    out = pl.BlockSpec(
        (1, count, width), lambda j, p: (p[jnp.maximum(j - tiles + 1, 0)], 0, 0)
    )

    def placed(i):
        return pl.BlockSpec((1, count, width), lambda j, p: (p[i], 0, 0))

    return call(
        functools.partial(expert_kernel, size, sub),
        [*blocks, *[cot] * size, inner, outer],
        after=after,
        flops=EXPERT_FLOPS,
        alias=earlier,
        prefetch=[place],
        grid=(tiles + size - 1,),
        in_specs=[whole((count, width))] * size
        + [placed(i) for i in range(size)]
        + [
            pl.BlockSpec((width, tile), lambda j, p: (0, held(j))),
            pl.BlockSpec((tile, width), lambda j, p: (held(j), 0)),
        ],
        out_specs=[wide, wide, out] + [whole((count, width))] * size,
        out_shape=[shaped((total, units), BF)] * 2
        + [shaped(cot.shape, BF)]
        + [shaped((count, width), BF)] * size,
        scratch_shapes=[pltpu.VMEM((count * size, width), BF)] * 2
        + [pltpu.VMEM((count * size, width), F32)] * 2,
        name="expert",
    )


def weight_kernel(is_outer, count, added, info_ref, wide_ref, *refs):
    row_count = 1 if is_outer else count
    row_refs, refs = refs[:row_count], refs[row_count:]
    if is_outer:
        row_refs = [row_refs[0].at[info_ref[ORDER + i]] for i in range(count)]
    got_ref = refs[0] if added else None
    *out_refs, rows = refs[1:] if added else refs
    at = pl.program_id(0)
    pl.when(at == 0)(lambda: fill(rows, row_refs))

    def put(out_ref):
        sides = (wide_ref[...], rows[...]) if is_outer else (rows[...], wide_ref[...])
        part = lax.dot_general(*sides, (((0,), (0,)), ((), ())), preferred_element_type=F32)
        if added:
            part = part + got_ref[...].astype(F32)
        out_ref[...] = part.astype(BF)

    if added:
        for i, out_ref in enumerate(out_refs):
            pl.when(at == i)(functools.partial(put, out_ref))
    else:
        put(out_refs[0])


def weight_part(info, is_outer, half, turn, blocks, wide, got=None, after=()):
    total, units = wide.shape
    width, added, tile = blocks[0].shape[1], got is not None, units // 4
    count = len(blocks) if not is_outer else blocks.shape[0]
    if is_outer:
        row_specs, blocks = [whole(blocks.shape)], [blocks]
    else:
        row_specs = [whole(block.shape) for block in blocks]

    def at(j):
        return (j, 0) if is_outer else (0, j)

    def place(j, w):
        return (w[turn] + j) % 2

    def shape(units):
        return (units, width) if is_outer else (width, units)

    block = pl.BlockSpec(shape(tile), lambda j, w: at(place(j, w)))
    if added:
        out, out_specs = [shaped(shape(tile), BF)] * 2, [whole(shape(tile))] * 2
    else:
        out, out_specs = [shaped(shape(2 * tile), BF)], [block]
    return call(
        functools.partial(weight_kernel, is_outer, count, added),
        [wide, *blocks] + ([got] if added else []),
        after=after,
        prefetch=[info],
        grid=(2,),
        in_specs=[pl.BlockSpec((total, tile), lambda j, w: (0, w[half] * 2 + place(j, w)))]
        + row_specs
        + ([block] if added else []),
        out_specs=out_specs,
        out_shape=out,
        scratch_shapes=[pltpu.VMEM((total, width), BF)],
        name="weight_part",
    )


def assemble_kernel(counts, info_ref, *refs):
    piece_refs, out_refs = refs[: sum(counts)], refs[sum(counts) :]
    targets = [out for out, count in zip(out_refs, counts) for _ in range(count)]
    for i, (ref, out_ref) in enumerate(zip(piece_refs, targets)):

        @pl.when(pl.program_id(0) == i)
        def _(ref=ref, out_ref=out_ref):
            out_ref[...] = ref[...].astype(F32)


def assemble(info, start, groups, shapes, earlier, after=()):
    counts = [len(pieces) for pieces in groups]
    pieces = [piece for group in groups for piece in group]
    size = pieces[0].shape

    def spec(first, count):
        def at(i, t):
            held = start + 2 * jnp.clip(i, first, first + count - 1)
            return t[held], t[held + 1]

        return pl.BlockSpec(size, at)

    firsts = [sum(counts[:i]) for i in range(len(counts))]
    return call(
        functools.partial(assemble_kernel, counts),
        pieces,
        after=after,
        alias=earlier,
        prefetch=[info],
        grid=(len(pieces),),
        in_specs=[whole(size)] * len(pieces),
        out_specs=[spec(first, count) for first, count in zip(firsts, counts)],
        out_shape=[shaped(shape, F32) for shape in shapes],
        name="assemble",
    )


def add_kernel(kept_ref, got_ref, out_ref):
    out_ref[...] = (kept_ref[...].astype(F32) + got_ref[...].astype(F32)).astype(BF)


def add(kept, got):
    return plain(add_kernel, [kept, got], shaped(kept.shape, BF), "add")


def gather_sum_kernel(kept_ref, got_ref, more_ref, out_ref, tail_ref):
    rows, more = out_ref.shape[0], more_ref.shape[0]
    first = rows - more
    out_ref[:first] = (kept_ref[:first].astype(F32) + got_ref[:first].astype(F32)).astype(BF)
    last = kept_ref[first:rows].astype(F32) + got_ref[first:rows].astype(F32)
    out_ref[first:] = (last + more_ref[...].astype(F32)).astype(BF)
    tail_ref[...] = (kept_ref[rows:].astype(F32) + got_ref[rows:].astype(F32)).astype(BF)


def gather_sum(kept, got, more, rows, after=()):
    lines, width = kept.shape
    out = [shaped((rows, width), BF), shaped((lines - rows, width), BF)]
    return plain(gather_sum_kernel, [kept, got, more], out, "gather_sum", after)


def adds_kernel(start, count, cuts, whole_sum, info_ref, *refs):
    in_refs, out_refs = refs[: 2 * count], refs[2 * count :]
    for i in range(count):
        kept_ref, got_ref = in_refs[2 * i : 2 * i + 2]
        for j in range(cuts):
            ref = out_refs[cuts * i + j]
            rows = ref.shape[0]
            at = 0 if whole_sum else info_ref[start + cuts * i + j]
            cut = pl.ds(pl.multiple_of(at * rows, rows), rows)
            ref[...] = (kept_ref[cut, :].astype(F32) + got_ref[cut, :].astype(F32)).astype(BF)


def adds(info, start, pairs, cuts, whole_sum=False, after=()):
    out = [
        shaped((kept.shape[0] // (1 if whole_sum else cuts), kept.shape[1]), BF)
        for kept, _ in pairs
        for _ in range(cuts)
    ]
    operands = [x for pair in pairs for x in pair]
    parts = call(
        functools.partial(adds_kernel, start, len(pairs), cuts, whole_sum),
        operands,
        after=after,
        prefetch=[info],
        grid=(1,),
        in_specs=[whole(x.shape) for x in operands],
        out_specs=[whole(o.shape) for o in out],
        out_shape=out,
        name="adds",
    )
    return [parts[cuts * i : cuts * (i + 1)] for i in range(len(pairs))]


def piece_places(steps, order):
    weights = {step: 1 << (len(steps) - 1 - i) for i, step in enumerate(steps)}
    place = sum(side(*step) * weight for step, weight in weights.items())
    places, newest = [place], [(0, place)]
    while newest:
        newest = [
            (i + 1, at + weights[order[i]] * (1 - 2 * side(*order[i])))
            for first, at in newest
            for i in range(first, len(order))
        ]
        places += [at for _, at in newest]
    return places


def gather_pieces(own, steps, order, flops, after):
    pieces, newest = [own], [(0, own)]
    while newest:
        found = [
            (i + 1, swap(piece, *order[i], "piece"))
            for first, piece in newest
            for i in range(first, len(order))
        ]
        if len(pieces) == 1:
            held = touch([piece for _, piece in found], after, flops=flops)
            found = [(first, piece) for (first, _), piece in zip(found, held)]
        pieces += [piece for _, piece in found]
        newest = found
    return list(zip(piece_places(steps, order), pieces))


def total_kernel(in_ref, tail_ref, got_ref, out_ref):
    count, rows = in_ref.shape[:2]
    value = sum(in_ref[i].astype(F32) for i in range(count)).astype(BF)
    tail = sum(ref[i : i + 1].astype(F32) for ref in (tail_ref, got_ref) for i in (0, 1))
    high = tail.astype(BF).astype(F32)
    line = lax.broadcasted_iota(jnp.int32, tail_ref.shape, 0)
    tail = jnp.where(line == 0, high, jnp.where(line == 1, tail - high, 0.0)).astype(BF)
    for i in range(count):
        out_ref[i, :rows] = value
        out_ref[i, rows:] = tail


def total(blocks, tail, got, after=()):
    count, rows, width = blocks.shape
    out = shaped((count, rows + tail.shape[0], width), BF)
    return plain(total_kernel, [blocks, tail, got], out, "total", after)


def halves(step):
    mine = side(*step)
    return [1 - mine, mine]


def touch_kernel(*out_refs):
    pass


def touch(values, after, flops=1):
    return call(
        touch_kernel,
        [],
        after=after,
        alias=values,
        flops=flops,
        in_specs=[],
        out_specs=[pl.BlockSpec(memory_space=pl.ANY)] * len(values),
        out_shape=[shaped(x.shape, x.dtype) for x in values],
        name="touch",
    )


def back_kernel(
    at_ref, own_ref, other_ref, q_ref, k_ref, v_ref, pd_ref, pc_ref, own_context_ref,
    other_context_ref, rl_ref, first_ref, wp_ref, gain_ref, second_ref, own_output_ref,
    sent_ref, kept_ref, mine_ref, theirs_ref,
    acc, scaled, through, key_acc, value_acc, queries, weights, scores,
):
    group = pl.program_id(0)
    count = own_ref.shape[0]
    step = count // 2
    me, core = at_ref[0], at_ref[CORE]
    lane = lax.broadcasted_iota(jnp.int32, (1, PAIR), 1) // HEAD_DIM

    for ref, context, at in (
        (own_ref, own_context_ref, me),
        (other_ref, other_context_ref, 1 - me),
    ):
        grad = ref[...].astype(F32) * rl_ref[at]
        scaled[at] = grad
        through[at] = grad.astype(BF).astype(F32) * context[...].astype(F32)
    @pl.when(group == 0)
    def _():
        for h in (0, 1):
            for a in (0, 1):
                scores[h, a, :step, step:] = jnp.zeros((step, step), BF)

    for h in (0, 1):
        for at in (0, step):
            rows = pl.ds(at, step)
            low = scaled[h, rows, :].astype(BF)
            query = 0.0
            for a in (0, 1):
                mine = jnp.where(lane == a, low, 0.0).astype(BF)
                along = jnp.sum(
                    jnp.where(lane == a, through[h, rows, :], 0.0), axis=-1, keepdims=True
                )
                parts = [(pd_ref, h, h, at + step)]
                if h:
                    parts.append((pc_ref, 0, 2, count))
                for p_ref, p_at, to, keys in parts:
                    source = 0 if to == 2 else h
                    prob_grad = dot_nt(mine, v_ref[0, source, :keys, :])
                    p = p_ref[p_at, a, rows, :keys]
                    score = (p.astype(F32) * (prob_grad - along)).astype(BF)
                    scores[to, a, rows, :keys] = score
                    k = jnp.where(lane == a, k_ref[0, source, :keys, :], 0.0).astype(BF)
                    query = query + dot(score, k)
            queries[pl.ds(h * count + at, step), :] = query * 0.125
    low_t = [jnp.transpose(scaled[h]).astype(BF) for h in (0, 1)]
    q_t = [jnp.transpose(q_ref[0, h].astype(F32)).astype(BF) for h in (0, 1)]
    for a in (0, 1):
        line = slice(a * HEAD_DIM, (a + 1) * HEAD_DIM)
        key_acc[line, :count] = dot(q_t[0][line], scores[0, a]) + dot(q_t[1][line], scores[2, a])
        key_acc[line, count:] = dot(q_t[1][line], scores[1, a])
        value_acc[line, :count] = dot(low_t[0][line], pd_ref[0, a]) + dot(
            low_t[1][line], pc_ref[0, a]
        )
        value_acc[line, count:] = dot(low_t[1][line], pd_ref[1, a])

    query = queries[...]
    key_t = key_acc[...] * 0.125
    value_t = value_acc[...]
    both = jnp.concatenate(
        [query.astype(BF), jnp.transpose(key_t).astype(BF), jnp.transpose(value_t).astype(BF)],
        axis=1,
    )
    both_t = jnp.concatenate(
        [jnp.transpose(query).astype(BF), key_t.astype(BF), value_t.astype(BF)], axis=0
    )
    first = jnp.concatenate([first_ref[0], first_ref[1]], axis=0)
    weights[...] = dot(both_t, first)
    size = 3 * PAIR // 2
    groups = pl.num_programs(0)
    here = pl.ds(pl.multiple_of(group * size, size), size)
    for ref, half in ((sent_ref, 1 - core), (kept_ref, core)):
        ref[here, :] = weights[pl.ds(pl.multiple_of(half * size, size), size), :].astype(BF)
    weight = jnp.concatenate([wp_ref[0], wp_ref[1], wp_ref[2]], axis=1)
    added = dot_nt(both, weight)

    @pl.when(group == 0)
    def _():
        for h in (0, 1):
            acc[h] = added[h * count : (h + 1) * count]

    @pl.when(group > 0)
    def _():
        for h in (0, 1):
            acc[h] += added[h * count : (h + 1) * count]

    @pl.when(group == groups - 1)
    def _():
        mine_ref[...] = acc[me]
        theirs_ref[...] = acc[1 - me].astype(BF)
        gain = 0.0
        for h in (0, 1):
            gain = gain + jnp.sum(acc[h] * first_ref[h].astype(F32), axis=0, keepdims=True)
        gain = gain / row_of(gain_ref)
        part = own_output_ref.shape[0] // 2
        at = groups * size
        end = at + part
        for ref, half in ((sent_ref, 1 - core), (kept_ref, core)):
            cut = pl.ds(pl.multiple_of(half * part, part), part)
            ref[at:end, :] = own_output_ref[cut, :]
            value = jnp.where(half == 0, gain, second_ref[...])
            high = value.astype(BF).astype(F32)
            line = lax.broadcasted_iota(jnp.int32, (ref.shape[0] - end, value.shape[1]), 0)
            tail = jnp.where(line == 0, high, jnp.where(line == 1, value - high, 0.0))
            ref[end:, :] = tail.astype(BF)


def attend_back(
    at, own, other, projected, p_diag, p_cross, own_context, other_context, inverse, first, weight,
    gain, second, own_output, lines, after=(),
):
    _, _, count, cols = projected.shape
    width = first.shape[2]
    rows = whole((count, width))
    pair = pl.BlockSpec((count, PAIR), lambda g, w: (0, g))

    def block(part):
        return pl.BlockSpec((1, 2, count, PAIR), lambda g, w: (part, 0, 0, g))

    sent = shaped((lines, width), BF)
    out = [sent, sent, shaped((count, width), F32), shaped((count, width), BF)]
    return call(
        back_kernel,
        [
            own, other, projected, projected, projected, p_diag, p_cross, own_context,
            other_context, inverse, first, weight, gain, second, own_output,
        ],
        after=after,
        flops=ATTBACK_FLOPS,
        prefetch=[at],
        grid=(cols // PAIR,),
        in_specs=[
            pair,
            pair,
            block(0),
            block(1),
            block(2),
            pl.BlockSpec((2, 2, count, count), lambda g, w: (0, g, 0, 0)),
            pl.BlockSpec((1, 2, count, count), lambda g, w: (1, g, 0, 0)),
            pair,
            pair,
            pl.BlockSpec((2, count, PAIR), lambda g, w: (0, 0, g)),
            whole((2, count, width)),
            pl.BlockSpec((3, width, PAIR), lambda g, w: (0, 0, g)),
            whole((width,)),
            whole((1, width)),
            whole((cols, width)),
        ],
        out_specs=[whole(o.shape) for o in out],
        scratch_shapes=[
            pltpu.VMEM((2, count, width), F32),
            pltpu.VMEM((2, count, PAIR), F32),
            pltpu.VMEM((2, count, PAIR), F32),
            pltpu.VMEM((PAIR, 2 * count), F32),
            pltpu.VMEM((PAIR, 2 * count), F32),
            pltpu.VMEM((2 * count, PAIR), F32),
            pltpu.VMEM((3 * PAIR, width), F32),
            pltpu.VMEM((3, 2, count, count), BF),
        ],
        out_shape=out,
        name="attend_back",
    )


def weight_outputs_kernel(rows, core_ref, kept_ref, got_ref, project_ref, output_ref, *gain_refs):
    group, groups = pl.program_id(0), pl.num_programs(0)
    size = 3 * PAIR // 2

    def halves_of(cut, which):
        kept, got = [
            jnp.concatenate([ref[block, cut, :] for block in which], axis=0).astype(F32)
            for ref in (kept_ref, got_ref)
        ]
        low = jnp.where(core_ref[0] == 0, kept, got)
        return low, jnp.where(core_ref[0] == 0, got, kept)

    body, blocks = slice(0, rows), size // rows
    low, high = halves_of(body, [group * blocks + i for i in range(blocks)])
    flat = jnp.transpose(jnp.concatenate([low, high], axis=0))
    for c in range(3):
        project_ref[c] = flat[:, c * PAIR : (c + 1) * PAIR]

    @pl.when(group == groups - 1)
    def _():
        part, count = output_ref.shape[0] // 2, kept_ref.shape[0]
        first = groups * size // rows
        output_ref[:part], output_ref[part:] = halves_of(body, range(first, count))
        tails = halves_of(slice(rows, rows + 16), range(count))
        for i, tail in enumerate(tails):
            gain_refs[i][...] = sum(
                tail[16 * b : 16 * b + 1] + tail[16 * b + 1 : 16 * b + 2] for b in range(count)
            )[0]


def weight_outputs(core, kept, got, cols, after=()):
    _, rows, width = kept.shape
    return call(
        functools.partial(weight_outputs_kernel, rows - 16),
        [kept, got],
        after=after,
        prefetch=[core],
        grid=(cols // PAIR,),
        in_specs=[whole(kept.shape)] * 2,
        out_specs=[
            pl.BlockSpec((3, width, PAIR), lambda g, w: (0, 0, g)),
            whole((cols, width)),
            whole((width,)),
            whole((width,)),
        ],
        out_shape=[shaped((3, width, cols), F32), shaped((cols, width), F32)]
        + [shaped((width,), F32)] * 2,
        name="weight_outputs",
    )


def on_device(
    block_input,
    output_cotangent,
    token_ids,
    positions,
    hash_table,
    first_gain,
    second_gain,
    project_weight,
    output_weight,
    expert_inner,
    expert_outer,
):
    tok_rows, model_width = block_input.shape
    local_cols = output_weight.shape[0]
    expert_count = lax.axis_size("expert")
    capacity = tok_rows // 2
    inner_weight = expert_inner[0]
    outer_weight = expert_outer[0]
    my_head = lax.axis_index("head")
    my_expert = lax.axis_index("expert")
    core = lax.axis_index("core")
    turns = bits_of("x") + bits_of("head")
    outer_steps, inner_steps = turns, turns[::-1]
    order = [my_expert ^ k for k in range(expert_count)]

    early = len(turns) + 1
    entries = [
        my_head, 1 - my_head, core, 1 - core, 0 * core,
        1 - side(*outer_steps[0]), 1 - side(*inner_steps[0]), *order,
    ]
    adds_at = [len(entries) + 4 * i for i in range(len(turns) - 1)]
    for i in range(1, len(turns)):
        entries += [*halves(outer_steps[i]), *halves(inner_steps[i])]
    half = 1 << (len(turns) - 1)

    def placed(place, which, is_outer):
        if is_outer:
            return [which * 2 * half + place, 0 * place]
        return [place % half, which * 2 + place // half]

    piece_at = []
    for chosen in (slice(early), slice(early, None)):
        for steps, is_outer in ((outer_steps, True), (inner_steps, False)):
            piece_at.append(len(entries))
            for which in (core, 1 - core):
                for place in piece_places(steps, steps[::-1])[chosen]:
                    entries += placed(place, which, is_outer)
    info = jnp.stack(entries).astype(jnp.int32)
    own_at, core_at = my_head.reshape(1).astype(jnp.int32), core.reshape(1).astype(jnp.int32)
    other_at = 1 - own_at

    other_input = swap(block_input, "head", 1, "rows")
    other_pos = swap(positions, "head", 1, "positions")

    chosen = jnp.take(hash_table, token_ids)
    relative = chosen ^ my_expert
    one_hot = relative[:, None] == jnp.arange(expert_count, dtype=jnp.int32)[None, :]
    rank_table = jnp.cumsum(one_hot.astype(jnp.int32), axis=0) - 1
    slot_index = relative * capacity + jnp.sum(jnp.where(one_hot, rank_table, 0), axis=1)
    slot_row = slot_index[None, :]
    absolute = slot_index + (chosen - relative) * capacity

    def exchange(blocks, name, first=0):
        return [
            swap(block, "expert", k, f"{name}{k}") if k else block
            for k, block in enumerate(blocks, first)
        ]

    def exchange_all(blocks):
        return lax.all_to_all(blocks, "expert", split_axis=0, concat_axis=0, tiled=True)

    done = project(own_at, block_input, first_gain, project_weight, [])
    sent, weight_sent = sent_rows(
        output_cotangent, absolute[None, :], output_weight, expert_count, after=[done[0], other_pos]
    )
    grad_blocks = exchange_all(sent)
    first_low, projected = project(other_at, other_input, first_gain, project_weight, done)
    other_weight = swap(weight_sent, "head", 1, "output_weight")
    *done, other_context = attend(other_at, projected, other_pos[None, :], [])
    got_context = swap(other_context, "head", 1, "context")
    p_diag, p_cross, inverse, own_context = attend(
        own_at,
        projected,
        positions[None, :],
        done,
        after=[other_weight],
        flops=ATTEND_FLOPS,
    )
    hidden, *outgoing = hidden_rows(
        block_input,
        own_context,
        got_context,
        output_weight,
        other_weight,
        second_gain,
        slot_row,
        expert_count,
    )

    row_blocks = exchange(outgoing, "dispatch")
    done, returned, at = [], [], 0
    while at < expert_count:
        size = 1
        parts = expert(
            order[at].reshape(1).astype(jnp.int32), at, row_blocks[at : at + size], grad_blocks if at else sent, inner_weight,
            outer_weight, done,
        )
        done, grads = parts[:3], parts[3:]
        returned += exchange(grads, "return", at)
        at += size
    activated, pre_grad, produced = done

    (outer_sent,) = weight_part(info, True, OTHER_CORE, NONE, grad_blocks, activated, after=grads)
    outer_got = swap(outer_sent, "core", 1, "outer_core")
    (inner_sent,) = weight_part(
        info, False, OTHER_CORE, NONE, row_blocks, pre_grad, after=[outer_sent]
    )
    inner_got = swap(inner_sent, "core", 1, "inner_core")
    token = touch([jnp.zeros((8, 128), F32)], [inner_sent], flops=BACK_FLOPS)
    outer_parts = weight_part(
        info, True, CORE, OUTER_TURN, grad_blocks, activated, outer_got, after=token
    )
    inner_parts = weight_part(
        info, False, CORE, INNER_TURN, row_blocks, pre_grad, inner_got, after=[outer_parts[0]]
    )

    hidden_grad, hidden_low, second_gain_part, own_grad, grad_sent = second_back(
        output_cotangent,
        hidden,
        second_gain,
        slot_row,
        output_weight,
        other_weight,
        returned,
        after=[inner_parts[0]],
    )
    other_grad = swap(grad_sent, "head", 1, "context_grad")
    def pairs_of(outer, inner, i):
        return [
            (outer[1], swap(outer[0], *outer_steps[i], f"outer{i}")),
            (inner[1], swap(inner[0], *inner_steps[i], f"inner{i}")),
        ]

    own_output, output_kept, output_sent = output_weight_parts(
        core_at, own_context, got_context, hidden_low, after=[grad_sent]
    )
    output_sent = add(output_kept, swap(output_sent, "core", 1, "output_core"))
    combined = exchange_all(touch([produced], [output_sent])[0])
    got_output = swap(output_sent, "head", 1, "output_grad")

    groups = local_cols // PAIR
    end = 2 * local_cols
    lines = end + 16
    sent, kept, mine, theirs = attend_back(
        info, own_grad, other_grad, projected, p_diag,
        p_cross, own_context, other_context, inverse, first_low, project_weight, first_gain,
        second_gain_part, own_output, lines, after=[inner_parts[0]],
    )
    at = 3 * local_cols // 2
    more = touch([got_output], [kept], flops=BACK_FLOPS)
    got = swap(sent, "core", 1, "weight")
    summed, tail = gather_sum(kept, got, more[0], end, after=more)
    crowd = ("x", "expert")
    summed = summed.reshape(-1, end // lax.axis_size(crowd), model_width)
    arrived = lax.all_to_all(summed, crowd, split_axis=0, concat_axis=0, tiled=True)
    for i in range(len(turns) - 1):
        outer_parts, inner_parts = adds(
            info, adds_at[i], pairs_of(outer_parts, inner_parts, i), 2, after=[summed]
        )
    block_output = output_rows(hidden, absolute[None, :], combined, after=outer_parts)
    got_tail = swap(tail, "head", 1, "gains")
    theirs = swap(touch([theirs], [got_tail])[0], "head", 1, "theirs")
    (outer_own, outer_copy), (inner_own, inner_copy) = adds(
        info, 0, pairs_of(outer_parts, inner_parts, -1), 2, True, after=[block_output, got_tail]
    )
    arrived = total(
        arrived, tail, got_tail, after=[outer_own, inner_own]
    )
    input_grad = first_back(
        block_input, first_gain, hidden_grad, mine, theirs, after=[arrived]
    )
    outer_pieces = gather_pieces(outer_own, outer_steps, outer_steps[::-1], BACK_FLOPS, [input_grad])
    inner_pieces = gather_pieces(inner_own, inner_steps, inner_steps[::-1], 1, [input_grad])
    summed = lax.all_to_all(arrived, crowd, split_axis=0, concat_axis=0, tiled=True)

    def core_swaps(pieces):
        return [(at, swap(piece, "core", 1, "piece_core")) for at, piece in pieces]

    others = []
    for pieces, own in ((outer_pieces, outer_copy), (inner_pieces, inner_copy)):
        (held,) = touch([own], [arrived])
        others.append(core_swaps([(pieces[0][0], held), *pieces[1:early]]))
    shapes = [outer_weight.shape, inner_weight.shape]
    totals = []
    for i, pieces in enumerate((outer_pieces, inner_pieces)):
        chosen = [piece for _, piece in pieces[:early] + others[i]]
        totals += assemble(
            info, piece_at[i], [chosen], shapes[i : i + 1], [], after=[arrived] + totals[-1:]
        )
    late = []
    for pieces in (outer_pieces, inner_pieces):
        held = touch([piece for _, piece in pieces[early:]], totals)
        late.append([(at, piece) for (at, _), piece in zip(pieces[early:], held)])
    late_others = [core_swaps(pieces) for pieces in late]
    (kept,) = touch([summed], [pieces[0][1] for pieces in late])
    got = swap(kept, "core", 1, "weight_back")
    project_grad, output_weight_grad, first_total, second_total = weight_outputs(core_at, kept, got, local_cols)
    chosen = [
        [piece for _, piece in own + other] for own, other in zip(late, late_others)
    ]
    outer_total, inner_total = assemble(
        info, piece_at[2], chosen, shapes, totals, after=[project_grad]
    )
    return (
        block_output,
        input_grad,
        first_total,
        second_total,
        project_grad,
        output_weight_grad,
        inner_total[None],
        outer_total[None],
    )


def solution(mesh):
    devices = mesh.devices
    mesh = Mesh(
        devices.reshape(devices.shape[0] // 2, 2, *devices.shape[1:]), ("x", "core", "expert", "head")
    )
    in_specs = (
        P(("x", "core", "expert", "head"), None),
        P(("x", "core", "expert", "head"), None),
        P(("x", "core", "expert", "head")),
        P(("x", "core", "expert", "head")),
        P(),
        P(),
        P(),
        P(None, None, "head"),
        P("head", None),
        P("expert", None, None),
        P("expert", None, None),
    )
    out_specs = (
        P(("x", "core", "expert", "head"), None),
        P(("x", "core", "expert", "head"), None),
        P(),
        P(),
        P(None, None, "head"),
        P("head", None),
        P("expert", None, None),
        P("expert", None, None),
    )
    return jax.shard_map(
        on_device, mesh=mesh, in_specs=in_specs, out_specs=out_specs, check_vma=False
    )
```
